32 devices in a mesh: seq: 16 (over z, x, core), head: 2 (over y).
Axes of the slice: x: 2, y: 2, z: 4, core: 2. Of those that a mesh axis runs over, the one named last changes fastest.
Arguments:
- queries: bfloat16 [4096, 8192], P('seq', 'head'), may hold values from -200 to 200
- layer_key_rows: bfloat16 [4096, 1024], P('seq', 'head'), may hold values from -7 to 7
- layer_value_rows: bfloat16 [4096, 1024], P('seq', 'head'), may hold values from -6 to 6
- output_gradient: bfloat16 [4096, 8192], P('seq', 'head'), may hold values from -24 to 24
- output_row_sums: float32 [64, 4096], P('head', 'seq'), may hold values from -72 to 72
- shifted_head_flags: int32 [64], P('head'), may hold values from 0 to 1, as said below
- inputs: bfloat16 [4096, 8192], P('seq', 'head'), may hold values from -6 to 6
- adapter_down_weight: bfloat16 [3, 16, 8192], P(None, None, 'head'), may hold values from -0.0625 to 0.0625
- query_up_weight: bfloat16 [16, 8192], P(None, 'head'), may hold values from -0.75 to 0.75
- key_value_up_weight: bfloat16 [2, 16, 1024], P(None, None, 'head'), may hold values from -0.75 to 0.75
Outputs:
- grad_inputs: bfloat16 [4096, 8192], P('seq', 'head')
- key_value_gradient: bfloat16 [2, 4096, 1024], P(None, 'seq', 'head')
- down_gradient: float32 [3, 16, 8192], P(None, None, 'head')
- grad_up_q: float32 [16, 8192], P(None, 'head')
- grad_up_kv: float32 [2, 16, 1024], P(None, None, 'head')
The draws below stay inside these ranges and needn't reach their ends.
Inputs may be any that keep to these rules, and one draw needn't show every extreme that they name: `shifted_head_flags`: exactly half of the 64 heads have 1.
All inputs are finite; a program needn't handle non-finite values.
Results may differ from the reference program's by a relative error of at most 0.013.
Values may be sent and summed in bfloat16 or wider, within the bound.
No kernel may reach another device: no remote copies, remote signals or barrier semaphores. Data moves between devices by JAX's collectives and lax.ppermute only.
A program may use at most 128 MiB of HBM per device.

```python
import math
import jax
import jax.numpy as jnp
from jax import lax

MODEL_WIDTH = 8192
QUERY_HEADS = 64
KEY_VALUE_HEADS = 8
HEAD_SIZE = 128
ADAPTER_RANK = 16
GROUP = 1024
SHIFT = 512
TOKENS = 4096


def shared_rows(key):
    base = jnp.clip(jax.random.normal(jax.random.fold_in(key, 101), (TOKENS, KEY_VALUE_HEADS * HEAD_SIZE), jnp.float32), -6.0, 6.0)
    return base


def draw_layer_key_rows(key, part):
    base = shared_rows(key)
    return base.astype(jnp.bfloat16)


def draw_queries(key, part):
    key = jax.random.fold_in(key, 2)
    return jnp.clip(jax.random.normal(key, (TOKENS, QUERY_HEADS * HEAD_SIZE), jnp.float32), -6.0, 6.0).astype(jnp.bfloat16)


def draw_shifted_head_flags(key, part):
    key = jax.random.fold_in(key, 3)
    order = jax.random.permutation(key, QUERY_HEADS)
    return (order < QUERY_HEADS // 2).astype(jnp.int32)


def steps_of(stream_key, extent, split, low, high):
    factor_of, own = 1.0, jax.random.fold_in(stream_key, 6)
    for dim, blocks in split:
        draws = jnp.exp(jax.random.uniform(jax.random.fold_in(own, dim), (blocks,), jnp.float32, low / len(split), high / len(split)))
        factor_of = factor_of * jnp.repeat(draws, extent[dim] // blocks).reshape([-1 if axis == dim else 1 for axis in range(len(extent))])
    return factor_of


def centred(rng, shape, scale, bound, shards=(), kind=jnp.bfloat16):
    loudness = steps_of(rng, shape, shards, -0.22, 0.18) if shards else 1.0
    values = jax.random.normal(rng, shape, jnp.float32) * scale * loudness
    return jnp.minimum(jnp.maximum(values, -bound), bound).astype(kind)


def setup_inputs(seed: int = 0) -> dict:
    splits = jax.random.split(jax.random.key(seed), 11)
    queries = draw_queries(jax.random.fold_in(splits[10], 71), 0)
    layer_key_rows = draw_layer_key_rows(jax.random.fold_in(splits[10], 71), 0)
    layer_value_rows = centred(splits[2], (TOKENS, KEY_VALUE_HEADS * HEAD_SIZE), 1.0, 6.0, ((0, 16), (1, 2)))
    output_gradient = centred(splits[3], (TOKENS, QUERY_HEADS * HEAD_SIZE), 4.0, 24.0, ((0, 16), (1, 2)))
    output_row_sums = centred(splits[4], (QUERY_HEADS, TOKENS), 12.0, 72.0, ((0, 2), (1, 16)), jnp.float32)
    shifted_head_flags = draw_shifted_head_flags(jax.random.fold_in(splits[10], 71), 0)
    inputs = centred(splits[6], (TOKENS, MODEL_WIDTH), 1.0, 6.0, ((0, 16), (1, 2)))
    adapter_down_weight = centred(splits[7], (3, ADAPTER_RANK, MODEL_WIDTH), MODEL_WIDTH ** -0.5, 0.0625, ((2, 2),))
    query_up_weight = centred(splits[8], (ADAPTER_RANK, QUERY_HEADS * HEAD_SIZE), (4 * ADAPTER_RANK) ** -0.5, 0.75, ((1, 2),))
    key_value_up_weight = centred(splits[9], (2, ADAPTER_RANK, KEY_VALUE_HEADS * HEAD_SIZE), (4 * ADAPTER_RANK) ** -0.5, 0.75, ((2, 2),))
    return {"queries": queries, "layer_key_rows": layer_key_rows, "layer_value_rows": layer_value_rows, "output_gradient": output_gradient, "output_row_sums": output_row_sums, "shifted_head_flags": shifted_head_flags, "inputs": inputs, "adapter_down_weight": adapter_down_weight, "query_up_weight": query_up_weight, "key_value_up_weight": key_value_up_weight}


adapter_scale = 2.0
masked_score = -1e+30

def to_bf16_f32(values):
    return lax.optimization_barrier(values.astype(jnp.bfloat16)).astype(jnp.float32)

def head_backward(query_head, key_head, value_head, grad_head, row_term, shifted):
    score_scale = HEAD_SIZE ** (-0.5)
    group_count = TOKENS // GROUP

    def roll_in(array):
        return jnp.where(shifted > 0, jnp.roll(array, -SHIFT, axis=0), array)

    def roll_out(array):
        return jnp.where(shifted > 0, jnp.roll(array, SHIFT, axis=0), array)
    query_g = roll_in(query_head).reshape(group_count, GROUP, HEAD_SIZE).astype(jnp.float32)
    key_g = roll_in(key_head).reshape(group_count, GROUP, HEAD_SIZE).astype(jnp.float32)
    value_g = roll_in(value_head).reshape(group_count, GROUP, HEAD_SIZE).astype(jnp.float32)
    grad_g = roll_in(grad_head).reshape(group_count, GROUP, HEAD_SIZE).astype(jnp.float32)
    term_g = roll_in(row_term).reshape(group_count, GROUP)
    causal = jnp.tril(jnp.ones((GROUP, GROUP), dtype=bool))
    scores = jnp.einsum('gid,gjd->gij', query_g, key_g) * score_scale
    scores = jnp.where(causal, scores, masked_score)
    row_max = lax.optimization_barrier(jnp.max(scores, axis=2, keepdims=True))
    weights = jnp.where(causal, jnp.exp(scores - row_max), 0.0)
    prob_rows = weights / lax.optimization_barrier(jnp.sum(weights, axis=2, keepdims=True))
    prob_low = to_bf16_f32(prob_rows)
    grad_values = jnp.einsum('gij,gid->gjd', prob_low, grad_g)
    grad_probs = jnp.einsum('gid,gjd->gij', grad_g, value_g)
    grad_scores = to_bf16_f32(prob_rows * (grad_probs - term_g[:, :, None]))
    grad_query = (jnp.einsum('gij,gjd->gid', grad_scores, key_g) * score_scale).astype(jnp.bfloat16)
    grad_keys = jnp.einsum('gij,gid->gjd', grad_scores, query_g) * score_scale
    return (roll_out(grad_query.reshape(TOKENS, HEAD_SIZE)), roll_out(grad_keys.reshape(TOKENS, HEAD_SIZE)), roll_out(grad_values.reshape(TOKENS, HEAD_SIZE)))

def reference(queries, layer_key_rows, layer_value_rows, output_gradient, output_row_sums, shifted_head_flags, inputs, adapter_down_weight, query_up_weight, key_value_up_weight):
    per_kv = QUERY_HEADS // KEY_VALUE_HEADS
    query_heads = queries.reshape(TOKENS, KEY_VALUE_HEADS, per_kv, HEAD_SIZE).transpose(1, 2, 0, 3)
    grad_heads = output_gradient.reshape(TOKENS, KEY_VALUE_HEADS, per_kv, HEAD_SIZE).transpose(1, 2, 0, 3)
    key_heads = layer_key_rows.reshape(TOKENS, KEY_VALUE_HEADS, HEAD_SIZE).transpose(1, 0, 2)
    value_heads = layer_value_rows.reshape(TOKENS, KEY_VALUE_HEADS, HEAD_SIZE).transpose(1, 0, 2)
    term_heads = output_row_sums.reshape(KEY_VALUE_HEADS, per_kv, TOKENS)
    shift_heads = shifted_head_flags.reshape(KEY_VALUE_HEADS, per_kv)

    def per_group(bundle):
        group_queries, group_grads, key_head, value_head, group_terms, group_shifts = bundle

        def one_head(running, head_item):
            query_head, grad_head, row_term, shifted = head_item
            grad_query, grad_keys, grad_values = head_backward(query_head, key_head, value_head, grad_head, row_term, shifted)
            return ((running[0] + grad_keys, running[1] + grad_values), grad_query)
        zeros_init = jnp.zeros((TOKENS, HEAD_SIZE), jnp.float32)
        (key_total, value_total), query_gradient_rows = lax.scan(one_head, (zeros_init, zeros_init), (group_queries, group_grads, group_terms, group_shifts))
        return (query_gradient_rows, key_total, value_total)
    grad_q_heads, key_totals, value_totals = lax.map(per_group, (query_heads, grad_heads, key_heads, value_heads, term_heads, shift_heads))
    query_gradient_rows = grad_q_heads.transpose(2, 0, 1, 3).reshape(TOKENS, QUERY_HEADS * HEAD_SIZE)
    key_value_gradient = jnp.stack([key_totals.transpose(1, 0, 2).reshape(TOKENS, KEY_VALUE_HEADS * HEAD_SIZE), value_totals.transpose(1, 0, 2).reshape(TOKENS, KEY_VALUE_HEADS * HEAD_SIZE)]).astype(jnp.bfloat16)
    flattened_down = adapter_down_weight.reshape(3 * ADAPTER_RANK, MODEL_WIDTH)
    down_in = jnp.dot(inputs, flattened_down.T, preferred_element_type=jnp.float32)
    down_low = down_in.astype(jnp.bfloat16)
    up_backward_term = jnp.concatenate([jnp.dot(query_gradient_rows, query_up_weight.T, preferred_element_type=jnp.float32), jnp.dot(key_value_gradient[0], key_value_up_weight[0].T, preferred_element_type=jnp.float32), jnp.dot(key_value_gradient[1], key_value_up_weight[1].T, preferred_element_type=jnp.float32)], axis=1)
    up_low = up_backward_term.astype(jnp.bfloat16)
    grad_inputs = (adapter_scale * jnp.dot(up_low, flattened_down, preferred_element_type=jnp.float32)).astype(jnp.bfloat16)
    multiplier = adapter_scale / math.sqrt(TOKENS)
    down_gradient = multiplier * jnp.dot(up_low.T, inputs, preferred_element_type=jnp.float32).reshape(3, ADAPTER_RANK, MODEL_WIDTH)
    grad_up_q = multiplier * jnp.dot(down_low[:, :ADAPTER_RANK].T, query_gradient_rows, preferred_element_type=jnp.float32)
    grad_up_kv = multiplier * jnp.stack([jnp.dot(down_low[:, ADAPTER_RANK:2 * ADAPTER_RANK].T, key_value_gradient[0], preferred_element_type=jnp.float32), jnp.dot(down_low[:, 2 * ADAPTER_RANK:].T, key_value_gradient[1], preferred_element_type=jnp.float32)])
    return (grad_inputs, key_value_gradient, down_gradient, grad_up_q, grad_up_kv)
```

```python
import functools
import math

import jax
import jax.numpy as jnp
from jax import lax
from jax.experimental import pallas as pl
from jax.experimental.pallas import tpu as pltpu
from jax.sharding import PartitionSpec as P

HEAD_SIZE = 128
GROUP = 1024
SHIFT = 512
CHUNK = 32

adapter_scale = 2.0
masked_score = -1e30
score_scale = HEAD_SIZE ** (-0.5)
exp2_scale = score_scale * math.log2(math.e)

NT = (((1,), (1,)), ((), ()))
NN = (((1,), (0,)), ((), ()))


def mm(left, right, dims=NN):
    return lax.dot_general(left, right, dims, preferred_element_type=jnp.float32)


def head_batch(
    heads, low, high, diag, tokens, q_ref, do_ref, term_ref, dq_ref, kwin, vwin, kt, s_ref, e_ref, ds_ref, dk_acc, dv_acc
):
    count = len(heads)
    wide = count * tokens
    columns = [pl.ds(pl.multiple_of(h * HEAD_SIZE, HEAD_SIZE), HEAD_SIZE) for h in heads]
    query = jnp.concatenate([q_ref[:, c] for c in columns], axis=0)
    grad = jnp.concatenate([do_ref[:, c] for c in columns], axis=0)
    term = jnp.concatenate([term_ref[pl.ds(h, 1), :] for h in heads], axis=1)
    top = None
    for row in range(low, high, tokens):
        scores = mm(kwin[row : row + tokens, :], query, NT)
        if row == diag:
            key_row = lax.broadcasted_iota(jnp.int32, (tokens, tokens), 0)
            query_row = lax.broadcasted_iota(jnp.int32, (tokens, tokens), 1)
            seen = jnp.concatenate([key_row <= query_row] * count, axis=1)
            scores = jnp.where(seen, scores, masked_score)
        s_ref[row : row + tokens, :wide] = scores
        here = jnp.max(scores.reshape(tokens // 8, 8, wide), axis=0)
        top = here if top is None else jnp.maximum(top, here)
    top = jnp.max(top, axis=0, keepdims=True)
    total = jnp.zeros((8, wide), jnp.float32)
    for row in range(low, high, tokens):
        grad_probs = mm(vwin[row : row + tokens, :], grad, NT)
        for at in range(0, tokens, CHUNK):
            rows = slice(row + at, row + at + CHUNK)
            weights = jnp.exp2((s_ref[rows, :wide] - top) * exp2_scale)
            total = total + jnp.sum(weights.reshape(CHUNK // 8, 8, wide), axis=0)
            e_ref[rows, :wide] = weights.astype(jnp.bfloat16)
            ds_ref[rows, :wide] = (weights * (grad_probs[at : at + CHUNK, :] - term)).astype(jnp.bfloat16)
    inverse = 1.0 / jnp.sum(total, axis=0, keepdims=True)
    inverse_rows = jnp.broadcast_to(inverse, (HEAD_SIZE, wide)).T
    grad_n = (grad.astype(jnp.float32) * inverse_rows).astype(jnp.bfloat16)
    query_n = (query.astype(jnp.float32) * (inverse_rows * score_scale)).astype(jnp.bfloat16)
    dv_acc[low:high, :] += mm(e_ref[low:high, :wide], grad_n)
    dk_acc[low:high, :] += mm(ds_ref[low:high, :wide], query_n)
    query_grad = mm(kt[:, low:high], ds_ref[low:high, :wide]) * (inverse * score_scale)
    for i, c in enumerate(columns):
        dq_ref[:, c] = query_grad[:, i * tokens : (i + 1) * tokens].T.astype(jnp.bfloat16)


def all_heads(with_previous, per_kv, tokens, place_ref, flags_ref, q_ref, do_ref, term_ref, dq_ref, listed, *scratch):
    first = pl.program_id(0) * per_kv
    core = place_ref[0]
    half = place_ref[1]
    count = jnp.int32(0)
    for h in range(per_kv):
        listed[count] = jnp.int32(h)
        needs = flags_ref[first + h] != half
        count = count + jnp.where(needs == with_previous, 1, 0).astype(jnp.int32)
    high = (4 if with_previous else 2) * tokens
    for which in range(2):
        low = (1 - which) * tokens
        run = functools.partial(
            head_batch,
            low=low,
            high=high,
            diag=tokens,
            tokens=tokens,
            q_ref=q_ref,
            do_ref=do_ref,
            term_ref=term_ref,
            dq_ref=dq_ref,
            **dict(zip(("kwin", "vwin", "kt", "s_ref", "e_ref", "ds_ref", "dk_acc", "dv_acc"), scratch)),
        )

        @pl.when(core == which)
        def _():
            def pair(i, carry):
                run([listed[2 * i], listed[2 * i + 1]])
                return carry

            lax.fori_loop(0, count // 2, pair, 0)

            @pl.when(count % 2 == 1)
            def _():
                run([listed[count - 1]])


def fill_window(tokens, kwin, vwin, kt, blocks):
    for at, (key, value) in enumerate(blocks):
        rows = slice(at * tokens, (at + 1) * tokens)
        kwin[rows, :] = key
        vwin[rows, :] = value
        kt[:, rows] = key.T


def own_kernel(
    per_kv, tokens, place, flags, q, do, term, k_own, v_own, kv_sib, dq, dk, dv, listed, kwin, vwin, kt, s, e, ds
):
    fill_window(tokens, kwin, vwin, kt, [(kv_sib[0], kv_sib[1]), (k_own[...], v_own[...])])
    dk[...] = jnp.zeros_like(dk)
    dv[...] = jnp.zeros_like(dv)
    all_heads(
        False, per_kv, tokens, place, flags, q, do, term, dq, listed, kwin, vwin, kt, s, e, ds, dk, dv
    )


def previous_kernel(
    per_kv, tokens, rank, place, flags, q, do, term, k_own, v_own, kv_sib, kv_pc, kv_px, dq_own, dk_own, dv_own,
    w_q, w_kv, down_q, down_win,
    dq, keep, send, up_q, up_keep, up_send, grad_q, grad_kv,
    listed, kwin, vwin, kt, s, e, ds, dk, dv,
):
    fill_window(
        tokens, kwin, vwin, kt,
        [(kv_sib[0], kv_sib[1]), (k_own[...], v_own[...]), (kv_pc[0], kv_pc[1]), (kv_px[0], kv_px[1])],
    )
    for acc, start in ((dk, dk_own), (dv, dv_own)):
        acc[: 2 * tokens, :] = start[...]
        acc[2 * tokens :, :] = jnp.zeros((2 * tokens, HEAD_SIZE), jnp.float32)
    all_heads(
        True, per_kv, tokens, place, flags, q, do, term, dq, listed, kwin, vwin, kt, s, e, ds, dk, dv
    )
    first = pl.program_id(0) * per_kv
    for h in range(per_kv):

        @pl.when(flags[first + h] == place[1])
        def _():
            columns = slice(h * HEAD_SIZE, (h + 1) * HEAD_SIZE)
            dq[:, columns] = dq_own[:, columns]

    @pl.when(pl.program_id(0) == 0)
    def _():
        up_q[...] = jnp.zeros_like(up_q)
        up_keep[...] = jnp.zeros_like(up_keep)
        up_send[...] = jnp.zeros_like(up_send)

    query_grads = dq[...]
    up_q[...] += mm(w_q[...], query_grads, NT)
    grad_q[...] = mm(down_q[...], query_grads)
    for c, acc in ((0, dk), (1, dv)):
        keep[c, 0] = acc[tokens : 2 * tokens, :]
        keep[c, 1] = acc[2 * tokens : 3 * tokens, :]
        send[c, 0] = acc[:tokens, :].astype(jnp.bfloat16)
        send[c, 1] = acc[3 * tokens :, :].astype(jnp.bfloat16)
        low = acc[...].astype(jnp.bfloat16)
        up = mm(w_kv[c], low, NT)
        own = slice(c * rank, (c + 1) * rank)
        up_send[own, :tokens] += up[:, :tokens]
        up_keep[own, :] += up[:, tokens : 3 * tokens]
        up_send[own, tokens:] += up[:, 3 * tokens :]
        grad_kv[own, :] = mm(down_win[own, :], low)


def attention(place, flags, queries, grads, terms, k_own, v_own, kv_sib):
    tokens, width = queries.shape
    kv_width = k_own.shape[1]
    kv_local = kv_width // HEAD_SIZE
    per_kv = width // kv_width
    block = per_kv * HEAD_SIZE
    smem = pl.BlockSpec(memory_space=pltpu.SMEM)

    def columns(rows, wide):
        return pl.BlockSpec((rows, wide), lambda g: (0, g))

    def stacked(*lead):
        return pl.BlockSpec((*lead, tokens, HEAD_SIZE), lambda g: (0,) * (len(lead) + 1) + (g,))

    def fixed(*shape):
        return pl.BlockSpec(shape, lambda g: (0,) * len(shape))

    def scratch(blocks):
        rows = blocks * tokens
        return [
            pltpu.SMEM((per_kv + 1,), jnp.int32),
            pltpu.VMEM((rows, HEAD_SIZE), jnp.bfloat16),
            pltpu.VMEM((rows, HEAD_SIZE), jnp.bfloat16),
            pltpu.VMEM((HEAD_SIZE, rows), jnp.bfloat16),
            pltpu.VMEM((rows, 2 * tokens), jnp.float32),
            pltpu.VMEM((rows, 2 * tokens), jnp.bfloat16),
            pltpu.VMEM((rows, 2 * tokens), jnp.bfloat16),
        ]

    per_head_specs = [
        smem,
        smem,
        columns(tokens, block),
        columns(tokens, block),
        pl.BlockSpec((per_kv, tokens), lambda g: (g, 0)),
        columns(tokens, HEAD_SIZE),
        columns(tokens, HEAD_SIZE),
        stacked(2),
    ]
    per_head = (place, flags, queries, grads, terms, k_own, v_own, kv_sib)
    params = pltpu.CompilerParams(
        dimension_semantics=("arbitrary",), vmem_limit_bytes=40 * 1024 * 1024
    )
    f32, bf16 = jnp.float32, jnp.bfloat16
    shape = jax.ShapeDtypeStruct
    pairs = kv_local * per_kv * tokens * tokens

    def own():
        return pl.pallas_call(
            functools.partial(own_kernel, per_kv, tokens),
            grid=(kv_local,),
            in_specs=per_head_specs,
            out_specs=[columns(tokens, block)] + [columns(2 * tokens, HEAD_SIZE)] * 2,
            out_shape=[shape((tokens, width), bf16)] + [shape((2 * tokens, kv_width), f32)] * 2,
            scratch_shapes=scratch(2),
            compiler_params=params,
            cost_estimate=pl.CostEstimate(
                flops=10 * pairs * HEAD_SIZE, bytes_accessed=6 * tokens * width, transcendentals=pairs
            ),
            name="own_chip_heads",
        )(*per_head)

    def previous(kv_pc, kv_px, own_grads, w_q, w_kv, down_low, down_win):
        rank = w_q.shape[0]
        return pl.pallas_call(
            functools.partial(previous_kernel, per_kv, tokens, rank),
            grid=(kv_local,),
            in_specs=per_head_specs
            + [stacked(2), stacked(2), columns(tokens, block)]
            + [columns(2 * tokens, HEAD_SIZE)] * 2
            + [
                columns(rank, block),
                pl.BlockSpec((2, rank, HEAD_SIZE), lambda g: (0, 0, g)),
                fixed(rank, tokens),
                fixed(2 * rank, 4 * tokens),
            ],
            out_specs=[
                columns(tokens, block),
                stacked(2, 2),
                stacked(2, 2),
                fixed(rank, tokens),
                fixed(2 * rank, 2 * tokens),
                fixed(2 * rank, 2 * tokens),
                columns(rank, block),
                columns(2 * rank, HEAD_SIZE),
            ],
            out_shape=[
                shape((tokens, width), bf16),
                shape((2, 2, tokens, kv_width), f32),
                shape((2, 2, tokens, kv_width), bf16),
                shape((rank, tokens), f32),
                shape((2 * rank, 2 * tokens), f32),
                shape((2 * rank, 2 * tokens), f32),
                shape((rank, width), f32),
                shape((2 * rank, kv_width), f32),
            ],
            scratch_shapes=scratch(4) + [pltpu.VMEM((4 * tokens, HEAD_SIZE), f32)] * 2,
            compiler_params=params,
            cost_estimate=pl.CostEstimate(
                flops=20 * pairs * HEAD_SIZE, bytes_accessed=12 * tokens * width, transcendentals=2 * pairs
            ),
            name="previous_chip_heads",
        )(*per_head, kv_pc, kv_px, *own_grads, w_q, w_kv, down_low, down_win)

    return own, previous


def exchanged(value, axis, bit):
    return lax.ppermute(value, axis, [(i, i ^ bit) for i in range(lax.axis_size(axis))])


def moved(value, axis, by):
    count = lax.axis_size(axis)
    return lax.ppermute(value, axis, [(i, (i + by) % count) for i in range(count)])


def summed(value, axis):
    bit = 1
    while bit < lax.axis_size(axis):
        value = value + exchanged(value, axis, bit)
        bit *= 2
    return value


def summed_by_halves(value, axis):
    count, index = lax.axis_size(axis), lax.axis_index(axis)
    bits = [1 << i for i in range(count.bit_length() - 1)]
    for bit in bits:
        low_half = (index & bit) == 0
        left, right = jnp.split(value, 2, axis=1)
        other = exchanged(jnp.where(low_half, right, left).astype(jnp.bfloat16), axis, bit)
        value = jnp.where(low_half, left, right).astype(jnp.float32) + other.astype(jnp.float32)
    value = value.astype(jnp.bfloat16)
    for bit in reversed(bits):
        low_half = (index & bit) == 0
        other = exchanged(value, axis, bit)
        value = jnp.concatenate(
            [jnp.where(low_half, value, other), jnp.where(low_half, other, value)], axis=1
        )
    return value.astype(jnp.float32)


def per_device(
    queries,
    layer_key_rows,
    layer_value_rows,
    output_gradient,
    output_row_sums,
    shifted_head_flags,
    inputs,
    adapter_down_weight,
    query_up_weight,
    key_value_up_weight,
):
    seq_count = lax.axis_size("seq")
    seq_index = lax.axis_index("seq")
    tokens, width = queries.shape
    kv_width = layer_key_rows.shape[1]
    whole_len = tokens * seq_count
    rank = adapter_down_weight.shape[1]
    assert GROUP == 4 * tokens and SHIFT == 2 * tokens
    assert seq_count % 4 == 0 and seq_count & (seq_count - 1) == 0
    flattened_down = adapter_down_weight.reshape(3 * rank, width)
    place = jnp.stack([seq_index % 2, seq_index // 2 % 2]).astype(jnp.int32)

    kv_own = jnp.stack([layer_key_rows, layer_value_rows])
    kv_sib = exchanged(kv_own, "seq", 1)
    kv_pc = moved(kv_own, "seq", 2)
    kv_px = exchanged(kv_pc, "seq", 1)

    down_low = summed(mm(flattened_down, inputs, NT), "head").astype(jnp.bfloat16)
    down_own = down_low[rank:]
    down_pc = moved(down_own, "seq", 2)
    down_others = exchanged(jnp.concatenate([down_own, down_pc]), "seq", 1)
    down_win = jnp.concatenate(
        [down_others[: 2 * rank], down_own, down_pc, down_others[2 * rank :]], axis=1
    )

    own, previous = attention(
        place,
        shifted_head_flags,
        queries,
        output_gradient,
        output_row_sums,
        layer_key_rows,
        layer_value_rows,
        kv_sib,
    )
    own_grads = own()
    query_grads, keep, send, up_q, up_keep, up_send, grad_q, grad_kv = previous(
        kv_pc, kv_px, own_grads, query_up_weight, key_value_up_weight, down_low[:rank], down_win
    )

    up_kv = up_keep + exchanged(up_send, "seq", 1)
    up_kv = up_kv[:, :tokens] + moved(up_kv[:, tokens:], "seq", -2)
    up_low = summed(jnp.concatenate([up_q, up_kv]), "head").astype(jnp.bfloat16)

    kv_grads = keep + exchanged(send, "seq", 1).astype(jnp.float32)
    back = moved(kv_grads[:, 1].astype(jnp.bfloat16), "seq", -2)
    key_value_gradient = (kv_grads[:, 0] + back.astype(jnp.float32)).astype(jnp.bfloat16)

    grad_inputs = (
        adapter_scale
        * lax.dot_general(
            up_low, flattened_down, (((0,), (0,)), ((), ())), preferred_element_type=jnp.float32
        )
    ).astype(jnp.bfloat16)
    weight_grads = jnp.concatenate(
        [mm(up_low, inputs), grad_q, grad_kv.reshape(-1, width)]
    ) * (adapter_scale / math.sqrt(whole_len))
    weight_grads = summed_by_halves(weight_grads, "seq")
    return (
        grad_inputs,
        key_value_gradient,
        weight_grads[: 3 * rank].reshape(3, rank, width),
        weight_grads[3 * rank : 4 * rank],
        weight_grads[4 * rank :].reshape(2, rank, kv_width),
    )


def solution(mesh):
    placed = (
        P("seq", "head"),
        P("seq", "head"),
        P("seq", "head"),
        P("seq", "head"),
        P("head", "seq"),
        P("head"),
        P("seq", "head"),
        P(None, None, "head"),
        P(None, "head"),
        P(None, None, "head"),
    )
    return jax.shard_map(
        per_device,
        mesh=mesh,
        in_specs=placed,
        out_specs=(
            P("seq", "head"),
            P(None, "seq", "head"),
            P(None, None, "head"),
            P(None, "head"),
            P(None, None, "head"),
        ),
        check_vma=False,
    )
```

```python
import functools
import math

import jax
import jax.numpy as jnp
from jax import lax
from jax.experimental import pallas as pl
from jax.experimental.pallas import tpu as pltpu
from jax.sharding import PartitionSpec as P

HEAD_SIZE = 128
GROUP = 1024
SHIFT = 512
CHUNK = 32
VMEM_LIMIT = 24 * 1024 * 1024

adapter_scale = 2.0
masked_score = -1e30
score_scale = HEAD_SIZE ** (-0.5)
exp2_scale = score_scale * math.log2(math.e)

NT = (((1,), (1,)), ((), ()))
NN = (((1,), (0,)), ((), ()))


def mm(left, right, dims=NN):
    return lax.dot_general(left, right, dims, preferred_element_type=jnp.float32)


def head_batch(
    heads, low, high, diag, tokens, q_ref, do_ref, term_ref, down, up_q,
    kwin, vwin, wk, s_ref, e_ref, ds_ref, dk_acc, dv_acc,
):
    count = len(heads)
    wide = count * tokens
    rank = up_q.shape[0]
    columns = [pl.ds(pl.multiple_of(h * HEAD_SIZE, HEAD_SIZE), HEAD_SIZE) for h in heads]
    query = jnp.concatenate([q_ref[:, c] for c in columns], axis=0)
    grad = jnp.concatenate([do_ref[:, c] for c in columns], axis=0)
    term = jnp.concatenate([term_ref[pl.ds(h, 1), :] for h in heads], axis=1)
    top = None
    for row in range(low, high, tokens):
        scores = mm(kwin[row : row + tokens, :], query, NT)
        if row == diag:
            key_row = lax.broadcasted_iota(jnp.int32, (tokens, tokens), 0)
            query_row = lax.broadcasted_iota(jnp.int32, (tokens, tokens), 1)
            seen = jnp.concatenate([key_row <= query_row] * count, axis=1)
            scores = jnp.where(seen, scores, masked_score)
        s_ref[row : row + tokens, :wide] = scores
        here = jnp.max(scores.reshape(tokens // 8, 8, wide), axis=0)
        top = here if top is None else jnp.maximum(top, here)
    top = jnp.max(top, axis=0, keepdims=True)
    total = jnp.zeros((8, wide), jnp.float32)
    for row in range(low, high, tokens):
        grad_probs = mm(vwin[row : row + tokens, :], grad, NT)
        for at in range(0, tokens, CHUNK):
            rows = slice(row + at, row + at + CHUNK)
            weights = jnp.exp2((s_ref[rows, :wide] - top) * exp2_scale)
            total = total + jnp.sum(weights.reshape(CHUNK // 8, 8, wide), axis=0)
            e_ref[rows, :wide] = weights.astype(jnp.bfloat16)
            ds_ref[rows, :wide] = (weights * (grad_probs[at : at + CHUNK, :] - term)).astype(jnp.bfloat16)
    inverse = 1.0 / jnp.sum(total, axis=0, keepdims=True)
    inverse_rows = jnp.broadcast_to(inverse, (HEAD_SIZE, wide)).T
    grad_n = (grad.astype(jnp.float32) * inverse_rows).astype(jnp.bfloat16)
    lane = lax.broadcasted_iota(jnp.int32, (tokens, HEAD_SIZE), 1) // rank
    tiled = down[...].astype(jnp.float32)
    own_columns = jnp.concatenate([jnp.where(lane == h, tiled, 0.0) for h in heads], axis=0)
    scaled = inverse_rows * score_scale
    query_n = jnp.concatenate(
        [query.astype(jnp.float32) * scaled, own_columns * scaled], axis=1
    ).astype(jnp.bfloat16)
    dv_acc[low:high, :] += mm(e_ref[low:high, :wide], grad_n)
    dk_acc[low:high, :] += mm(ds_ref[low:high, :wide], query_n)
    back = None
    for i, h in enumerate(heads):
        own = slice(i * tokens, (i + 1) * tokens)
        part = mm(wk[pl.ds(pl.multiple_of(h * rank, rank), rank), low:high], ds_ref[low:high, own])
        part = part * (inverse[:, own] * score_scale)
        back = part if back is None else back + part
    up_q[...] += back


def all_heads(with_previous, per_kv, tokens, place_ref, flags_ref, q_ref, do_ref, term_ref, down, up_q, listed, *scratch):
    first = pl.program_id(0) * per_kv
    core = place_ref[0]
    half = place_ref[1]
    count = jnp.int32(0)
    for h in range(per_kv):
        listed[count] = jnp.int32(h)
        needs = flags_ref[first + h] != half
        count = count + jnp.where(needs == with_previous, 1, 0).astype(jnp.int32)
    high = (4 if with_previous else 2) * tokens
    for which in range(2):
        low = (1 - which) * tokens
        run = functools.partial(
            head_batch,
            low=low,
            high=high,
            diag=tokens,
            tokens=tokens,
            q_ref=q_ref,
            do_ref=do_ref,
            term_ref=term_ref,
            down=down,
            up_q=up_q,
            **dict(zip(("kwin", "vwin", "wk", "s_ref", "e_ref", "ds_ref", "dk_acc", "dv_acc"), scratch)),
        )

        @pl.when(core == which)
        def _():
            def pair(i, carry):
                run([listed[2 * i], listed[2 * i + 1]])
                return carry

            lax.fori_loop(0, count // 2, pair, 0)

            @pl.when(count % 2 == 1)
            def _():
                run([listed[count - 1]])


def fill_window(per_kv, tokens, kwin, vwin, wk, w_q, blocks):
    for at, (key, value) in enumerate(blocks):
        rows = slice(at * tokens, (at + 1) * tokens)
        kwin[rows, :] = key[...]
        vwin[rows, :] = value[...]
    stacked = jnp.concatenate(
        [w_q[:, h * HEAD_SIZE : (h + 1) * HEAD_SIZE] for h in range(per_kv)], axis=0
    )
    wk[...] = mm(stacked, kwin[...], NT).astype(jnp.bfloat16)


def own_kernel(
    per_kv, tokens, place, flags, q, do, term, w_q, down, k_own, v_own, k_sib, v_sib,
    up_q, dk, dv,
    listed, kwin, vwin, wk, s, e, ds,
):
    fill_window(per_kv, tokens, kwin, vwin, wk, w_q, [(k_sib, v_sib), (k_own, v_own)])
    dk[...] = jnp.zeros_like(dk)
    dv[...] = jnp.zeros_like(dv)

    @pl.when(pl.program_id(0) == 0)
    def _():
        up_q[...] = jnp.zeros_like(up_q)

    all_heads(False, per_kv, tokens, place, flags, q, do, term, down, up_q, listed, kwin, vwin, wk, s, e, ds, dk, dv)


def previous_kernel(
    per_kv, tokens, rank, place, flags, q, do, term, w_q, down, k_own, v_own, k_sib, v_sib, k_pc, v_pc, k_px, v_px,
    up_q_own, dk_own, dv_own, w_kv, down_win,
    keep_own, keep_pc, send, up_q, up_keep, up_send, grad_q, grad_kv,
    listed, kwin, vwin, wk, s, e, ds, dk, dv,
):
    fill_window(
        per_kv, tokens, kwin, vwin, wk, w_q, [(k_sib, v_sib), (k_own, v_own), (k_pc, v_pc), (k_px, v_px)]
    )
    for acc, start in ((dk, dk_own), (dv, dv_own)):
        acc[: 2 * tokens, :] = start[...]
        acc[2 * tokens :, :] = jnp.zeros((2 * tokens, acc.shape[1]), jnp.float32)

    @pl.when(pl.program_id(0) == 0)
    def _():
        up_q[...] = up_q_own[...]
        up_keep[...] = jnp.zeros_like(up_keep)
        up_send[...] = jnp.zeros_like(up_send)

    all_heads(True, per_kv, tokens, place, flags, q, do, term, down, up_q, listed, kwin, vwin, wk, s, e, ds, dk, dv)
    by_head = mm(dk[:, HEAD_SIZE:].T.astype(jnp.bfloat16), kwin[...])
    for h in range(per_kv):
        grad_q[:, h * HEAD_SIZE : (h + 1) * HEAD_SIZE] = by_head[h * rank : (h + 1) * rank, :]
    for c, acc in ((0, dk), (1, dv)):
        total = acc[:, :HEAD_SIZE]
        keep_own[c] = total[tokens : 2 * tokens, :]
        keep_pc[c] = total[2 * tokens : 3 * tokens, :]
        low = total.astype(jnp.bfloat16)
        send[0, c] = low[:tokens, :]
        send[1, c] = low[3 * tokens :, :]
        up = mm(w_kv[c], low, NT)
        own = slice(c * rank, (c + 1) * rank)
        up_send[own, :tokens] += up[:, :tokens]
        up_keep[own, :] += up[:, tokens : 3 * tokens]
        up_send[own, tokens:] += up[:, 3 * tokens :]
        grad_kv[own, :] = mm(down_win[own, :], low)


def attention(place, flags, queries, grads, terms, w_q, down, own_pair, sib_pair):
    tokens, width = queries.shape
    kv_width = own_pair[0].shape[1]
    kv_local = kv_width // HEAD_SIZE
    per_kv = width // kv_width
    rank = w_q.shape[0]
    assert per_kv * rank == HEAD_SIZE
    block = per_kv * HEAD_SIZE
    smem = pl.BlockSpec(memory_space=pltpu.SMEM)

    def columns(rows, wide):
        return pl.BlockSpec((rows, wide), lambda g: (0, g))

    def stacked(*lead):
        return pl.BlockSpec((*lead, tokens, HEAD_SIZE), lambda g: (0,) * (len(lead) + 1) + (g,))

    def fixed(*shape):
        return pl.BlockSpec(shape, lambda g: (0,) * len(shape))

    def scratch(blocks):
        rows = blocks * tokens
        return [
            pltpu.SMEM((per_kv + 1,), jnp.int32),
            pltpu.VMEM((rows, HEAD_SIZE), jnp.bfloat16),
            pltpu.VMEM((rows, HEAD_SIZE), jnp.bfloat16),
            pltpu.VMEM((HEAD_SIZE, rows), jnp.bfloat16),
            pltpu.VMEM((rows, 2 * tokens), jnp.float32),
            pltpu.VMEM((rows, 2 * tokens), jnp.bfloat16),
            pltpu.VMEM((rows, 2 * tokens), jnp.bfloat16),
        ]

    key_spec = columns(tokens, HEAD_SIZE)
    per_head_specs = [
        smem,
        smem,
        columns(tokens, block),
        columns(tokens, block),
        pl.BlockSpec((per_kv, tokens), lambda g: (g, 0)),
        columns(rank, block),
        fixed(tokens, HEAD_SIZE),
    ] + [key_spec] * 4
    per_head = (place, flags, queries, grads, terms, w_q, down, *own_pair, *sib_pair)
    params = pltpu.CompilerParams(dimension_semantics=("arbitrary",), vmem_limit_bytes=VMEM_LIMIT)
    f32, bf16 = jnp.float32, jnp.bfloat16
    shape = jax.ShapeDtypeStruct
    pairs = kv_local * per_kv * tokens * tokens

    def own():
        return pl.pallas_call(
            functools.partial(own_kernel, per_kv, tokens),
            grid=(kv_local,),
            in_specs=per_head_specs,
            out_specs=[fixed(rank, tokens), columns(2 * tokens, 2 * HEAD_SIZE), columns(2 * tokens, HEAD_SIZE)],
            out_shape=[
                shape((rank, tokens), f32),
                shape((2 * tokens, 2 * kv_width), f32),
                shape((2 * tokens, kv_width), f32),
            ],
            scratch_shapes=scratch(2),
            compiler_params=params,
            cost_estimate=pl.CostEstimate(
                flops=40 * pairs * HEAD_SIZE, bytes_accessed=6 * tokens * width, transcendentals=pairs
            ),
            name="own_chip_heads",
        )(*per_head)

    def previous(pc_pair, px_pair, own_grads, w_kv, down_win):
        return pl.pallas_call(
            functools.partial(previous_kernel, per_kv, tokens, rank),
            grid=(kv_local,),
            in_specs=per_head_specs
            + [key_spec] * 4
            + [
                fixed(rank, tokens),
                columns(2 * tokens, 2 * HEAD_SIZE),
                columns(2 * tokens, HEAD_SIZE),
                pl.BlockSpec((2, rank, HEAD_SIZE), lambda g: (0, 0, g)),
                fixed(2 * rank, 4 * tokens),
            ],
            out_specs=[
                stacked(2),
                stacked(2),
                stacked(2, 2),
                fixed(rank, tokens),
                fixed(2 * rank, 2 * tokens),
                fixed(2 * rank, 2 * tokens),
                columns(rank, block),
                columns(2 * rank, HEAD_SIZE),
            ],
            out_shape=[
                shape((2, tokens, kv_width), f32),
                shape((2, tokens, kv_width), f32),
                shape((2, 2, tokens, kv_width), bf16),
                shape((rank, tokens), f32),
                shape((2 * rank, 2 * tokens), f32),
                shape((2 * rank, 2 * tokens), f32),
                shape((rank, width), f32),
                shape((2 * rank, kv_width), f32),
            ],
            scratch_shapes=scratch(4)
            + [pltpu.VMEM((4 * tokens, 2 * HEAD_SIZE), f32), pltpu.VMEM((4 * tokens, HEAD_SIZE), f32)],
            compiler_params=params,
            cost_estimate=pl.CostEstimate(
                flops=80 * pairs * HEAD_SIZE, bytes_accessed=12 * tokens * width, transcendentals=2 * pairs
            ),
            name="previous_chip_heads",
        )(*per_head, *pc_pair, *px_pair, *own_grads, w_kv, down_win)

    return own, previous


def exchanged(value, axis, bit):
    return lax.ppermute(value, axis, [(i, i ^ bit) for i in range(lax.axis_size(axis))])


def moved(value, axis, by):
    count = lax.axis_size(axis)
    return lax.ppermute(value, axis, [(i, (i + by) % count) for i in range(count)])


def summed(value, axis):
    bit = 1
    while bit < lax.axis_size(axis):
        value = value + exchanged(value, axis, bit)
        bit *= 2
    return value


def small_call(kernel, out_shape, *args, scratch=()):
    vmem = pl.BlockSpec(memory_space=pltpu.VMEM)
    return pl.pallas_call(
        kernel,
        in_specs=[pl.BlockSpec(memory_space=pltpu.SMEM)] + [vmem] * (len(args) - 1),
        out_specs=[vmem] * len(out_shape),
        out_shape=out_shape,
        scratch_shapes=list(scratch),
        compiler_params=pltpu.CompilerParams(vmem_limit_bytes=VMEM_LIMIT),
    )(*args)


def lanes(index, wide):
    return pl.ds(pl.multiple_of(index * wide, HEAD_SIZE), wide)


def first_pieces(place, up_low, inputs, grad_q, grad_kv, scale):
    wide = inputs.shape[1] // 4
    rows = up_low.shape[0] + grad_q.shape[0] + grad_kv.shape[0]

    def kernel(place, up, tokens_in, q, kv, *out):
        for d in range(4):
            at = lanes(place[2] ^ d, wide)
            piece = jnp.concatenate([mm(up[...], tokens_in[:, at]), q[:, at], kv[:, at]]) * scale
            out[d][...] = piece.astype(jnp.bfloat16)

    shape = jax.ShapeDtypeStruct((rows, wide), jnp.bfloat16)
    return small_call(kernel, [shape] * 4, place, up_low, inputs, grad_q, grad_kv)


def exchanged_pieces(pieces, axis, unit):
    return [pieces[0]] + [exchanged(pieces[d], axis, d * unit) for d in range(1, 4)]


def summed_into_four(place, level, pieces):
    rows, whole = pieces[0].shape
    wide = whole // 4
    shape = jax.ShapeDtypeStruct((rows, wide), jnp.bfloat16)
    if wide % HEAD_SIZE:
        total = sum(p.astype(jnp.float32) for p in pieces).astype(jnp.bfloat16)
        return [
            lax.dynamic_slice_in_dim(total, (place[2 + level] ^ d) * wide, wide, 1) for d in range(4)
        ]

    def kernel(place, *refs):
        total = refs[8]
        total[...] = sum(p[...].astype(jnp.float32) for p in refs[:4])
        for d in range(4):
            refs[4 + d][...] = total[:, lanes(place[2 + level] ^ d, wide)].astype(jnp.bfloat16)

    return small_call(
        kernel, [shape] * 4, place, *pieces, scratch=[pltpu.VMEM((rows, whole), jnp.float32)]
    )


def joined(place, level, pieces):
    rows, wide = pieces[0].shape
    if wide % HEAD_SIZE:
        whole = jnp.zeros((rows, 4 * wide), jnp.bfloat16)
        for d in range(4):
            whole = lax.dynamic_update_slice_in_dim(whole, pieces[d], (place[2 + level] ^ d) * wide, 1)
        return whole

    def kernel(place, *refs):
        for d in range(4):
            refs[4][:, lanes(place[2 + level] ^ d, wide)] = refs[d][...]

    return small_call(
        kernel, [jax.ShapeDtypeStruct((rows, 4 * wide), jnp.bfloat16)], place, *pieces
    )[0]


def joined_outputs(place, pieces, cuts):
    wide = pieces[0].shape[1]
    bounds = list(zip((0,) + cuts, cuts + (pieces[0].shape[0],)))

    def kernel(place, *refs):
        for d in range(4):
            piece = refs[d][...].astype(jnp.float32)
            for out, (low, high) in zip(refs[4:], bounds):
                out[:, lanes(place[2] ^ d, wide)] = piece[low:high, :]

    shapes = [jax.ShapeDtypeStruct((high - low, 4 * wide), jnp.float32) for low, high in bounds]
    return small_call(kernel, shapes, place, *pieces)


def per_device(
    queries,
    layer_key_rows,
    layer_value_rows,
    output_gradient,
    output_row_sums,
    shifted_head_flags,
    inputs,
    adapter_down_weight,
    query_up_weight,
    key_value_up_weight,
):
    seq_count = lax.axis_size("seq")
    seq_index = lax.axis_index("seq")
    tokens, width = queries.shape
    kv_width = layer_key_rows.shape[1]
    whole_len = tokens * seq_count
    rank = adapter_down_weight.shape[1]
    assert GROUP == 4 * tokens and SHIFT == 2 * tokens
    levels = (seq_count.bit_length() - 1) // 2
    assert 4**levels == seq_count
    flattened_down = adapter_down_weight.reshape(3 * rank, width)
    place = jnp.stack(
        [seq_index % 2, seq_index // 2 % 2] + [seq_index // 4**i % 4 for i in range(levels)]
    ).astype(jnp.int32)

    own_pair = (layer_key_rows, layer_value_rows)
    sib_pair = [exchanged(a, "seq", 1) for a in own_pair]
    pc_pair = [moved(a, "seq", 2) for a in own_pair]

    down_low = summed(mm(flattened_down, inputs, NT), "head").astype(jnp.bfloat16)
    down_tiled = jnp.tile(down_low[:rank].T, (1, HEAD_SIZE // rank))
    down_own = down_low[rank:]
    down_pc = moved(down_own, "seq", 2)

    own, previous = attention(
        place,
        shifted_head_flags,
        queries,
        output_gradient,
        output_row_sums,
        query_up_weight,
        down_tiled,
        own_pair,
        sib_pair,
    )
    own_grads, pc_pair, down_pc = lax.optimization_barrier((own(), pc_pair, down_pc))
    px_pair = [exchanged(a, "seq", 1) for a in pc_pair]
    down_others = exchanged(jnp.concatenate([down_own, down_pc]), "seq", 1)
    down_win = jnp.concatenate(
        [down_others[: 2 * rank], down_own, down_pc, down_others[2 * rank :]], axis=1
    )
    keep_own, keep_pc, send, up_q, up_keep, up_send, grad_q, grad_kv = previous(
        pc_pair, px_pair, own_grads, key_value_up_weight, down_win
    )

    up_kv = up_keep + exchanged(up_send, "seq", 1)
    received = exchanged(send, "seq", 1).astype(jnp.float32)
    back = (keep_pc + received[1]).astype(jnp.bfloat16)
    kv_total = keep_own + received[0]
    up_prev = moved(up_kv[:, tokens:], "seq", -2)
    up_prev, back = lax.optimization_barrier((up_prev, back))
    back = moved(back, "seq", -2)
    up_low = summed(jnp.concatenate([up_q, up_kv[:, :tokens] + up_prev]), "head").astype(jnp.bfloat16)

    pieces = first_pieces(
        place, up_low, inputs, grad_q, grad_kv.reshape(-1, width), adapter_scale / math.sqrt(whole_len)
    )
    for level in range(levels):
        pieces = exchanged_pieces(pieces, "seq", 4**level)
        if level < levels - 1:
            pieces = summed_into_four(place, level + 1, pieces)
    total = sum(p.astype(jnp.float32) for p in pieces).astype(jnp.bfloat16)
    total, back = lax.optimization_barrier((total, back))
    key_value_gradient = (kv_total + back.astype(jnp.float32)).astype(jnp.bfloat16)
    grad_inputs = (
        adapter_scale
        * lax.dot_general(
            up_low, flattened_down, (((0,), (0,)), ((), ())), preferred_element_type=jnp.float32
        )
    ).astype(jnp.bfloat16)
    for level in range(levels - 1, -1, -1):
        pieces = exchanged_pieces([total] * 4, "seq", 4**level)
        if level:
            total = joined(place, level, pieces)
    down_gradient, grad_up_q, grad_up_kv = joined_outputs(place, pieces, (3 * rank, 4 * rank))
    return (
        grad_inputs,
        key_value_gradient,
        down_gradient.reshape(3, rank, width),
        grad_up_q,
        grad_up_kv.reshape(2, rank, kv_width),
    )


def solution(mesh):
    placed = (
        P("seq", "head"),
        P("seq", "head"),
        P("seq", "head"),
        P("seq", "head"),
        P("head", "seq"),
        P("head"),
        P("seq", "head"),
        P(None, None, "head"),
        P(None, "head"),
        P(None, None, "head"),
    )
    return jax.shard_map(
        per_device,
        mesh=mesh,
        in_specs=placed,
        out_specs=(
            P("seq", "head"),
            P(None, "seq", "head"),
            P(None, None, "head"),
            P(None, "head"),
            P(None, None, "head"),
        ),
        check_vma=False,
    )
```

```python
import functools
import math

import jax
import jax.numpy as jnp
from jax import lax
from jax.experimental import pallas as pl
from jax.experimental.pallas import tpu as pltpu
from jax.sharding import PartitionSpec as P

HEAD_SIZE = 128
GROUP = 1024
SHIFT = 512
CHUNK = 32
VMEM_LIMIT = 24 * 1024 * 1024

adapter_scale = 2.0
masked_score = -1e30
score_scale = HEAD_SIZE ** (-0.5)
exp2_scale = score_scale * math.log2(math.e)

NT = (((1,), (1,)), ((), ()))
NN = (((1,), (0,)), ((), ()))


def mm(left, right, dims=NN):
    return lax.dot_general(left, right, dims, preferred_element_type=jnp.float32)


def head_batch(
    heads, low, high, diag, tokens, q_ref, do_ref, term_ref, down, up_q,
    kwin, vwin, wk, s_ref, e_ref, ds_ref, dk_acc, dv_acc,
):
    count = len(heads)
    wide = count * tokens
    rank = up_q.shape[0]
    columns = [pl.ds(pl.multiple_of(h * HEAD_SIZE, HEAD_SIZE), HEAD_SIZE) for h in heads]
    query = jnp.concatenate([q_ref[:, c] for c in columns], axis=0)
    grad = jnp.concatenate([do_ref[:, c] for c in columns], axis=0)
    term = jnp.concatenate([term_ref[pl.ds(h, 1), :] for h in heads], axis=1)
    top = None
    for row in range(low, high, tokens):
        scores = mm(kwin[row : row + tokens, :], query, NT)
        if row == diag:
            key_row = lax.broadcasted_iota(jnp.int32, (tokens, tokens), 0)
            query_row = lax.broadcasted_iota(jnp.int32, (tokens, tokens), 1)
            seen = jnp.concatenate([key_row <= query_row] * count, axis=1)
            scores = jnp.where(seen, scores, masked_score)
        s_ref[row : row + tokens, :wide] = scores
        here = jnp.max(scores.reshape(tokens // 8, 8, wide), axis=0)
        top = here if top is None else jnp.maximum(top, here)
    top = jnp.max(top, axis=0, keepdims=True)
    total = jnp.zeros((8, wide), jnp.float32)
    for row in range(low, high, tokens):
        grad_probs = mm(vwin[row : row + tokens, :], grad, NT)
        for at in range(0, tokens, CHUNK):
            rows = slice(row + at, row + at + CHUNK)
            weights = jnp.exp2((s_ref[rows, :wide] - top) * exp2_scale)
            total = total + jnp.sum(weights.reshape(CHUNK // 8, 8, wide), axis=0)
            e_ref[rows, :wide] = weights.astype(jnp.bfloat16)
            ds_ref[rows, :wide] = (weights * (grad_probs[at : at + CHUNK, :] - term)).astype(jnp.bfloat16)
    inverse = 1.0 / jnp.sum(total, axis=0, keepdims=True)
    inverse_rows = jnp.broadcast_to(inverse, (HEAD_SIZE, wide)).T
    grad_n = (grad.astype(jnp.float32) * inverse_rows).astype(jnp.bfloat16)
    lane = lax.broadcasted_iota(jnp.int32, (tokens, HEAD_SIZE), 1) // rank
    tiled = down[...].astype(jnp.float32)
    own_columns = jnp.concatenate([jnp.where(lane == h, tiled, 0.0) for h in heads], axis=0)
    scaled = inverse_rows * score_scale
    query_n = jnp.concatenate(
        [query.astype(jnp.float32) * scaled, own_columns * scaled], axis=1
    ).astype(jnp.bfloat16)
    dv_acc[low:high, :] += mm(e_ref[low:high, :wide], grad_n)
    dk_acc[low:high, :] += mm(ds_ref[low:high, :wide], query_n)
    back = None
    for i, h in enumerate(heads):
        own = slice(i * tokens, (i + 1) * tokens)
        part = mm(wk[pl.ds(pl.multiple_of(h * rank, rank), rank), low:high], ds_ref[low:high, own])
        part = part * (inverse[:, own] * score_scale)
        back = part if back is None else back + part
    up_q[...] += back


def all_heads(with_previous, per_kv, tokens, place_ref, flags_ref, q_ref, do_ref, term_ref, down, up_q, listed, *scratch):
    first = pl.program_id(0) * per_kv
    core = place_ref[0]
    half = place_ref[1]
    count = jnp.int32(0)
    for h in range(per_kv):
        listed[count] = jnp.int32(h)
        needs = flags_ref[first + h] != half
        count = count + jnp.where(needs == with_previous, 1, 0).astype(jnp.int32)
    high = (4 if with_previous else 2) * tokens
    for which in range(2):
        low = (1 - which) * tokens
        run = functools.partial(
            head_batch,
            low=low,
            high=high,
            diag=tokens,
            tokens=tokens,
            q_ref=q_ref,
            do_ref=do_ref,
            term_ref=term_ref,
            down=down,
            up_q=up_q,
            **dict(zip(("kwin", "vwin", "wk", "s_ref", "e_ref", "ds_ref", "dk_acc", "dv_acc"), scratch)),
        )

        @pl.when(core == which)
        def _():
            def pair(i, carry):
                run([listed[2 * i], listed[2 * i + 1]])
                return carry

            lax.fori_loop(0, count // 2, pair, 0)

            @pl.when(count % 2 == 1)
            def _():
                run([listed[count - 1]])


def fill_window(per_kv, tokens, kwin, vwin, wk, w_q, blocks):
    for at, (key, value) in enumerate(blocks):
        rows = slice(at * tokens, (at + 1) * tokens)
        kwin[rows, :] = key[...]
        vwin[rows, :] = value[...]
    stacked = jnp.concatenate(
        [w_q[:, h * HEAD_SIZE : (h + 1) * HEAD_SIZE] for h in range(per_kv)], axis=0
    )
    wk[...] = mm(stacked, kwin[...], NT).astype(jnp.bfloat16)


def own_kernel(
    per_kv, tokens, place, flags, q, do, term, w_q, down, k_own, v_own, k_sib, v_sib,
    up_q, dk, dv,
    listed, kwin, vwin, wk, s, e, ds,
):
    fill_window(per_kv, tokens, kwin, vwin, wk, w_q, [(k_sib, v_sib), (k_own, v_own)])
    dk[...] = jnp.zeros_like(dk)
    dv[...] = jnp.zeros_like(dv)

    @pl.when(pl.program_id(0) == 0)
    def _():
        up_q[...] = jnp.zeros_like(up_q)

    all_heads(False, per_kv, tokens, place, flags, q, do, term, down, up_q, listed, kwin, vwin, wk, s, e, ds, dk, dv)


def previous_kernel(
    per_kv, tokens, rank, place, flags, q, do, term, w_q, down, k_own, v_own, k_sib, v_sib, k_pc, v_pc, k_px, v_px,
    up_q_own, dk_own, dv_own, w_kv, down_win,
    keep_own, keep_pc, send, ups, grad_q, grad_kv,
    listed, kwin, vwin, wk, s, e, ds, dk, dv, up_q, up_kv,
):
    fill_window(
        per_kv, tokens, kwin, vwin, wk, w_q, [(k_sib, v_sib), (k_own, v_own), (k_pc, v_pc), (k_px, v_px)]
    )
    for acc, start in ((dk, dk_own), (dv, dv_own)):
        acc[: 2 * tokens, :] = start[...]
        acc[2 * tokens :, :] = jnp.zeros((2 * tokens, acc.shape[1]), jnp.float32)

    @pl.when(pl.program_id(0) == 0)
    def _():
        up_q[...] = up_q_own[...]
        up_kv[...] = jnp.zeros_like(up_kv)

    all_heads(True, per_kv, tokens, place, flags, q, do, term, down, up_q, listed, kwin, vwin, wk, s, e, ds, dk, dv)
    by_head = mm(dk[:, HEAD_SIZE:].T.astype(jnp.bfloat16), kwin[...])
    for h in range(per_kv):
        grad_q[:, h * HEAD_SIZE : (h + 1) * HEAD_SIZE] = by_head[h * rank : (h + 1) * rank, :]
    for c, acc in ((0, dk), (1, dv)):
        total = acc[:, :HEAD_SIZE]
        keep_own[c] = total[tokens : 2 * tokens, :]
        keep_pc[c] = total[2 * tokens : 3 * tokens, :]
        low = total.astype(jnp.bfloat16)
        send[0, c] = low[:tokens, :]
        send[1, c] = low[3 * tokens :, :]
        up = mm(w_kv[c], low, NT)
        for block in range(4):
            at = (2 * block + c) * rank
            up_kv[at : at + rank, :] += up[:, block * tokens : (block + 1) * tokens]
        own = slice(c * rank, (c + 1) * rank)
        grad_kv[own, :] = mm(down_win[own, :], low)

    @pl.when(pl.program_id(0) == pl.num_programs(0) - 1)
    def _():
        ups[...] = jnp.concatenate([up_q[...], up_kv[...]]).astype(jnp.bfloat16)


def attention(place, flags, queries, grads, terms, w_q, down, own_pair, sib_pair):
    tokens, width = queries.shape
    kv_width = own_pair[0].shape[1]
    kv_local = kv_width // HEAD_SIZE
    per_kv = width // kv_width
    rank = w_q.shape[0]
    assert per_kv * rank == HEAD_SIZE
    block = per_kv * HEAD_SIZE
    smem = pl.BlockSpec(memory_space=pltpu.SMEM)

    def columns(rows, wide):
        return pl.BlockSpec((rows, wide), lambda g: (0, g))

    def stacked(*lead):
        return pl.BlockSpec((*lead, tokens, HEAD_SIZE), lambda g: (0,) * (len(lead) + 1) + (g,))

    def fixed(*shape):
        return pl.BlockSpec(shape, lambda g: (0,) * len(shape))

    def scratch(blocks):
        rows = blocks * tokens
        return [
            pltpu.SMEM((per_kv + 1,), jnp.int32),
            pltpu.VMEM((rows, HEAD_SIZE), jnp.bfloat16),
            pltpu.VMEM((rows, HEAD_SIZE), jnp.bfloat16),
            pltpu.VMEM((HEAD_SIZE, rows), jnp.bfloat16),
            pltpu.VMEM((rows, 2 * tokens), jnp.float32),
            pltpu.VMEM((rows, 2 * tokens), jnp.bfloat16),
            pltpu.VMEM((rows, 2 * tokens), jnp.bfloat16),
        ]

    key_spec = columns(tokens, HEAD_SIZE)
    per_head_specs = [
        smem,
        smem,
        columns(tokens, block),
        columns(tokens, block),
        pl.BlockSpec((per_kv, tokens), lambda g: (g, 0)),
        columns(rank, block),
        fixed(tokens, HEAD_SIZE),
    ] + [key_spec] * 4
    queries, grads = (pltpu.with_memory_space_constraint(a, pltpu.HBM) for a in (queries, grads))
    per_head = (place, flags, queries, grads, terms, w_q, down, *own_pair, *sib_pair)
    params = pltpu.CompilerParams(dimension_semantics=("arbitrary",), vmem_limit_bytes=VMEM_LIMIT)
    f32, bf16 = jnp.float32, jnp.bfloat16
    shape = jax.ShapeDtypeStruct
    pairs = kv_local * per_kv * tokens * tokens

    def own():
        return pl.pallas_call(
            functools.partial(own_kernel, per_kv, tokens),
            grid=(kv_local,),
            in_specs=per_head_specs,
            out_specs=[fixed(rank, tokens), columns(2 * tokens, 2 * HEAD_SIZE), columns(2 * tokens, HEAD_SIZE)],
            out_shape=[
                shape((rank, tokens), f32),
                shape((2 * tokens, 2 * kv_width), f32),
                shape((2 * tokens, kv_width), f32),
            ],
            scratch_shapes=scratch(2),
            compiler_params=params,
            cost_estimate=pl.CostEstimate(
                flops=40 * pairs * HEAD_SIZE, bytes_accessed=6 * tokens * width, transcendentals=pairs
            ),
            name="own_chip_heads",
        )(*per_head)

    def previous(pc_pair, px_pair, own_grads, w_kv, down_win):
        return pl.pallas_call(
            functools.partial(previous_kernel, per_kv, tokens, rank),
            grid=(kv_local,),
            in_specs=per_head_specs
            + [key_spec] * 4
            + [
                fixed(rank, tokens),
                columns(2 * tokens, 2 * HEAD_SIZE),
                columns(2 * tokens, HEAD_SIZE),
                pl.BlockSpec((2, rank, HEAD_SIZE), lambda g: (0, 0, g)),
                fixed(2 * rank, 4 * tokens),
            ],
            out_specs=[
                stacked(2),
                stacked(2),
                stacked(2, 2),
                fixed(9 * rank, tokens),
                columns(rank, block),
                columns(2 * rank, HEAD_SIZE),
            ],
            out_shape=[
                shape((2, tokens, kv_width), f32),
                shape((2, tokens, kv_width), f32),
                shape((2, 2, tokens, kv_width), bf16),
                shape((9 * rank, tokens), bf16),
                shape((rank, width), f32),
                shape((2 * rank, kv_width), f32),
            ],
            scratch_shapes=scratch(4)
            + [
                pltpu.VMEM((4 * tokens, 2 * HEAD_SIZE), f32),
                pltpu.VMEM((4 * tokens, HEAD_SIZE), f32),
                pltpu.VMEM((rank, tokens), f32),
                pltpu.VMEM((8 * rank, tokens), f32),
            ],
            compiler_params=params,
            cost_estimate=pl.CostEstimate(
                flops=80 * pairs * HEAD_SIZE, bytes_accessed=12 * tokens * width, transcendentals=2 * pairs
            ),
            name="previous_chip_heads",
        )(*per_head, *pc_pair, *px_pair, *own_grads, w_kv, down_win)

    return own, previous


def exchanged(value, axis, bit):
    return lax.ppermute(value, axis, [(i, i ^ bit) for i in range(lax.axis_size(axis))])


def moved(value, axis, by):
    count = lax.axis_size(axis)
    return lax.ppermute(value, axis, [(i, (i + by) % count) for i in range(count)])


def summed(value, axis):
    bit = 1
    while bit < lax.axis_size(axis):
        value = value + exchanged(value, axis, bit)
        bit *= 2
    return value


def small_call(kernel, out_shape, *args):
    vmem = pl.BlockSpec(memory_space=pltpu.VMEM)
    return pl.pallas_call(
        kernel,
        in_specs=[vmem] * len(args),
        out_specs=[vmem] * len(out_shape),
        out_shape=out_shape,
        compiler_params=pltpu.CompilerParams(vmem_limit_bytes=VMEM_LIMIT),
    )(*args)


def head_sum(ups, rank):
    count = lax.axis_size("head")
    bit = 1
    while 2 * bit < count:
        other = exchanged(ups, "head", bit)
        ups = (ups.astype(jnp.float32) + other.astype(jnp.float32)).astype(jnp.bfloat16)
        bit *= 2
    other = exchanged(ups, "head", bit)
    tokens = ups.shape[1]

    def kernel(here, there, mine, *others):
        total = here[...].astype(jnp.float32) + there[...].astype(jnp.float32)
        mine[...] = jnp.concatenate([total[:rank], total[3 * rank : 5 * rank]])
        for out, at in zip(others, (rank, 5 * rank, 7 * rank)):
            out[...] = total[at : at + 2 * rank].astype(jnp.bfloat16)

    shape = jax.ShapeDtypeStruct
    return small_call(
        kernel,
        [shape((3 * rank, tokens), jnp.float32)] + [shape((2 * rank, tokens), jnp.bfloat16)] * 3,
        ups,
        other,
    )


def weight_pieces(count, mine, others, inputs, grad_q, grad_kv, scale):
    width = inputs.shape[1]
    wide = width // count
    rank = grad_q.shape[0]
    extra = grad_kv.size // width
    rows = 4 * rank + extra
    aligned = wide % HEAD_SIZE == 0 and grad_kv.shape[1] % wide == 0
    up_shape = jax.ShapeDtypeStruct(mine.shape, jnp.bfloat16)

    def up_total(mine, others):
        tail = mine[rank:, :] + sum(o[...].astype(jnp.float32) for o in others)
        return jnp.concatenate([mine[:rank, :], tail]).astype(jnp.bfloat16)

    if not aligned:
        up_low = up_total(mine, others)
        whole = jnp.concatenate([mm(up_low, inputs), grad_q, grad_kv.reshape(extra, width)]) * scale
        pieces = whole.astype(jnp.bfloat16).reshape(rows, count, wide).transpose(1, 0, 2)
        return up_low, pieces
    lanes = grad_kv.shape[1] // wide
    deep = extra // lanes

    def kernel(mine, one, two, three, tokens_in, q, kv, up_low, pieces):
        up = up_total(mine, (one, two, three))
        up_low[...] = up
        for j in range(count):
            at = slice(j * wide, (j + 1) * wide)
            tail = [
                kv[j * deep : (j + 1) * deep, i * wide : (i + 1) * wide] for i in range(lanes)
            ]
            piece = jnp.concatenate([mm(up, tokens_in[:, at]), q[:, at], *tail]) * scale
            pieces[j] = piece.astype(jnp.bfloat16)

    return small_call(
        kernel,
        [up_shape, jax.ShapeDtypeStruct((count, rows, wide), jnp.bfloat16)],
        mine,
        *others,
        inputs,
        grad_q,
        grad_kv,
    )


def joined_pieces(pieces, rank, kv_shape):
    count, rows, wide = pieces.shape
    width = count * wide
    extra = rows - 4 * rank
    if wide % HEAD_SIZE or kv_shape[1] % wide:
        whole = pieces.transpose(1, 0, 2).reshape(rows, width).astype(jnp.float32)
        return whole[: 3 * rank], whole[3 * rank : 4 * rank], whole[4 * rank :].reshape(kv_shape)
    lanes = kv_shape[1] // wide
    deep = extra // lanes

    def kernel(pieces, down, up_q, up_kv):
        for j in range(count):
            at = slice(j * wide, (j + 1) * wide)
            piece = pieces[j].astype(jnp.float32)
            down[:, at] = piece[: 3 * rank]
            up_q[:, at] = piece[3 * rank : 4 * rank]
            for i in range(lanes):
                low = 4 * rank + i * deep
                up_kv[j * deep : (j + 1) * deep, i * wide : (i + 1) * wide] = piece[low : low + deep]

    shape = jax.ShapeDtypeStruct
    return small_call(
        kernel,
        [
            shape((3 * rank, width), jnp.float32),
            shape((rank, width), jnp.float32),
            shape(kv_shape, jnp.float32),
        ],
        pieces,
    )


def per_device(
    queries,
    layer_key_rows,
    layer_value_rows,
    output_gradient,
    output_row_sums,
    shifted_head_flags,
    inputs,
    adapter_down_weight,
    query_up_weight,
    key_value_up_weight,
):
    seq_count = lax.axis_size("seq")
    seq_index = lax.axis_index("seq")
    tokens, width = queries.shape
    kv_width = layer_key_rows.shape[1]
    whole_len = tokens * seq_count
    rank = adapter_down_weight.shape[1]
    assert GROUP == 4 * tokens and SHIFT == 2 * tokens
    flattened_down = adapter_down_weight.reshape(3 * rank, width)
    place = jnp.stack([seq_index % 2, seq_index // 2 % 2]).astype(jnp.int32)

    own_pair = (layer_key_rows, layer_value_rows)
    sib_pair = [exchanged(a, "seq", 1) for a in own_pair]
    pc_pair = [moved(a, "seq", 2) for a in own_pair]

    down_low = summed(mm(flattened_down, inputs, NT), "head").astype(jnp.bfloat16)
    down_tiled = jnp.tile(down_low[:rank].T, (1, HEAD_SIZE // rank))
    down_own = down_low[rank:]
    down_pc = moved(down_own, "seq", 2)

    own, previous = attention(
        place,
        shifted_head_flags,
        queries,
        output_gradient,
        output_row_sums,
        query_up_weight,
        down_tiled,
        own_pair,
        sib_pair,
    )
    own_grads, pc_pair, down_pc = lax.optimization_barrier((own(), pc_pair, down_pc))
    px_pair = [exchanged(a, "seq", 1) for a in pc_pair]
    down_others = exchanged(jnp.concatenate([down_own, down_pc]), "seq", 1)
    down_win = jnp.concatenate(
        [down_others[: 2 * rank], down_own, down_pc, down_others[2 * rank :]], axis=1
    )
    keep_own, keep_pc, send, ups, grad_q, grad_kv = previous(
        pc_pair, px_pair, own_grads, key_value_up_weight, down_win
    )

    mine, up_sib, up_pc, up_px = head_sum(ups, rank)
    received = exchanged(send, "seq", 1).astype(jnp.float32)
    back = (keep_pc + received[1]).astype(jnp.bfloat16)
    kv_total = keep_own + received[0]
    up_others = [
        exchanged(up_sib, "seq", 1),
        moved(up_pc, "seq", -2),
        lax.ppermute(up_px, "seq", [(i, (i - 2) % seq_count ^ 1) for i in range(seq_count)]),
    ]
    up_others, back = lax.optimization_barrier((up_others, back))
    back = moved(back, "seq", -2)

    up_low, pieces = weight_pieces(
        seq_count, mine, up_others, inputs, grad_q, grad_kv, adapter_scale / math.sqrt(whole_len)
    )
    pieces = lax.all_to_all(pieces, "seq", 0, 0, tiled=True)
    total = jnp.sum(pieces.astype(jnp.float32), axis=0).astype(jnp.bfloat16)
    grad_inputs = (
        adapter_scale
        * lax.dot_general(
            up_low, flattened_down, (((0,), (0,)), ((), ())), preferred_element_type=jnp.float32
        )
    ).astype(jnp.bfloat16)
    pieces = lax.all_gather(total, "seq")
    key_value_gradient = (kv_total + back.astype(jnp.float32)).astype(jnp.bfloat16)
    down_gradient, grad_up_q, grad_up_kv = joined_pieces(pieces, rank, (2 * rank, kv_width))
    return (
        grad_inputs,
        key_value_gradient,
        down_gradient.reshape(3, rank, width),
        grad_up_q,
        grad_up_kv.reshape(2, rank, kv_width),
    )


def solution(mesh):
    placed = (
        P("seq", "head"),
        P("seq", "head"),
        P("seq", "head"),
        P("seq", "head"),
        P("head", "seq"),
        P("head"),
        P("seq", "head"),
        P(None, None, "head"),
        P(None, "head"),
        P(None, None, "head"),
    )
    return jax.shard_map(
        per_device,
        mesh=mesh,
        in_specs=placed,
        out_specs=(
            P("seq", "head"),
            P(None, "seq", "head"),
            P(None, None, "head"),
            P(None, "head"),
            P(None, None, "head"),
        ),
        check_vma=False,
    )
```

```python
import functools
import math

import jax
import jax.numpy as jnp
from jax import lax
from jax.experimental import pallas as pl
from jax.experimental.pallas import tpu as pltpu
from jax.sharding import PartitionSpec as P

HEAD_SIZE = 128
GROUP = 1024
SHIFT = 512
CHUNK = 32
VMEM_LIMIT = 32 * 1024 * 1024

adapter_scale = 2.0
masked_score = -1e30
score_scale = HEAD_SIZE ** (-0.5)
exp2_scale = score_scale * math.log2(math.e)

NT = (((1,), (1,)), ((), ()))
NN = (((1,), (0,)), ((), ()))


def mm(left, right, dims=NN):
    return lax.dot_general(left, right, dims, preferred_element_type=jnp.float32)


def scores_and_softmax(head, low, diag, keys, values, q_ref, do_ref, term_ref, slot):
    tokens = q_ref.shape[0]
    s_ref, e_ref, ds_ref, inv_ref = slot
    group, column, key_column = head
    query = q_ref[:, column]
    grad = do_ref[:, column]
    term = term_ref[pl.ds(group[0], 1), :]
    top = None
    for block in range(low, len(keys)):
        rows = slice(block * tokens, (block + 1) * tokens)
        scores = mm(keys[block][:, key_column], query, NT)
        if block == diag:
            key_row = lax.broadcasted_iota(jnp.int32, (tokens, tokens), 0)
            query_row = lax.broadcasted_iota(jnp.int32, (tokens, tokens), 1)
            scores = jnp.where(key_row <= query_row, scores, masked_score)
        s_ref[rows, :] = scores
        here = jnp.max(scores.reshape(tokens // 8, 8, tokens), axis=0)
        top = here if top is None else jnp.maximum(top, here)
    top = jnp.max(top, axis=0, keepdims=True)
    total = jnp.zeros((8, tokens), jnp.float32)
    for block in range(low, len(keys)):
        grad_probs = mm(values[block][:, key_column], grad, NT)
        for at in range(0, tokens, CHUNK):
            rows = slice(block * tokens + at, block * tokens + at + CHUNK)
            weights = jnp.exp2((s_ref[rows, :] - top) * exp2_scale)
            total = total + jnp.sum(weights.reshape(CHUNK // 8, 8, tokens), axis=0)
            e_ref[rows, :] = weights.astype(jnp.bfloat16)
            ds_ref[rows, :] = (weights * (grad_probs[at : at + CHUNK, :] - term)).astype(jnp.bfloat16)
    inv_ref[...] = 1.0 / jnp.sum(total, axis=0, keepdims=True)


def add_gradients(head, valid, low, high, rank, q_ref, do_ref, down, up_q, wk, dk_acc, dv_acc, slot):
    tokens = q_ref.shape[0]
    _, e_ref, ds_ref, inv_ref = slot
    (_, group, inner), column, _ = head
    height = wk.shape[1]
    inverse = inv_ref[...] * valid
    inverse_rows = jnp.broadcast_to(inverse, (HEAD_SIZE, tokens)).T
    scaled = inverse_rows * score_scale
    lane = lax.broadcasted_iota(jnp.int32, (tokens, HEAD_SIZE), 1) // rank
    own_columns = jnp.where(lane == inner, down[...].astype(jnp.float32), 0.0)
    grad_n = (do_ref[:, column].astype(jnp.float32) * inverse_rows).astype(jnp.bfloat16)
    query_n = jnp.concatenate(
        [q_ref[:, column].astype(jnp.float32) * scaled, own_columns * scaled], axis=1
    ).astype(jnp.bfloat16)
    rows = pl.ds(pl.multiple_of(group * height + low, tokens), high - low)
    dv_acc[rows, :] += mm(e_ref[low:high, :], grad_n)
    dk_acc[rows, :] += mm(ds_ref[low:high, :], query_n)
    own = pl.ds(pl.multiple_of(group * HEAD_SIZE + inner * rank, rank), rank)
    up_q[...] += mm(wk[own, low:high], ds_ref[low:high, :]) * (inverse * score_scale)


def all_heads(with_previous, per_kv, rank, place, flags, keys, values, q, do, term, w_q, down, up_q, dk, dv, scratch):
    listed, wk, *buffers = scratch
    tokens, width = q.shape
    height = wk.shape[1]
    groups = width // (per_kv * HEAD_SIZE)
    for g in range(groups):
        stacked = jnp.concatenate(
            [w_q[:, h * HEAD_SIZE : (h + 1) * HEAD_SIZE] for h in range(g * per_kv, (g + 1) * per_kv)], axis=0
        )
        for block, key in enumerate(keys):
            wk[g * HEAD_SIZE : (g + 1) * HEAD_SIZE, block * tokens : (block + 1) * tokens] = mm(
                stacked, key[:, g * HEAD_SIZE : (g + 1) * HEAD_SIZE], NT
            ).astype(jnp.bfloat16)
    dk[...] = jnp.zeros_like(dk)
    dv[...] = jnp.zeros_like(dv)
    slots = (buffers[:4], buffers[4:])
    for _, e_ref, ds_ref, inv_ref in slots:
        e_ref[...] = jnp.zeros_like(e_ref)
        ds_ref[...] = jnp.zeros_like(ds_ref)
        inv_ref[...] = jnp.zeros_like(inv_ref)
    core = place[0]
    half = place[1]
    count = jnp.int32(0)
    for h in range(groups * per_kv):
        listed[count] = jnp.int32(h)
        needs = flags[h] != half
        count = count + jnp.where(needs == with_previous, 1, 0).astype(jnp.int32)

    def head_at(i):
        h = listed[jnp.clip(i, 0, count - 1)]
        group = h // per_kv
        return (
            (h, group, h - group * per_kv),
            pl.ds(pl.multiple_of(h * HEAD_SIZE, HEAD_SIZE), HEAD_SIZE),
            pl.ds(pl.multiple_of(group * HEAD_SIZE, HEAD_SIZE), HEAD_SIZE),
        )

    for which in range(2):
        low = 1 - which

        def softmax(i, slot):
            scores_and_softmax(head_at(i), low, 1, keys, values, q, do, term, slot)

        def gradients(i, slot):
            valid = jnp.where((i >= 0) & (i < count), 1.0, 0.0).astype(jnp.float32)
            add_gradients(
                head_at(i), valid, low * tokens, height, rank, q, do, down, up_q, wk, dk, dv, slot
            )

        @pl.when((core == which) & (count > 0))
        def _():
            def two(t, carry):
                softmax(2 * t, slots[0])
                gradients(2 * t - 1, slots[1])
                softmax(2 * t + 1, slots[1])
                gradients(2 * t, slots[0])
                return carry

            lax.fori_loop(0, (count + 1) // 2, two, 0)

            @pl.when(count % 2 == 0)
            def _():
                gradients(count - 1, slots[1])


def own_kernel(
    per_kv, rank, place, flags, q, do, term, w_q, down, k_own, v_own, k_sib, v_sib, up_q, dk, dv, *scratch
):
    up_q[...] = jnp.zeros_like(up_q)
    all_heads(
        False, per_kv, rank, place, flags, (k_sib, k_own), (v_sib, v_own), q, do, term, w_q, down, up_q, dk, dv, scratch
    )


def previous_kernel(
    per_kv, rank, place, flags, q, do, term, w_q, down, k_own, v_own, k_sib, v_sib, k_pc, v_pc, k_px, v_px,
    up_q_own, dk_own, dv_own, w_kv, down_win,
    keep_own, keep_pc, send, ups, grad_q, grad_kv,
    dk, dv, up_q, *scratch,
):
    tokens = q.shape[0]
    up_q[...] = up_q_own[...]
    keys = (k_sib, k_own, k_pc, k_px)
    values = (v_sib, v_own, v_pc, v_px)
    all_heads(True, per_kv, rank, place, flags, keys, values, q, do, term, w_q, down, up_q, dk, dv, scratch)
    up_kv = [jnp.zeros((rank, 4 * tokens), jnp.float32) for _ in range(2)]
    for g in range(k_own.shape[1] // HEAD_SIZE):
        columns = slice(g * HEAD_SIZE, (g + 1) * HEAD_SIZE)
        low_row, own_row = g * 4 * tokens, g * 2 * tokens
        by_head = None
        for block in range(4):
            tail = dk[low_row + block * tokens : low_row + (block + 1) * tokens, HEAD_SIZE:]
            if block < 2:
                tail = tail + dk_own[own_row + block * tokens : own_row + (block + 1) * tokens, HEAD_SIZE:]
            part = mm(tail.T.astype(jnp.bfloat16), keys[block][:, columns])
            by_head = part if by_head is None else by_head + part
        for h in range(per_kv):
            at = (g * per_kv + h) * HEAD_SIZE
            grad_q[:, at : at + HEAD_SIZE] = by_head[h * rank : (h + 1) * rank, :]
        for c, acc, start in ((0, dk, dk_own), (1, dv, dv_own)):
            total = acc[low_row : low_row + 4 * tokens, :HEAD_SIZE]
            near = total[: 2 * tokens] + start[own_row : own_row + 2 * tokens, :HEAD_SIZE]
            low = jnp.concatenate([near, total[2 * tokens :]]).astype(jnp.bfloat16)
            keep_own[c, :, columns] = near[tokens:]
            keep_pc[c, :, columns] = total[2 * tokens : 3 * tokens]
            send[0, c, :, columns] = low[:tokens]
            send[1, c, :, columns] = low[3 * tokens :]
            up_kv[c] = up_kv[c] + mm(w_kv[c, :, columns], low, NT)
            own = slice(c * rank, (c + 1) * rank)
            grad_kv[own, columns] = mm(down_win[own, :], low)
    parts = [up_q[...]]
    for block in range(4):
        parts += [up_kv[c][:, block * tokens : (block + 1) * tokens] for c in range(2)]
    ups[...] = jnp.concatenate(parts).astype(jnp.bfloat16)


def attention(place, flags, queries, grads, terms, w_q, down, own_pair, sib_pair):
    tokens, width = queries.shape
    kv_width = own_pair[0].shape[1]
    kv_local = kv_width // HEAD_SIZE
    per_kv = width // kv_width
    rank = w_q.shape[0]
    assert per_kv * rank == HEAD_SIZE
    f32, bf16 = jnp.float32, jnp.bfloat16
    shape = jax.ShapeDtypeStruct
    pairs = kv_local * per_kv * tokens * tokens
    smem = pl.BlockSpec(memory_space=pltpu.SMEM)
    vmem = pl.BlockSpec(memory_space=pltpu.VMEM)

    def scratch(blocks):
        rows = blocks * tokens
        slot = [
            pltpu.VMEM((rows, tokens), f32),
            pltpu.VMEM((rows, tokens), bf16),
            pltpu.VMEM((rows, tokens), bf16),
            pltpu.VMEM((1, tokens), f32),
        ]
        return [
            pltpu.SMEM((kv_local * per_kv + 1,), jnp.int32),
            pltpu.VMEM((kv_local * HEAD_SIZE, rows), bf16),
        ] + slot * 2

    def call(kernel, out_shape, scratch_shapes, work, name, *args):
        return pl.pallas_call(
            functools.partial(kernel, per_kv, rank),
            in_specs=[smem, smem] + [vmem] * (len(args) - 2),
            out_specs=[vmem] * len(out_shape),
            out_shape=out_shape,
            scratch_shapes=scratch_shapes,
            compiler_params=pltpu.CompilerParams(vmem_limit_bytes=VMEM_LIMIT),
            cost_estimate=pl.CostEstimate(
                flops=work * pairs * HEAD_SIZE, bytes_accessed=6 * tokens * width, transcendentals=pairs
            ),
            name=name,
        )(*args)

    common = (place, flags, queries, grads, terms, w_q, down, *own_pair, *sib_pair)

    def own():
        return call(
            own_kernel,
            [
                shape((rank, tokens), f32),
                shape((2 * tokens * kv_local, 2 * HEAD_SIZE), f32),
                shape((2 * tokens * kv_local, HEAD_SIZE), f32),
            ],
            scratch(2),
            40,
            "own_chip_heads",
            *common,
        )

    def previous(pc_pair, px_pair, own_grads, w_kv, down_win):
        return call(
            previous_kernel,
            [
                shape((2, tokens, kv_width), f32),
                shape((2, tokens, kv_width), f32),
                shape((2, 2, tokens, kv_width), bf16),
                shape((9 * rank, tokens), bf16),
                shape((rank, width), f32),
                shape((2 * rank, kv_width), f32),
            ],
            [
                pltpu.VMEM((4 * tokens * kv_local, 2 * HEAD_SIZE), f32),
                pltpu.VMEM((4 * tokens * kv_local, HEAD_SIZE), f32),
                pltpu.VMEM((rank, tokens), f32),
            ]
            + scratch(4),
            80,
            "previous_chip_heads",
            *common,
            *pc_pair,
            *px_pair,
            *own_grads,
            w_kv,
            down_win,
        )

    return own, previous


def exchanged(value, axis, bit):
    return lax.ppermute(value, axis, [(i, i ^ bit) for i in range(lax.axis_size(axis))])


def moved(value, axis, by):
    count = lax.axis_size(axis)
    return lax.ppermute(value, axis, [(i, (i + by) % count) for i in range(count)])


def summed(value, axis):
    bit = 1
    while bit < lax.axis_size(axis):
        value = value + exchanged(value, axis, bit)
        bit *= 2
    return value


def small_call(kernel, out_shape, *args):
    vmem = pl.BlockSpec(memory_space=pltpu.VMEM)
    return pl.pallas_call(
        kernel,
        in_specs=[vmem] * len(args),
        out_specs=[vmem] * len(out_shape),
        out_shape=out_shape,
        compiler_params=pltpu.CompilerParams(vmem_limit_bytes=VMEM_LIMIT),
    )(*args)


def head_sum(ups, rank):
    count = lax.axis_size("head")
    bit = 1
    while 2 * bit < count:
        other = exchanged(ups, "head", bit)
        ups = (ups.astype(jnp.float32) + other.astype(jnp.float32)).astype(jnp.bfloat16)
        bit *= 2
    other = exchanged(ups, "head", bit)
    tokens = ups.shape[1]

    def kernel(here, there, mine, *others):
        total = here[...].astype(jnp.float32) + there[...].astype(jnp.float32)
        mine[...] = jnp.concatenate([total[:rank], total[3 * rank : 5 * rank]])
        for out, at in zip(others, (rank, 5 * rank, 7 * rank)):
            out[...] = total[at : at + 2 * rank].astype(jnp.bfloat16)

    shape = jax.ShapeDtypeStruct
    return small_call(
        kernel,
        [shape((3 * rank, tokens), jnp.float32)] + [shape((2 * rank, tokens), jnp.bfloat16)] * 3,
        ups,
        other,
    )


def weight_pieces(count, mine, others, inputs, grad_q, grad_kv, scale):
    width = inputs.shape[1]
    wide = width // count
    rank = grad_q.shape[0]
    extra = grad_kv.size // width
    rows = 4 * rank + extra
    aligned = wide % HEAD_SIZE == 0 and grad_kv.shape[1] % wide == 0
    up_shape = jax.ShapeDtypeStruct(mine.shape, jnp.bfloat16)

    def up_total(mine, others):
        tail = mine[rank:, :] + sum(o[...].astype(jnp.float32) for o in others)
        return jnp.concatenate([mine[:rank, :], tail]).astype(jnp.bfloat16)

    if not aligned:
        up_low = up_total(mine, others)
        whole = jnp.concatenate([mm(up_low, inputs), grad_q, grad_kv.reshape(extra, width)]) * scale
        pieces = whole.astype(jnp.bfloat16).reshape(rows, count, wide).transpose(1, 0, 2)
        return up_low, pieces
    lanes = grad_kv.shape[1] // wide
    deep = extra // lanes

    def kernel(mine, one, two, three, tokens_in, q, kv, up_low, pieces):
        up = up_total(mine, (one, two, three))
        up_low[...] = up
        for j in range(count):
            at = slice(j * wide, (j + 1) * wide)
            tail = [
                kv[j * deep : (j + 1) * deep, i * wide : (i + 1) * wide] for i in range(lanes)
            ]
            piece = jnp.concatenate([mm(up, tokens_in[:, at]), q[:, at], *tail]) * scale
            pieces[j] = piece.astype(jnp.bfloat16)

    return small_call(
        kernel,
        [up_shape, jax.ShapeDtypeStruct((count, rows, wide), jnp.bfloat16)],
        mine,
        *others,
        inputs,
        grad_q,
        grad_kv,
    )


def joined_pieces(pieces, rank, kv_shape):
    count, rows, wide = pieces.shape
    width = count * wide
    extra = rows - 4 * rank
    if wide % HEAD_SIZE or kv_shape[1] % wide:
        whole = pieces.transpose(1, 0, 2).reshape(rows, width).astype(jnp.float32)
        return whole[: 3 * rank], whole[3 * rank : 4 * rank], whole[4 * rank :].reshape(kv_shape)
    lanes = kv_shape[1] // wide
    deep = extra // lanes

    def kernel(pieces, down, up_q, up_kv):
        for j in range(count):
            at = slice(j * wide, (j + 1) * wide)
            piece = pieces[j].astype(jnp.float32)
            down[:, at] = piece[: 3 * rank]
            up_q[:, at] = piece[3 * rank : 4 * rank]
            for i in range(lanes):
                low = 4 * rank + i * deep
                up_kv[j * deep : (j + 1) * deep, i * wide : (i + 1) * wide] = piece[low : low + deep]

    shape = jax.ShapeDtypeStruct
    return small_call(
        kernel,
        [
            shape((3 * rank, width), jnp.float32),
            shape((rank, width), jnp.float32),
            shape(kv_shape, jnp.float32),
        ],
        pieces,
    )


def per_device(
    queries,
    layer_key_rows,
    layer_value_rows,
    output_gradient,
    output_row_sums,
    shifted_head_flags,
    inputs,
    adapter_down_weight,
    query_up_weight,
    key_value_up_weight,
):
    seq_count = lax.axis_size("seq")
    seq_index = lax.axis_index("seq")
    tokens, width = queries.shape
    kv_width = layer_key_rows.shape[1]
    whole_len = tokens * seq_count
    rank = adapter_down_weight.shape[1]
    assert GROUP == 4 * tokens and SHIFT == 2 * tokens
    flattened_down = adapter_down_weight.reshape(3 * rank, width)
    place = jnp.stack([seq_index % 2, seq_index // 2 % 2]).astype(jnp.int32)

    down_part, own_pair = lax.optimization_barrier(
        (mm(flattened_down, inputs, NT), (layer_key_rows, layer_value_rows))
    )
    sib_pair = [exchanged(a, "seq", 1) for a in own_pair]
    pc_pair = [moved(a, "seq", 2) for a in own_pair]

    down_low = summed(down_part, "head").astype(jnp.bfloat16)
    down_tiled = jnp.tile(down_low[:rank].T, (1, HEAD_SIZE // rank))
    down_own = down_low[rank:]
    down_pc = moved(down_own, "seq", 2)

    own, previous = attention(
        place,
        shifted_head_flags,
        queries,
        output_gradient,
        output_row_sums,
        query_up_weight,
        down_tiled,
        own_pair,
        sib_pair,
    )
    own_grads, pc_pair, down_pc = lax.optimization_barrier((own(), pc_pair, down_pc))
    px_pair = [exchanged(a, "seq", 1) for a in pc_pair]
    down_others = exchanged(jnp.concatenate([down_own, down_pc]), "seq", 1)
    down_win = jnp.concatenate(
        [down_others[: 2 * rank], down_own, down_pc, down_others[2 * rank :]], axis=1
    )
    keep_own, keep_pc, send, ups, grad_q, grad_kv = previous(
        pc_pair, px_pair, own_grads, key_value_up_weight, down_win
    )

    mine, up_sib, up_pc, up_px = head_sum(ups, rank)
    received = exchanged(send, "seq", 1).astype(jnp.float32)
    back = (keep_pc + received[1]).astype(jnp.bfloat16)
    kv_total = keep_own + received[0]
    up_others = [
        exchanged(up_sib, "seq", 1),
        moved(up_pc, "seq", -2),
        lax.ppermute(up_px, "seq", [(i, (i - 2) % seq_count ^ 1) for i in range(seq_count)]),
    ]
    up_others, back = lax.optimization_barrier((up_others, back))
    back = moved(back, "seq", -2)

    up_low, pieces = weight_pieces(
        seq_count, mine, up_others, inputs, grad_q, grad_kv, adapter_scale / math.sqrt(whole_len)
    )
    grad_inputs = (
        adapter_scale
        * lax.dot_general(
            up_low, flattened_down, (((0,), (0,)), ((), ())), preferred_element_type=jnp.float32
        )
    ).astype(jnp.bfloat16)
    pieces, back, grad_inputs = lax.optimization_barrier((pieces, back, grad_inputs))
    pieces = lax.all_to_all(pieces, "seq", 0, 0, tiled=True)
    total = jnp.sum(pieces.astype(jnp.float32), axis=0).astype(jnp.bfloat16)
    pieces = lax.all_gather(total, "seq")
    key_value_gradient = (kv_total + back.astype(jnp.float32)).astype(jnp.bfloat16)
    down_gradient, grad_up_q, grad_up_kv = joined_pieces(pieces, rank, (2 * rank, kv_width))
    return (
        grad_inputs,
        key_value_gradient,
        down_gradient.reshape(3, rank, width),
        grad_up_q,
        grad_up_kv.reshape(2, rank, kv_width),
    )


def solution(mesh):
    placed = (
        P("seq", "head"),
        P("seq", "head"),
        P("seq", "head"),
        P("seq", "head"),
        P("head", "seq"),
        P("head"),
        P("seq", "head"),
        P(None, None, "head"),
        P(None, "head"),
        P(None, None, "head"),
    )
    return jax.shard_map(
        per_device,
        mesh=mesh,
        in_specs=placed,
        out_specs=(
            P("seq", "head"),
            P(None, "seq", "head"),
            P(None, None, "head"),
            P(None, "head"),
            P(None, None, "head"),
        ),
        check_vma=False,
    )
```

```python
import functools
import math

import jax
import jax.numpy as jnp
from jax import lax
from jax.experimental import pallas as pl
from jax.experimental.pallas import tpu as pltpu
from jax.sharding import PartitionSpec as P

HEAD_SIZE = 128
GROUP = 1024
SHIFT = 512
CHUNK = 32
VMEM_LIMIT = 32 * 1024 * 1024

adapter_scale = 2.0
masked_score = -1e30
score_scale = HEAD_SIZE ** (-0.5)
exp2_scale = score_scale * math.log2(math.e)

NT = (((1,), (1,)), ((), ()))
NN = (((1,), (0,)), ((), ()))


def mm(left, right, dims=NN):
    return lax.dot_general(left, right, dims, preferred_element_type=jnp.float32)


def scores_and_softmax(head, low, diag, keys, values, q_ref, do_ref, term_ref, slot):
    tokens = q_ref.shape[0]
    s_ref, e_ref, ds_ref, inv_ref = slot
    group, column, key_column = head
    query = q_ref[:, column]
    grad = do_ref[:, column]
    term = term_ref[pl.ds(group[0], 1), :]
    top = None
    for block in range(low, len(keys)):
        rows = slice(block * tokens, (block + 1) * tokens)
        scores = mm(keys[block][:, key_column], query, NT)
        if block == diag:
            key_row = lax.broadcasted_iota(jnp.int32, (tokens, tokens), 0)
            query_row = lax.broadcasted_iota(jnp.int32, (tokens, tokens), 1)
            scores = jnp.where(key_row <= query_row, scores, masked_score)
        s_ref[rows, :] = scores
        here = jnp.max(scores.reshape(tokens // 8, 8, tokens), axis=0)
        top = here if top is None else jnp.maximum(top, here)
    top = jnp.max(top, axis=0, keepdims=True)
    total = jnp.zeros((8, tokens), jnp.float32)
    for block in range(low, len(keys)):
        grad_probs = mm(values[block][:, key_column], grad, NT)
        for at in range(0, tokens, CHUNK):
            rows = slice(block * tokens + at, block * tokens + at + CHUNK)
            weights = jnp.exp2((s_ref[rows, :] - top) * exp2_scale)
            total = total + jnp.sum(weights.reshape(CHUNK // 8, 8, tokens), axis=0)
            e_ref[rows, :] = weights.astype(jnp.bfloat16)
            ds_ref[rows, :] = (weights * (grad_probs[at : at + CHUNK, :] - term)).astype(jnp.bfloat16)
    inv_ref[...] = 1.0 / jnp.sum(total, axis=0, keepdims=True)


def add_gradients(head, valid, low, high, rank, q_ref, do_ref, down, up_q, wk, dk_acc, dv_acc, slot):
    tokens = q_ref.shape[0]
    _, e_ref, ds_ref, inv_ref = slot
    (_, group, inner), column, _ = head
    height = wk.shape[1]
    inverse = inv_ref[...] * valid
    inverse_rows = jnp.broadcast_to(inverse, (HEAD_SIZE, tokens)).T
    scaled = inverse_rows * score_scale
    lane = lax.broadcasted_iota(jnp.int32, (tokens, HEAD_SIZE), 1) // rank
    own_columns = jnp.where(lane == inner, down[...].astype(jnp.float32), 0.0)
    grad_n = (do_ref[:, column].astype(jnp.float32) * inverse_rows).astype(jnp.bfloat16)
    query_n = jnp.concatenate(
        [q_ref[:, column].astype(jnp.float32) * scaled, own_columns * scaled], axis=1
    ).astype(jnp.bfloat16)
    rows = pl.ds(pl.multiple_of(group * height + low, tokens), high - low)
    dv_acc[rows, :] += mm(e_ref[low:high, :], grad_n)
    dk_acc[rows, :] += mm(ds_ref[low:high, :], query_n)
    own = pl.ds(pl.multiple_of(group * HEAD_SIZE + inner * rank, rank), rank)
    up_q[...] += mm(wk[own, low:high], ds_ref[low:high, :]) * (inverse * score_scale)


def all_heads(
    with_previous, per_kv, rank, place, flags, keys, values, q_hbm, do_hbm, term, w_q, down, up_q, dk, dv, scratch
):
    listed, q, do, q_sem, do_sem, wk, *buffers = scratch
    loads = [pltpu.make_async_copy(q_hbm, q, q_sem), pltpu.make_async_copy(do_hbm, do, do_sem)]
    for load in loads:
        load.start()
    tokens, width = q.shape
    height = wk.shape[1]
    groups = width // (per_kv * HEAD_SIZE)
    for g in range(groups):
        stacked = jnp.concatenate(
            [w_q[:, h * HEAD_SIZE : (h + 1) * HEAD_SIZE] for h in range(g * per_kv, (g + 1) * per_kv)], axis=0
        )
        for block, key in enumerate(keys):
            wk[g * HEAD_SIZE : (g + 1) * HEAD_SIZE, block * tokens : (block + 1) * tokens] = mm(
                stacked, key[:, g * HEAD_SIZE : (g + 1) * HEAD_SIZE], NT
            ).astype(jnp.bfloat16)
    dk[...] = jnp.zeros_like(dk)
    dv[...] = jnp.zeros_like(dv)
    slots = (buffers[:4], buffers[4:])
    for _, e_ref, ds_ref, inv_ref in slots:
        e_ref[...] = jnp.zeros_like(e_ref)
        ds_ref[...] = jnp.zeros_like(ds_ref)
        inv_ref[...] = jnp.zeros_like(inv_ref)
    for load in loads:
        load.wait()
    core = place[0]
    half = place[1]
    count = jnp.int32(0)
    for h in range(groups * per_kv):
        listed[count] = jnp.int32(h)
        needs = flags[h] != half
        count = count + jnp.where(needs == with_previous, 1, 0).astype(jnp.int32)

    def head_at(i):
        h = listed[jnp.clip(i, 0, count - 1)]
        group = h // per_kv
        return (
            (h, group, h - group * per_kv),
            pl.ds(pl.multiple_of(h * HEAD_SIZE, HEAD_SIZE), HEAD_SIZE),
            pl.ds(pl.multiple_of(group * HEAD_SIZE, HEAD_SIZE), HEAD_SIZE),
        )

    for which in range(2):
        low = 1 - which

        def softmax(i, slot):
            scores_and_softmax(head_at(i), low, 1, keys, values, q, do, term, slot)

        def gradients(i, slot):
            valid = jnp.where((i >= 0) & (i < count), 1.0, 0.0).astype(jnp.float32)
            add_gradients(
                head_at(i), valid, low * tokens, height, rank, q, do, down, up_q, wk, dk, dv, slot
            )

        @pl.when((core == which) & (count > 0))
        def _():
            def two(t, carry):
                softmax(2 * t, slots[0])
                gradients(2 * t - 1, slots[1])
                softmax(2 * t + 1, slots[1])
                gradients(2 * t, slots[0])
                return carry

            lax.fori_loop(0, (count + 1) // 2, two, 0)

            @pl.when(count % 2 == 0)
            def _():
                gradients(count - 1, slots[1])


def own_kernel(
    per_kv, rank, place, flags, q, do, term, w_q, down, k_own, v_own, k_sib, v_sib, up_q, dk, dv, *scratch
):
    up_q[...] = jnp.zeros_like(up_q)
    all_heads(
        False, per_kv, rank, place, flags, (k_sib, k_own), (v_sib, v_own), q, do, term, w_q, down, up_q, dk, dv, scratch
    )


def previous_kernel(
    per_kv, rank, place, flags, q, do, term, w_q, down, k_own, v_own, k_sib, v_sib, k_pc, v_pc, k_px, v_px,
    up_q_own, dk_own, dv_own, w_kv, down_win,
    keep_own, keep_pc, send, ups, grad_q, grad_kv,
    dk, dv, up_q, *scratch,
):
    tokens = q.shape[0]
    up_q[...] = up_q_own[...]
    keys = (k_sib, k_own, k_pc, k_px)
    values = (v_sib, v_own, v_pc, v_px)
    all_heads(True, per_kv, rank, place, flags, keys, values, q, do, term, w_q, down, up_q, dk, dv, scratch)
    up_kv = [jnp.zeros((rank, 4 * tokens), jnp.float32) for _ in range(2)]
    for g in range(k_own.shape[1] // HEAD_SIZE):
        columns = slice(g * HEAD_SIZE, (g + 1) * HEAD_SIZE)
        low_row, own_row = g * 4 * tokens, g * 2 * tokens
        by_head = None
        for block in range(4):
            tail = dk[low_row + block * tokens : low_row + (block + 1) * tokens, HEAD_SIZE:]
            if block < 2:
                tail = tail + dk_own[own_row + block * tokens : own_row + (block + 1) * tokens, HEAD_SIZE:]
            part = mm(tail.T.astype(jnp.bfloat16), keys[block][:, columns])
            by_head = part if by_head is None else by_head + part
        for h in range(per_kv):
            at = (g * per_kv + h) * HEAD_SIZE
            grad_q[:, at : at + HEAD_SIZE] = by_head[h * rank : (h + 1) * rank, :]
        for c, acc, start in ((0, dk, dk_own), (1, dv, dv_own)):
            total = acc[low_row : low_row + 4 * tokens, :HEAD_SIZE]
            near = total[: 2 * tokens] + start[own_row : own_row + 2 * tokens, :HEAD_SIZE]
            low = jnp.concatenate([near, total[2 * tokens :]]).astype(jnp.bfloat16)
            keep_own[c, :, columns] = near[tokens:]
            keep_pc[c, :, columns] = total[2 * tokens : 3 * tokens]
            send[0, c, :, columns] = low[:tokens]
            send[1, c, :, columns] = low[3 * tokens :]
            up_kv[c] = up_kv[c] + mm(w_kv[c, :, columns], low, NT)
            own = slice(c * rank, (c + 1) * rank)
            grad_kv[own, columns] = mm(down_win[own, :], low)
    parts = [up_q[...]]
    for block in range(4):
        parts += [up_kv[c][:, block * tokens : (block + 1) * tokens] for c in range(2)]
    ups[...] = jnp.concatenate(parts).astype(jnp.bfloat16)


def attention(place, flags, queries, grads, terms, w_q, down, own_pair, sib_pair):
    tokens, width = queries.shape
    kv_width = own_pair[0].shape[1]
    kv_local = kv_width // HEAD_SIZE
    per_kv = width // kv_width
    rank = w_q.shape[0]
    assert per_kv * rank == HEAD_SIZE
    f32, bf16 = jnp.float32, jnp.bfloat16
    shape = jax.ShapeDtypeStruct
    pairs = kv_local * per_kv * tokens * tokens
    smem = pl.BlockSpec(memory_space=pltpu.SMEM)
    vmem = pl.BlockSpec(memory_space=pltpu.VMEM)
    hbm = pl.BlockSpec(memory_space=pltpu.HBM)

    def scratch(blocks):
        rows = blocks * tokens
        slot = [
            pltpu.VMEM((rows, tokens), f32),
            pltpu.VMEM((rows, tokens), bf16),
            pltpu.VMEM((rows, tokens), bf16),
            pltpu.VMEM((1, tokens), f32),
        ]
        return [
            pltpu.SMEM((kv_local * per_kv + 1,), jnp.int32),
            pltpu.VMEM((tokens, width), bf16),
            pltpu.VMEM((tokens, width), bf16),
            pltpu.SemaphoreType.DMA,
            pltpu.SemaphoreType.DMA,
            pltpu.VMEM((kv_local * HEAD_SIZE, rows), bf16),
        ] + slot * 2

    def call(kernel, out_shape, scratch_shapes, work, name, *args):
        return pl.pallas_call(
            functools.partial(kernel, per_kv, rank),
            in_specs=[smem, smem, hbm, hbm] + [vmem] * (len(args) - 4),
            out_specs=[vmem] * len(out_shape),
            out_shape=out_shape,
            scratch_shapes=scratch_shapes,
            compiler_params=pltpu.CompilerParams(vmem_limit_bytes=VMEM_LIMIT),
            cost_estimate=pl.CostEstimate(
                flops=work * pairs * HEAD_SIZE, bytes_accessed=6 * tokens * width, transcendentals=pairs
            ),
            name=name,
        )(*args)

    queries, grads = (pltpu.with_memory_space_constraint(a, pltpu.HBM) for a in (queries, grads))
    common = (place, flags, queries, grads, terms, w_q, down, *own_pair, *sib_pair)

    def own():
        return call(
            own_kernel,
            [
                shape((rank, tokens), f32),
                shape((2 * tokens * kv_local, 2 * HEAD_SIZE), f32),
                shape((2 * tokens * kv_local, HEAD_SIZE), f32),
            ],
            scratch(2),
            40,
            "own_chip_heads",
            *common,
        )

    def previous(pc_pair, px_pair, own_grads, w_kv, down_win):
        return call(
            previous_kernel,
            [
                shape((2, tokens, kv_width), f32),
                shape((2, tokens, kv_width), f32),
                shape((2, 2, tokens, kv_width), bf16),
                shape((9 * rank, tokens), bf16),
                shape((rank, width), f32),
                shape((2 * rank, kv_width), f32),
            ],
            [
                pltpu.VMEM((4 * tokens * kv_local, 2 * HEAD_SIZE), f32),
                pltpu.VMEM((4 * tokens * kv_local, HEAD_SIZE), f32),
                pltpu.VMEM((rank, tokens), f32),
            ]
            + scratch(4),
            80,
            "previous_chip_heads",
            *common,
            *pc_pair,
            *px_pair,
            *own_grads,
            w_kv,
            down_win,
        )

    return own, previous


def exchanged(value, axis, bit):
    return lax.ppermute(value, axis, [(i, i ^ bit) for i in range(lax.axis_size(axis))])


def moved(value, axis, by):
    count = lax.axis_size(axis)
    return lax.ppermute(value, axis, [(i, (i + by) % count) for i in range(count)])


def summed(value, axis):
    bit = 1
    while bit < lax.axis_size(axis):
        value = value + exchanged(value, axis, bit)
        bit *= 2
    return value


def small_call(kernel, out_shape, *args, scratch=()):
    vmem = pl.BlockSpec(memory_space=pltpu.VMEM)
    return pl.pallas_call(
        kernel,
        in_specs=[pl.BlockSpec(memory_space=pltpu.SMEM)] + [vmem] * (len(args) - 1),
        out_specs=[vmem] * len(out_shape),
        out_shape=out_shape,
        scratch_shapes=list(scratch),
        compiler_params=pltpu.CompilerParams(vmem_limit_bytes=VMEM_LIMIT),
    )(*args)


def lanes(index, wide):
    return pl.ds(pl.multiple_of(index * wide, HEAD_SIZE), wide)


def head_sum(place, ups, rank):
    count = lax.axis_size("head")
    bit = 1
    while 2 * bit < count:
        other = exchanged(ups, "head", bit)
        ups = (ups.astype(jnp.float32) + other.astype(jnp.float32)).astype(jnp.bfloat16)
        bit *= 2
    other = exchanged(ups, "head", bit)
    tokens = ups.shape[1]

    def kernel(place, here, there, mine, *others):
        total = here[...].astype(jnp.float32) + there[...].astype(jnp.float32)
        mine[...] = jnp.concatenate([total[:rank], total[3 * rank : 5 * rank]])
        for out, at in zip(others, (rank, 5 * rank, 7 * rank)):
            out[...] = total[at : at + 2 * rank].astype(jnp.bfloat16)

    shape = jax.ShapeDtypeStruct
    return small_call(
        kernel,
        [shape((3 * rank, tokens), jnp.float32)] + [shape((2 * rank, tokens), jnp.bfloat16)] * 3,
        place,
        ups,
        other,
    )


def weight_halves(place, mine, others, inputs, grad_q, grad_kv, scale):
    rank, width = grad_q.shape
    wide = width // 2
    rows = 4 * rank + grad_kv.shape[0]

    def kernel(place, mine, one, two, three, tokens_in, q, kv, up_low, *out):
        tail = mine[rank:, :] + sum(o[...].astype(jnp.float32) for o in (one, two, three))
        up = jnp.concatenate([mine[:rank, :], tail]).astype(jnp.bfloat16)
        up_low[...] = up
        for d in range(2):
            at = lanes(place[0] ^ d, wide)
            piece = jnp.concatenate([mm(up, tokens_in[:, at]), q[:, at], kv[:, at]]) * scale
            out[d][...] = piece.astype(jnp.bfloat16)

    shape = jax.ShapeDtypeStruct
    return small_call(
        kernel,
        [shape(mine.shape, jnp.bfloat16)] + [shape((rows, wide), jnp.bfloat16)] * 2,
        place,
        mine,
        *others,
        inputs,
        grad_q,
        grad_kv,
    )


def exchanged_pieces(pieces, unit):
    return [pieces[0]] + [exchanged(p, "seq", d * unit) for d, p in enumerate(pieces) if d]


def summed_and_cut(place, which, pieces, radix):
    rows, whole = pieces[0].shape
    wide = whole // radix
    if wide % HEAD_SIZE:
        total = sum(p.astype(jnp.float32) for p in pieces).astype(jnp.bfloat16)
        return [
            lax.dynamic_slice_in_dim(total, (place[which] ^ d) * wide, wide, 1) for d in range(radix)
        ]
    given = len(pieces)

    def kernel(place, *refs):
        total = refs[-1]
        total[...] = sum(p[...].astype(jnp.float32) for p in refs[:given])
        for d in range(radix):
            refs[given + d][...] = total[:, lanes(place[which] ^ d, wide)].astype(jnp.bfloat16)

    return small_call(
        kernel,
        [jax.ShapeDtypeStruct((rows, wide), jnp.bfloat16)] * radix,
        place,
        *pieces,
        scratch=[pltpu.VMEM((rows, whole), jnp.float32)],
    )


def joined(place, which, pieces):
    rows, wide = pieces[0].shape
    radix = len(pieces)
    if wide % HEAD_SIZE:
        whole = jnp.zeros((rows, radix * wide), jnp.bfloat16)
        for d in range(radix):
            whole = lax.dynamic_update_slice_in_dim(whole, pieces[d], (place[which] ^ d) * wide, 1)
        return whole

    def kernel(place, *refs):
        for d in range(radix):
            refs[radix][:, lanes(place[which] ^ d, wide)] = refs[d][...]

    return small_call(
        kernel, [jax.ShapeDtypeStruct((rows, radix * wide), jnp.bfloat16)], place, *pieces
    )[0]


def joined_outputs(place, pieces, rank, kv_shape):
    rows, wide = pieces[0].shape
    extra = rows - 4 * rank
    each = wide // kv_shape[1]
    per_row = kv_shape[0] // extra

    def kernel(place, *refs):
        down, up_q, up_kv = refs[4:]
        for d, turned in enumerate((0, 2, 1, 3)):
            at = place[2] ^ turned
            piece = refs[d][...].astype(jnp.float32)
            down[:, lanes(at, wide)] = piece[: 3 * rank]
            up_q[:, lanes(at, wide)] = piece[3 * rank : 4 * rank]
            for i in range(extra):
                for b in range(each):
                    up_kv[pl.ds(per_row * i + each * at + b, 1), :] = piece[
                        4 * rank + i : 4 * rank + i + 1, b * kv_shape[1] : (b + 1) * kv_shape[1]
                    ]

    shape = jax.ShapeDtypeStruct
    return small_call(
        kernel,
        [
            shape((3 * rank, 4 * wide), jnp.float32),
            shape((rank, 4 * wide), jnp.float32),
            shape(kv_shape, jnp.float32),
        ],
        place,
        *pieces,
    )


def per_device(
    queries,
    layer_key_rows,
    layer_value_rows,
    output_gradient,
    output_row_sums,
    shifted_head_flags,
    inputs,
    adapter_down_weight,
    query_up_weight,
    key_value_up_weight,
):
    seq_count = lax.axis_size("seq")
    seq_index = lax.axis_index("seq")
    tokens, width = queries.shape
    kv_width = layer_key_rows.shape[1]
    whole_len = tokens * seq_count
    rank = adapter_down_weight.shape[1]
    assert GROUP == 4 * tokens and SHIFT == 2 * tokens
    levels = (seq_count.bit_length() - 1) // 2
    assert 4**levels == seq_count
    flattened_down = adapter_down_weight.reshape(3 * rank, width)
    core, half = seq_index % 2, seq_index // 2 % 2
    place = jnp.stack(
        [core, half, 2 * core + half] + [seq_index // 4**i % 4 for i in range(1, levels)]
    ).astype(jnp.int32)
    across = [(i, (i - 2) % seq_count ^ 1) for i in range(seq_count)]

    own_pair = (layer_key_rows, layer_value_rows)
    pc_pair = [moved(a, "seq", 2) for a in own_pair]
    sib_pair = [exchanged(a, "seq", 1) for a in own_pair]

    down_low = summed(mm(flattened_down, inputs, NT), "head").astype(jnp.bfloat16)
    down_tiled = jnp.tile(down_low[:rank].T, (1, HEAD_SIZE // rank))

    own, previous = attention(
        place,
        shifted_head_flags,
        queries,
        output_gradient,
        output_row_sums,
        query_up_weight,
        down_tiled,
        own_pair,
        sib_pair,
    )
    own_grads, pc_pair, down_own = lax.optimization_barrier((own(), pc_pair, down_low[rank:]))
    px_pair = [exchanged(a, "seq", 1) for a in pc_pair]
    down_win = jnp.concatenate(
        [
            exchanged(down_own, "seq", 1),
            down_own,
            moved(down_own, "seq", 2),
            lax.ppermute(down_own, "seq", [(to, start) for start, to in across]),
        ],
        axis=1,
    )
    keep_own, keep_pc, send, ups, grad_q, grad_kv = previous(
        pc_pair, px_pair, own_grads, key_value_up_weight, down_win
    )

    mine, *up_others = head_sum(place, ups, rank)
    received = exchanged(send, "seq", 1)
    back = (keep_pc + received[1].astype(jnp.float32)).astype(jnp.bfloat16)
    up_others, back = lax.optimization_barrier((up_others, back))
    up_others = [
        exchanged(up_others[0], "seq", 1),
        moved(up_others[1], "seq", -2),
        lax.ppermute(up_others[2], "seq", across),
    ]
    back = moved(back, "seq", -2)

    up_low, *pieces = weight_halves(
        place, mine, up_others, inputs, grad_q, grad_kv.reshape(-1, width), adapter_scale / math.sqrt(whole_len)
    )
    pieces = summed_and_cut(place, 1, exchanged_pieces(pieces, 1), 2)
    pieces, back = lax.optimization_barrier((pieces, back))
    pieces = exchanged_pieces(pieces, 2)
    for level in range(1, levels):
        pieces = exchanged_pieces(summed_and_cut(place, 2 + level, pieces, 4), 4**level)
    total = sum(p.astype(jnp.float32) for p in pieces).astype(jnp.bfloat16)
    key_value_gradient = (
        keep_own + received[0].astype(jnp.float32) + back.astype(jnp.float32)
    ).astype(jnp.bfloat16)
    grad_inputs = (
        adapter_scale
        * lax.dot_general(
            up_low, flattened_down, (((0,), (0,)), ((), ())), preferred_element_type=jnp.float32
        )
    ).astype(jnp.bfloat16)
    for level in range(levels - 1, 0, -1):
        total = joined(place, 2 + level, exchanged_pieces([total] * 4, 4**level))
    down_gradient, grad_up_q, grad_up_kv = joined_outputs(
        place, exchanged_pieces([total] * 4, 1), rank, (2 * rank, kv_width)
    )
    return (
        grad_inputs,
        key_value_gradient,
        down_gradient.reshape(3, rank, width),
        grad_up_q,
        grad_up_kv.reshape(2, rank, kv_width),
    )


def solution(mesh):
    placed = (
        P("seq", "head"),
        P("seq", "head"),
        P("seq", "head"),
        P("seq", "head"),
        P("head", "seq"),
        P("head"),
        P("seq", "head"),
        P(None, None, "head"),
        P(None, "head"),
        P(None, None, "head"),
    )
    return jax.shard_map(
        per_device,
        mesh=mesh,
        in_specs=placed,
        out_specs=(
            P("seq", "head"),
            P(None, "seq", "head"),
            P(None, None, "head"),
            P(None, "head"),
            P(None, None, "head"),
        ),
        check_vma=False,
    )
```

```python
import functools
import math

import jax
import jax.numpy as jnp
from jax import lax
from jax.experimental import pallas as pl
from jax.experimental.pallas import tpu as pltpu
from jax.sharding import PartitionSpec as P

HEAD_SIZE = 128
GROUP = 1024
SHIFT = 512
CHUNK = 32
LOADS = 8
SMALL_VMEM = 8 * 1024 * 1024
VMEM_LIMIT = 32 * 1024 * 1024

adapter_scale = 2.0
masked_score = -1e30
score_scale = HEAD_SIZE ** (-0.5)
exp2_scale = score_scale * math.log2(math.e)

NT = (((1,), (1,)), ((), ()))
NN = (((1,), (0,)), ((), ()))


def mm(left, right, dims=NN):
    return lax.dot_general(left, right, dims, preferred_element_type=jnp.float32)


def scores_and_softmax(head, low, diag, keys, values, q_ref, do_ref, term_ref, slot):
    tokens = q_ref.shape[0]
    s_ref, e_ref, ds_ref, inv_ref = slot
    group, column, key_column = head
    query = q_ref[:, column]
    grad = do_ref[:, column]
    term = term_ref[pl.ds(group[0], 1), :]
    top = None
    for block in range(low, len(keys)):
        rows = slice(block * tokens, (block + 1) * tokens)
        scores = mm(keys[block][:, key_column], query, NT)
        if block == diag:
            key_row = lax.broadcasted_iota(jnp.int32, (tokens, tokens), 0)
            query_row = lax.broadcasted_iota(jnp.int32, (tokens, tokens), 1)
            scores = jnp.where(key_row <= query_row, scores, masked_score)
        s_ref[rows, :] = scores
        here = jnp.max(scores.reshape(tokens // 8, 8, tokens), axis=0)
        top = here if top is None else jnp.maximum(top, here)
    top = jnp.max(top, axis=0, keepdims=True)
    total = jnp.zeros((8, tokens), jnp.float32)
    for block in range(low, len(keys)):
        grad_probs = mm(values[block][:, key_column], grad, NT)
        for at in range(0, tokens, CHUNK):
            rows = slice(block * tokens + at, block * tokens + at + CHUNK)
            weights = jnp.exp2((s_ref[rows, :] - top) * exp2_scale)
            total = total + jnp.sum(weights.reshape(CHUNK // 8, 8, tokens), axis=0)
            e_ref[rows, :] = weights.astype(jnp.bfloat16)
            ds_ref[rows, :] = (weights * (grad_probs[at : at + CHUNK, :] - term)).astype(jnp.bfloat16)
    inv_ref[...] = 1.0 / jnp.sum(total, axis=0, keepdims=True)


def add_gradients(head, valid, low, high, rank, q_ref, do_ref, down, up_q, wk, dk_acc, dv_acc, slot):
    tokens = q_ref.shape[0]
    _, e_ref, ds_ref, inv_ref = slot
    (_, group, inner), column, _ = head
    height = wk.shape[1]
    inverse = inv_ref[...] * valid
    inverse_rows = jnp.broadcast_to(inverse, (HEAD_SIZE, tokens)).T
    scaled = inverse_rows * score_scale
    lane = lax.broadcasted_iota(jnp.int32, (tokens, HEAD_SIZE), 1) // rank
    own_columns = jnp.where(lane == inner, down[...].astype(jnp.float32), 0.0)
    grad_n = (do_ref[:, column].astype(jnp.float32) * inverse_rows).astype(jnp.bfloat16)
    query_n = jnp.concatenate(
        [q_ref[:, column].astype(jnp.float32) * scaled, own_columns * scaled], axis=1
    ).astype(jnp.bfloat16)
    rows = pl.ds(pl.multiple_of(group * height + low, tokens), high - low)
    dv_acc[rows, :] += mm(e_ref[low:high, :], grad_n)
    dk_acc[rows, :] += mm(ds_ref[low:high, :], query_n)
    own = pl.ds(pl.multiple_of(group * HEAD_SIZE + inner * rank, rank), rank)
    up_q[...] += mm(wk[own, low:high], ds_ref[low:high, :]) * (inverse * score_scale)


def all_heads(
    with_previous, per_kv, rank, flags, keys, values, q_hbm, do_hbm, term, w_q, down, up_q, dk, dv, scratch
):
    listed, q, do, q_sem, do_sem, wk, *buffers = scratch
    tokens, width = q.shape
    part = tokens // LOADS
    loads = []
    for i in range(LOADS):
        rows = pl.ds(i * part, part)
        loads.append(pltpu.make_async_copy(q_hbm.at[rows], q.at[rows], q_sem.at[i]))
        loads.append(pltpu.make_async_copy(do_hbm.at[rows], do.at[rows], do_sem.at[i]))
    for load in loads:
        load.start()
    height = wk.shape[1]
    groups = width // (per_kv * HEAD_SIZE)
    for g in range(groups):
        stacked = jnp.concatenate(
            [w_q[:, h * HEAD_SIZE : (h + 1) * HEAD_SIZE] for h in range(g * per_kv, (g + 1) * per_kv)], axis=0
        )
        for block, key in enumerate(keys):
            wk[g * HEAD_SIZE : (g + 1) * HEAD_SIZE, block * tokens : (block + 1) * tokens] = mm(
                stacked, key[:, g * HEAD_SIZE : (g + 1) * HEAD_SIZE], NT
            ).astype(jnp.bfloat16)
    dk[...] = jnp.zeros_like(dk)
    dv[...] = jnp.zeros_like(dv)
    slots = (buffers[:4], buffers[4:])
    for _, e_ref, ds_ref, inv_ref in slots:
        e_ref[...] = jnp.zeros_like(e_ref)
        ds_ref[...] = jnp.zeros_like(ds_ref)
        inv_ref[...] = jnp.zeros_like(inv_ref)
    for load in loads:
        load.wait()
    index = lax.axis_index("seq")
    core = index % 2
    half = index // 2 % 2
    count = jnp.int32(0)
    for h in range(groups * per_kv):
        listed[count] = jnp.int32(h)
        needs = flags[h] != half
        count = count + jnp.where(needs == with_previous, 1, 0).astype(jnp.int32)

    def head_at(i):
        h = listed[jnp.clip(i, 0, count - 1)]
        group = h // per_kv
        return (
            (h, group, h - group * per_kv),
            pl.ds(pl.multiple_of(h * HEAD_SIZE, HEAD_SIZE), HEAD_SIZE),
            pl.ds(pl.multiple_of(group * HEAD_SIZE, HEAD_SIZE), HEAD_SIZE),
        )

    for which in range(2):
        low = 1 - which

        def softmax(i, slot):
            scores_and_softmax(head_at(i), low, 1, keys, values, q, do, term, slot)

        def gradients(i, slot):
            valid = jnp.where((i >= 0) & (i < count), 1.0, 0.0).astype(jnp.float32)
            add_gradients(
                head_at(i), valid, low * tokens, height, rank, q, do, down, up_q, wk, dk, dv, slot
            )

        @pl.when((core == which) & (count > 0))
        def _():
            def two(t, carry):
                softmax(2 * t, slots[0])
                gradients(2 * t - 1, slots[1])
                softmax(2 * t + 1, slots[1])
                gradients(2 * t, slots[0])
                return carry

            lax.fori_loop(0, (count + 1) // 2, two, 0)

            @pl.when(count % 2 == 0)
            def _():
                gradients(count - 1, slots[1])


def own_kernel(
    per_kv, rank, flags, q, do, term, w_q, down, k_own, v_own, k_sib, v_sib, up_q, dk, dv, *scratch
):
    up_q[...] = jnp.zeros_like(up_q)
    all_heads(
        False, per_kv, rank, flags, (k_sib, k_own), (v_sib, v_own), q, do, term, w_q, down, up_q, dk, dv, scratch
    )


def previous_kernel(
    per_kv, rank, flags, q, do, term, w_q, down, k_own, v_own, k_sib, v_sib, k_pc, v_pc, k_px, v_px,
    up_q_own, dk_own, dv_own, w_kv, down_win,
    keep_own, keep_pc, send, up_q, up_keep, up_send, grad_q, grad_kv,
    dk, dv, *scratch,
):
    tokens = q.shape[0]
    up_q[...] = up_q_own[...]
    keys = (k_sib, k_own, k_pc, k_px)
    values = (v_sib, v_own, v_pc, v_px)
    all_heads(True, per_kv, rank, flags, keys, values, q, do, term, w_q, down, up_q, dk, dv, scratch)
    up_kv = [jnp.zeros((rank, 4 * tokens), jnp.float32) for _ in range(2)]
    for g in range(k_own.shape[1] // HEAD_SIZE):
        columns = slice(g * HEAD_SIZE, (g + 1) * HEAD_SIZE)
        low_row, own_row = g * 4 * tokens, g * 2 * tokens
        by_head = None
        for block in range(4):
            tail = dk[low_row + block * tokens : low_row + (block + 1) * tokens, HEAD_SIZE:]
            if block < 2:
                tail = tail + dk_own[own_row + block * tokens : own_row + (block + 1) * tokens, HEAD_SIZE:]
            part = mm(tail.T.astype(jnp.bfloat16), keys[block][:, columns])
            by_head = part if by_head is None else by_head + part
        for h in range(per_kv):
            at = (g * per_kv + h) * HEAD_SIZE
            grad_q[:, at : at + HEAD_SIZE] = by_head[h * rank : (h + 1) * rank, :]
        for c, acc, start in ((0, dk, dk_own), (1, dv, dv_own)):
            total = acc[low_row : low_row + 4 * tokens, :HEAD_SIZE]
            near = total[: 2 * tokens] + start[own_row : own_row + 2 * tokens, :HEAD_SIZE]
            low = jnp.concatenate([near, total[2 * tokens :]]).astype(jnp.bfloat16)
            keep_own[c, :, columns] = near[tokens:]
            keep_pc[c, :, columns] = total[2 * tokens : 3 * tokens]
            send[0, c, :, columns] = low[:tokens]
            send[1, c, :, columns] = low[3 * tokens :]
            up_kv[c] = up_kv[c] + mm(w_kv[c, :, columns], low, NT)
            own = slice(c * rank, (c + 1) * rank)
            grad_kv[own, columns] = mm(down_win[own, :], low)
    sib, near, pc, px = (
        jnp.concatenate([up_kv[c][:, block * tokens : (block + 1) * tokens] for c in range(2)])
        for block in range(4)
    )
    up_keep[...] = jnp.concatenate([near, pc])
    up_send[...] = jnp.concatenate([sib, px]).astype(jnp.bfloat16)


def attention(flags, queries, grads, terms, w_q, down, own_pair, sib_pair):
    tokens, width = queries.shape
    kv_width = own_pair[0].shape[1]
    kv_local = kv_width // HEAD_SIZE
    per_kv = width // kv_width
    rank = w_q.shape[0]
    assert per_kv * rank == HEAD_SIZE
    f32, bf16 = jnp.float32, jnp.bfloat16
    shape = jax.ShapeDtypeStruct
    pairs = kv_local * per_kv * tokens * tokens
    smem = pl.BlockSpec(memory_space=pltpu.SMEM)
    vmem = pl.BlockSpec(memory_space=pltpu.VMEM)
    hbm = pl.BlockSpec(memory_space=pltpu.HBM)

    def scratch(blocks):
        rows = blocks * tokens
        slot = [
            pltpu.VMEM((rows, tokens), f32),
            pltpu.VMEM((rows, tokens), bf16),
            pltpu.VMEM((rows, tokens), bf16),
            pltpu.VMEM((1, tokens), f32),
        ]
        return [
            pltpu.SMEM((kv_local * per_kv + 1,), jnp.int32),
            pltpu.VMEM((tokens, width), bf16),
            pltpu.VMEM((tokens, width), bf16),
            pltpu.SemaphoreType.DMA((LOADS,)),
            pltpu.SemaphoreType.DMA((LOADS,)),
            pltpu.VMEM((kv_local * HEAD_SIZE, rows), bf16),
        ] + slot * 2

    def call(kernel, out_shape, scratch_shapes, work, name, *args):
        return pl.pallas_call(
            functools.partial(kernel, per_kv, rank),
            in_specs=[smem, hbm, hbm] + [vmem] * (len(args) - 3),
            out_specs=[vmem] * len(out_shape),
            out_shape=out_shape,
            scratch_shapes=scratch_shapes,
            compiler_params=pltpu.CompilerParams(vmem_limit_bytes=VMEM_LIMIT),
            cost_estimate=pl.CostEstimate(
                flops=work * pairs * HEAD_SIZE, bytes_accessed=6 * tokens * width, transcendentals=pairs
            ),
            name=name,
        )(*args)

    queries, grads = (pltpu.with_memory_space_constraint(a, pltpu.HBM) for a in (queries, grads))
    common = (flags, queries, grads, terms, w_q, down, *own_pair, *sib_pair)

    def own():
        return call(
            own_kernel,
            [
                shape((rank, tokens), f32),
                shape((2 * tokens * kv_local, 2 * HEAD_SIZE), f32),
                shape((2 * tokens * kv_local, HEAD_SIZE), f32),
            ],
            scratch(2),
            40,
            "own_chip_heads",
            *common,
        )

    def previous(pc_pair, px_pair, own_grads, w_kv, down_win):
        return call(
            previous_kernel,
            [
                shape((2, tokens, kv_width), f32),
                shape((2, tokens, kv_width), f32),
                shape((2, 2, tokens, kv_width), bf16),
                shape((rank, tokens), f32),
                shape((4 * rank, tokens), f32),
                shape((4 * rank, tokens), bf16),
                shape((rank, width), f32),
                shape((2 * rank, kv_width), f32),
            ],
            [
                pltpu.VMEM((4 * tokens * kv_local, 2 * HEAD_SIZE), f32),
                pltpu.VMEM((4 * tokens * kv_local, HEAD_SIZE), f32),
            ]
            + scratch(4),
            80,
            "previous_chip_heads",
            *common,
            *pc_pair,
            *px_pair,
            *own_grads,
            w_kv,
            down_win,
        )

    return own, previous


def exchanged(value, axis, bit):
    return lax.ppermute(value, axis, [(i, i ^ bit) for i in range(lax.axis_size(axis))])


def moved(value, axis, by):
    count = lax.axis_size(axis)
    return lax.ppermute(value, axis, [(i, (i + by) % count) for i in range(count)])


def summed(value, axis):
    bit = 1
    while bit < lax.axis_size(axis):
        value = value + exchanged(value, axis, bit)
        bit *= 2
    return value


def small_call(kernel, out_shape, *args, scratch=(), limit=1):
    vmem = pl.BlockSpec(memory_space=pltpu.VMEM)
    return pl.pallas_call(
        kernel,
        in_specs=[vmem] * len(args),
        out_specs=[vmem] * len(out_shape),
        out_shape=out_shape,
        scratch_shapes=list(scratch),
        compiler_params=pltpu.CompilerParams(vmem_limit_bytes=limit * SMALL_VMEM),
    )(*args)


def place(unit, radix):
    return lax.axis_index("seq") // unit % radix


def lanes(index, wide):
    return pl.ds(pl.multiple_of(index * wide, HEAD_SIZE), wide)


def up_near(up_keep, received):
    rows, tokens = up_keep.shape

    def kernel(keep, other, own, previous):
        total = keep[...] + other[...].astype(jnp.float32)
        own[...] = total[: rows // 2]
        previous[...] = total[rows // 2 :].astype(jnp.bfloat16)

    shape = jax.ShapeDtypeStruct
    return small_call(
        kernel,
        [shape((rows // 2, tokens), jnp.float32), shape((rows // 2, tokens), jnp.bfloat16)],
        up_keep,
        received,
    )


def up_here(up_q, own, received):
    def kernel(up_q, own, other, out):
        out[...] = jnp.concatenate([up_q[...], own[...] + other[...].astype(jnp.float32)]).astype(jnp.bfloat16)

    rows = up_q.shape[0] + own.shape[0]
    return small_call(
        kernel, [jax.ShapeDtypeStruct((rows, own.shape[1]), jnp.bfloat16)], up_q, own, received
    )[0]


def weight_halves(here, there, inputs, grad_q, grad_kv, scale):
    rank, width = grad_q.shape
    wide = width // 2
    rows = 4 * rank + grad_kv.shape[0]

    def kernel(here, there, tokens_in, q, kv, up_low, *out):
        up = (here[...].astype(jnp.float32) + there[...].astype(jnp.float32)).astype(jnp.bfloat16)
        up_low[...] = up
        for d in range(2):
            at = lanes(place(1, 2) ^ d, wide)
            piece = jnp.concatenate([mm(up, tokens_in[:, at]), q[:, at], kv[:, at]]) * scale
            out[d][...] = piece.astype(jnp.bfloat16)

    shape = jax.ShapeDtypeStruct
    return small_call(
        kernel,
        [shape(here.shape, jnp.bfloat16)] + [shape((rows, wide), jnp.bfloat16)] * 2,
        here,
        there,
        inputs,
        grad_q,
        grad_kv,
        limit=2,
    )


def exchanged_pieces(pieces, unit):
    return [pieces[0]] + [exchanged(p, "seq", d * unit) for d, p in enumerate(pieces) if d]


def summed_and_cut(pieces, unit, radix):
    rows, whole = pieces[0].shape
    wide = whole // radix
    if wide % HEAD_SIZE:
        total = sum(p.astype(jnp.float32) for p in pieces).astype(jnp.bfloat16)
        return [
            lax.dynamic_slice_in_dim(total, (place(unit, radix) ^ d) * wide, wide, 1)
            for d in range(radix)
        ]
    given = len(pieces)

    def kernel(*refs):
        total = refs[-1]
        total[...] = sum(p[...].astype(jnp.float32) for p in refs[:given])
        for d in range(radix):
            refs[given + d][...] = total[:, lanes(place(unit, radix) ^ d, wide)].astype(jnp.bfloat16)

    return small_call(
        kernel,
        [jax.ShapeDtypeStruct((rows, wide), jnp.bfloat16)] * radix,
        *pieces,
        scratch=[pltpu.VMEM((rows, whole), jnp.float32)],
    )


def joined(pieces, unit):
    rows, wide = pieces[0].shape
    radix = len(pieces)
    if wide % HEAD_SIZE:
        whole = jnp.zeros((rows, radix * wide), jnp.bfloat16)
        for d in range(radix):
            whole = lax.dynamic_update_slice_in_dim(
                whole, pieces[d], (place(unit, radix) ^ d) * wide, 1
            )
        return whole

    def kernel(*refs):
        for d in range(radix):
            refs[radix][:, lanes(place(unit, radix) ^ d, wide)] = refs[d][...]

    return small_call(kernel, [jax.ShapeDtypeStruct((rows, radix * wide), jnp.bfloat16)], *pieces)[0]


def joined_outputs(pieces, rank, kv_shape):
    rows, wide = pieces[0].shape
    extra = rows - 4 * rank
    each = wide // kv_shape[1]
    per_row = kv_shape[0] // extra

    def kernel(one, two, down, up_q, up_kv):
        for d, half in enumerate((one, two)):
            at = place(1, 2) ^ d
            piece = half[...].astype(jnp.float32)
            down[:, lanes(at, wide)] = piece[: 3 * rank]
            up_q[:, lanes(at, wide)] = piece[3 * rank : 4 * rank]
            for i in range(extra):
                for b in range(each):
                    up_kv[pl.ds(per_row * i + each * at + b, 1), :] = piece[
                        4 * rank + i : 4 * rank + i + 1, b * kv_shape[1] : (b + 1) * kv_shape[1]
                    ]

    shape = jax.ShapeDtypeStruct
    return small_call(
        kernel,
        [
            shape((3 * rank, 2 * wide), jnp.float32),
            shape((rank, 2 * wide), jnp.float32),
            shape(kv_shape, jnp.float32),
        ],
        *pieces,
    )


def per_device(
    queries,
    layer_key_rows,
    layer_value_rows,
    output_gradient,
    output_row_sums,
    shifted_head_flags,
    inputs,
    adapter_down_weight,
    query_up_weight,
    key_value_up_weight,
):
    seq_count = lax.axis_size("seq")
    tokens, width = queries.shape
    kv_width = layer_key_rows.shape[1]
    whole_len = tokens * seq_count
    rank = adapter_down_weight.shape[1]
    assert GROUP == 4 * tokens and SHIFT == 2 * tokens
    levels = (seq_count.bit_length() - 1) // 2
    assert 4**levels == seq_count
    flattened_down = adapter_down_weight.reshape(3 * rank, width)
    own_pair = (layer_key_rows, layer_value_rows)
    pc_pair = [moved(a, "seq", 2) for a in own_pair]
    sib_pair = [exchanged(a, "seq", 1) for a in own_pair]

    down_low = summed(mm(flattened_down, inputs, NT), "head").astype(jnp.bfloat16)
    down_tiled = jnp.tile(down_low[:rank].T, (1, HEAD_SIZE // rank))
    down_own = down_low[rank:]
    down_pc = moved(down_own, "seq", 2)

    own, previous = attention(
        shifted_head_flags,
        queries,
        output_gradient,
        output_row_sums,
        query_up_weight,
        down_tiled,
        own_pair,
        sib_pair,
    )
    own_grads, pc_pair, down_pc = lax.optimization_barrier((own(), pc_pair, down_pc))
    px_pair = [exchanged(a, "seq", 1) for a in pc_pair]
    down_others = exchanged(jnp.concatenate([down_own, down_pc]), "seq", 1)
    down_win = jnp.concatenate(
        [down_others[: 2 * rank], down_own, down_pc, down_others[2 * rank :]], axis=1
    )
    keep_own, keep_pc, send, up_q, up_keep, up_send, grad_q, grad_kv = previous(
        pc_pair, px_pair, own_grads, key_value_up_weight, down_win
    )

    up_own, up_prev = up_near(up_keep, exchanged(up_send, "seq", 1))
    received = exchanged(send, "seq", 1)
    back = (keep_pc + received[1].astype(jnp.float32)).astype(jnp.bfloat16)
    up_prev, back = lax.optimization_barrier((moved(up_prev, "seq", -2), back))
    back = moved(back, "seq", -2)
    here = up_here(up_q, up_own, up_prev)
    bit = 1
    while 2 * bit < lax.axis_size("head"):
        there = exchanged(here, "head", bit)
        here = (here.astype(jnp.float32) + there.astype(jnp.float32)).astype(jnp.bfloat16)
        bit *= 2
    up_low, *pieces = weight_halves(
        here,
        exchanged(here, "head", bit),
        inputs,
        grad_q,
        grad_kv.reshape(-1, width),
        adapter_scale / math.sqrt(whole_len),
    )
    pieces = exchanged_pieces(summed_and_cut(exchanged_pieces(pieces, 1), 2, 2), 2)
    for level in range(1, levels):
        pieces = summed_and_cut(pieces, 4**level, 4)
        if level == 1:
            pieces, back = lax.optimization_barrier((pieces, back))
        pieces = exchanged_pieces(pieces, 4**level)
    total = sum(p.astype(jnp.float32) for p in pieces).astype(jnp.bfloat16)
    key_value_gradient = (
        keep_own + received[0].astype(jnp.float32) + back.astype(jnp.float32)
    ).astype(jnp.bfloat16)
    grad_inputs = (
        adapter_scale
        * lax.dot_general(
            up_low, flattened_down, (((0,), (0,)), ((), ())), preferred_element_type=jnp.float32
        )
    ).astype(jnp.bfloat16)
    for level in range(levels - 1, 0, -1):
        total = joined(exchanged_pieces([total] * 4, 4**level), 4**level)
    total = joined(exchanged_pieces([total] * 2, 2), 2)
    down_gradient, grad_up_q, grad_up_kv = joined_outputs(
        exchanged_pieces([total] * 2, 1), rank, (2 * rank, kv_width)
    )
    return (
        grad_inputs,
        key_value_gradient,
        down_gradient.reshape(3, rank, width),
        grad_up_q,
        grad_up_kv.reshape(2, rank, kv_width),
    )


def solution(mesh):
    placed = (
        P("seq", "head"),
        P("seq", "head"),
        P("seq", "head"),
        P("seq", "head"),
        P("head", "seq"),
        P("head"),
        P("seq", "head"),
        P(None, None, "head"),
        P(None, "head"),
        P(None, None, "head"),
    )
    return jax.shard_map(
        per_device,
        mesh=mesh,
        in_specs=placed,
        out_specs=(
            P("seq", "head"),
            P(None, "seq", "head"),
            P(None, None, "head"),
            P(None, "head"),
            P(None, None, "head"),
        ),
        check_vma=False,
    )
```

```python
import functools
import math

import jax
import jax.numpy as jnp
from jax import lax
from jax.experimental import pallas as pl
from jax.experimental.pallas import tpu as pltpu
from jax.sharding import PartitionSpec as P

HEAD_SIZE = 128
GROUP = 1024
SHIFT = 512
CHUNK = 32
SMALL_VMEM = 8 * 1024 * 1024
VMEM_LIMIT = 32 * 1024 * 1024

adapter_scale = 2.0
masked_score = -1e30
score_scale = HEAD_SIZE ** (-0.5)
exp2_scale = score_scale * math.log2(math.e)

NT = (((1,), (1,)), ((), ()))
NN = (((1,), (0,)), ((), ()))


def mm(left, right, dims=NN):
    return lax.dot_general(left, right, dims, preferred_element_type=jnp.float32)


def scores_and_softmax(head, low, diag, keys, values, q_ref, do_ref, term_ref, slot):
    tokens = q_ref.shape[0]
    s_ref, e_ref, ds_ref, inv_ref = slot
    group, column, key_column = head
    query = q_ref[:, column]
    grad = do_ref[:, column]
    term = term_ref[pl.ds(group[0], 1), :]
    top = None
    for block in range(low, len(keys)):
        rows = slice(block * tokens, (block + 1) * tokens)
        scores = mm(keys[block][:, key_column], query, NT)
        if block == diag:
            key_row = lax.broadcasted_iota(jnp.int32, (tokens, tokens), 0)
            query_row = lax.broadcasted_iota(jnp.int32, (tokens, tokens), 1)
            scores = jnp.where(key_row <= query_row, scores, masked_score)
        s_ref[rows, :] = scores
        here = jnp.max(scores.reshape(tokens // 8, 8, tokens), axis=0)
        top = here if top is None else jnp.maximum(top, here)
    top = jnp.max(top, axis=0, keepdims=True)
    total = jnp.zeros((8, tokens), jnp.float32)
    for block in range(low, len(keys)):
        grad_probs = mm(values[block][:, key_column], grad, NT)
        for at in range(0, tokens, CHUNK):
            rows = slice(block * tokens + at, block * tokens + at + CHUNK)
            weights = jnp.exp2((s_ref[rows, :] - top) * exp2_scale)
            total = total + jnp.sum(weights.reshape(CHUNK // 8, 8, tokens), axis=0)
            e_ref[rows, :] = weights.astype(jnp.bfloat16)
            ds_ref[rows, :] = (weights * (grad_probs[at : at + CHUNK, :] - term)).astype(jnp.bfloat16)
    inv_ref[...] = 1.0 / jnp.sum(total, axis=0, keepdims=True)


def add_gradients(head, valid, low, high, rank, q_ref, do_ref, down, up_q, wk, dk_acc, dv_acc, slot):
    tokens = q_ref.shape[0]
    _, e_ref, ds_ref, inv_ref = slot
    (_, group, inner), column, _ = head
    height = wk.shape[1]
    inverse = inv_ref[...] * valid
    inverse_rows = jnp.broadcast_to(inverse, (HEAD_SIZE, tokens)).T
    scaled = inverse_rows * score_scale
    lane = lax.broadcasted_iota(jnp.int32, (tokens, HEAD_SIZE), 1) // rank
    own_columns = jnp.where(lane == inner, down[...].astype(jnp.float32), 0.0)
    grad_n = (do_ref[:, column].astype(jnp.float32) * inverse_rows).astype(jnp.bfloat16)
    query_n = jnp.concatenate(
        [q_ref[:, column].astype(jnp.float32) * scaled, own_columns * scaled], axis=1
    ).astype(jnp.bfloat16)
    rows = pl.ds(pl.multiple_of(group * height + low, tokens), high - low)
    dv_acc[rows, :] += mm(e_ref[low:high, :], grad_n)
    dk_acc[rows, :] += mm(ds_ref[low:high, :], query_n)
    own = pl.ds(pl.multiple_of(group * HEAD_SIZE + inner * rank, rank), rank)
    up_q[...] += mm(wk[own, low:high], ds_ref[low:high, :]) * (inverse * score_scale)


def all_heads(
    with_previous, per_kv, rank, flags, keys, values, q_hbm, do_hbm, term, w_q, down, up_q, dk, dv, scratch
):
    listed, q, do, q_sem, do_sem, wk, *buffers = scratch
    tokens, width = q.shape
    groups = width // (per_kv * HEAD_SIZE)
    loads = []
    for g in range(groups):
        part = slice(g * per_kv * HEAD_SIZE, (g + 1) * per_kv * HEAD_SIZE)
        loads.append(
            [
                pltpu.make_async_copy(q_hbm.at[:, part], q.at[:, part], q_sem.at[g]),
                pltpu.make_async_copy(do_hbm.at[:, part], do.at[:, part], do_sem.at[g]),
            ]
        )
    for load in sum(loads, []):
        load.start()

    def wait(group):
        for load in loads[group]:
            load.wait()

    def wait_between(held, wanted):
        for g in range(1, groups):
            pl.when((g > held) & (g <= wanted))(functools.partial(wait, g))
        return jnp.maximum(held, wanted)

    height = wk.shape[1]
    for g in range(groups):
        stacked = jnp.concatenate(
            [w_q[:, h * HEAD_SIZE : (h + 1) * HEAD_SIZE] for h in range(g * per_kv, (g + 1) * per_kv)], axis=0
        )
        for block, key in enumerate(keys):
            wk[g * HEAD_SIZE : (g + 1) * HEAD_SIZE, block * tokens : (block + 1) * tokens] = mm(
                stacked, key[:, g * HEAD_SIZE : (g + 1) * HEAD_SIZE], NT
            ).astype(jnp.bfloat16)
    dk[...] = jnp.zeros_like(dk)
    dv[...] = jnp.zeros_like(dv)
    slots = (buffers[:4], buffers[4:])
    for _, e_ref, ds_ref, inv_ref in slots:
        e_ref[...] = jnp.zeros_like(e_ref)
        ds_ref[...] = jnp.zeros_like(ds_ref)
        inv_ref[...] = jnp.zeros_like(inv_ref)
    wait(0)
    index = lax.axis_index("seq")
    core = index % 2
    half = index // 2 % 2
    count = jnp.int32(0)
    for h in range(groups * per_kv):
        listed[count] = jnp.int32(h)
        needs = flags[h] != half
        count = count + jnp.where(needs == with_previous, 1, 0).astype(jnp.int32)

    def head_at(i):
        h = listed[jnp.clip(i, 0, count - 1)]
        group = h // per_kv
        return (
            (h, group, h - group * per_kv),
            pl.ds(pl.multiple_of(h * HEAD_SIZE, HEAD_SIZE), HEAD_SIZE),
            pl.ds(pl.multiple_of(group * HEAD_SIZE, HEAD_SIZE), HEAD_SIZE),
        )

    for which in range(2):
        low = 1 - which

        def softmax(i, slot):
            scores_and_softmax(head_at(i), low, 1, keys, values, q, do, term, slot)

        def gradients(i, slot):
            valid = jnp.where((i >= 0) & (i < count), 1.0, 0.0).astype(jnp.float32)
            add_gradients(
                head_at(i), valid, low * tokens, height, rank, q, do, down, up_q, wk, dk, dv, slot
            )

        @pl.when((core == which) & (count > 0))
        def _():
            def two(t, held):
                held = wait_between(held, head_at(2 * t + 1)[0][1])
                softmax(2 * t, slots[0])
                gradients(2 * t - 1, slots[1])
                softmax(2 * t + 1, slots[1])
                gradients(2 * t, slots[0])
                return held

            held = lax.fori_loop(0, (count + 1) // 2, two, jnp.int32(0))
            wait_between(held, jnp.int32(groups - 1))

            @pl.when(count % 2 == 0)
            def _():
                gradients(count - 1, slots[1])

    @pl.when(count == 0)
    def _():
        wait_between(jnp.int32(0), jnp.int32(groups - 1))


def own_kernel(
    per_kv, rank, flags, q, do, term, w_q, down, kv_own, kv_sib, up_q, dk, dv, *scratch
):
    up_q[...] = jnp.zeros_like(up_q)
    keys, values = ([kv.at[c] for kv in (kv_sib, kv_own)] for c in range(2))
    all_heads(False, per_kv, rank, flags, keys, values, q, do, term, w_q, down, up_q, dk, dv, scratch)


def previous_kernel(
    scale, per_kv, rank, flags, q, do, term, w_q, down, kv_own, kv_sib, kv_pc, kv_px,
    up_q_own, dk_own, dv_own, w_kv, down_win,
    keep_own, keep_pc, send, up_q, up_keep, up_send, grad_up,
    dk, dv, grads, *scratch,
):
    tokens = q.shape[0]
    up_q[...] = up_q_own[...]
    keys, values = ([kv.at[c] for kv in (kv_sib, kv_own, kv_pc, kv_px)] for c in range(2))
    all_heads(True, per_kv, rank, flags, keys, values, q, do, term, w_q, down, up_q, dk, dv, scratch)
    up_kv = [jnp.zeros((rank, 4 * tokens), jnp.float32) for _ in range(2)]
    kv_width = kv_own.shape[2]
    for g in range(kv_width // HEAD_SIZE):
        columns = slice(g * HEAD_SIZE, (g + 1) * HEAD_SIZE)
        low_row, own_row = g * 4 * tokens, g * 2 * tokens
        by_head = None
        for block in range(4):
            tail = dk[low_row + block * tokens : low_row + (block + 1) * tokens, HEAD_SIZE:]
            if block < 2:
                tail = tail + dk_own[own_row + block * tokens : own_row + (block + 1) * tokens, HEAD_SIZE:]
            part = mm(tail.T.astype(jnp.bfloat16), keys[block][:, columns])
            by_head = part if by_head is None else by_head + part
        for h in range(per_kv):
            at = (g * per_kv + h) * HEAD_SIZE
            grads[:rank, at : at + HEAD_SIZE] = by_head[h * rank : (h + 1) * rank, :]
        for c, acc, start in ((0, dk, dk_own), (1, dv, dv_own)):
            total = acc[low_row : low_row + 4 * tokens, :HEAD_SIZE]
            near = total[: 2 * tokens] + start[own_row : own_row + 2 * tokens, :HEAD_SIZE]
            low = jnp.concatenate([near, total[2 * tokens :]]).astype(jnp.bfloat16)
            keep_own[c, :, columns] = near[tokens:]
            keep_pc[c, :, columns] = total[2 * tokens : 3 * tokens]
            send[0, c, :, columns] = low[:tokens]
            send[1, c, :, columns] = low[3 * tokens :]
            up_kv[c] = up_kv[c] + mm(w_kv[c, :, columns], low, NT)
            own = slice(c * rank, (c + 1) * rank)
            grad_kv = mm(down_win[own, :], low)
            for r in range(rank):
                row, at = divmod((c * rank + r) * kv_width + g * HEAD_SIZE, grads.shape[1])
                grads[rank + row : rank + row + 1, at : at + HEAD_SIZE] = grad_kv[r : r + 1, :]
    sib, near, pc, px = (
        jnp.concatenate([up_kv[c][:, block * tokens : (block + 1) * tokens] for c in range(2)])
        for block in range(4)
    )
    grad_up[...] = (grads[...] * scale).astype(jnp.bfloat16)
    up_keep[...] = jnp.concatenate([near, pc])
    up_send[...] = jnp.concatenate([sib, px]).astype(jnp.bfloat16)


def attention(scale, flags, queries, grads, terms, w_q, down, kv_own, kv_sib):
    tokens, width = queries.shape
    kv_width = kv_own.shape[2]
    kv_local = kv_width // HEAD_SIZE
    per_kv = width // kv_width
    rank = w_q.shape[0]
    assert per_kv * rank == HEAD_SIZE
    f32, bf16 = jnp.float32, jnp.bfloat16
    shape = jax.ShapeDtypeStruct
    pairs = kv_local * per_kv * tokens * tokens
    smem = pl.BlockSpec(memory_space=pltpu.SMEM)
    vmem = pl.BlockSpec(memory_space=pltpu.VMEM)
    hbm = pl.BlockSpec(memory_space=pltpu.HBM)

    def scratch(blocks):
        rows = blocks * tokens
        slot = [
            pltpu.VMEM((rows, tokens), f32),
            pltpu.VMEM((rows, tokens), bf16),
            pltpu.VMEM((rows, tokens), bf16),
            pltpu.VMEM((1, tokens), f32),
        ]
        return [
            pltpu.SMEM((kv_local * per_kv + 1,), jnp.int32),
            pltpu.VMEM((tokens, width), bf16),
            pltpu.VMEM((tokens, width), bf16),
            pltpu.SemaphoreType.DMA((kv_local,)),
            pltpu.SemaphoreType.DMA((kv_local,)),
            pltpu.VMEM((kv_local * HEAD_SIZE, rows), bf16),
        ] + slot * 2

    def call(kernel, out_shape, scratch_shapes, work, name, *args):
        return pl.pallas_call(
            functools.partial(kernel, per_kv, rank),
            in_specs=[smem, hbm, hbm] + [vmem] * (len(args) - 3),
            out_specs=[vmem] * len(out_shape),
            out_shape=out_shape,
            scratch_shapes=scratch_shapes,
            compiler_params=pltpu.CompilerParams(vmem_limit_bytes=VMEM_LIMIT),
            cost_estimate=pl.CostEstimate(
                flops=work * pairs * HEAD_SIZE, bytes_accessed=6 * tokens * width, transcendentals=pairs
            ),
            name=name,
        )(*args)

    queries, grads = (pltpu.with_memory_space_constraint(a, pltpu.HBM) for a in (queries, grads))
    common = (flags, queries, grads, terms, w_q, down, kv_own, kv_sib)

    def own():
        return call(
            own_kernel,
            [
                shape((rank, tokens), f32),
                shape((2 * tokens * kv_local, 2 * HEAD_SIZE), f32),
                shape((2 * tokens * kv_local, HEAD_SIZE), f32),
            ],
            scratch(2),
            40,
            "own_chip_heads",
            *common,
        )

    def previous(kv_pc, kv_px, own_grads, w_kv, down_win):
        grad_rows = rank + 2 * rank * kv_width // width
        return call(
            functools.partial(previous_kernel, scale),
            [
                shape((2, tokens, kv_width), f32),
                shape((2, tokens, kv_width), f32),
                shape((2, 2, tokens, kv_width), bf16),
                shape((rank, tokens), f32),
                shape((4 * rank, tokens), f32),
                shape((4 * rank, tokens), bf16),
                shape((grad_rows, width), bf16),
            ],
            [
                pltpu.VMEM((4 * tokens * kv_local, 2 * HEAD_SIZE), f32),
                pltpu.VMEM((4 * tokens * kv_local, HEAD_SIZE), f32),
                pltpu.VMEM((grad_rows, width), f32),
            ]
            + scratch(4),
            80,
            "previous_chip_heads",
            *common,
            kv_pc,
            kv_px,
            *own_grads,
            w_kv,
            down_win,
        )

    return own, previous


def exchanged(value, axis, bit):
    return lax.ppermute(value, axis, [(i, i ^ bit) for i in range(lax.axis_size(axis))])


def moved(value, axis, by):
    count = lax.axis_size(axis)
    return lax.ppermute(value, axis, [(i, (i + by) % count) for i in range(count)])


def summed(value, axis):
    bit = 1
    while bit < lax.axis_size(axis):
        value = value + exchanged(value, axis, bit)
        bit *= 2
    return value


def small_call(kernel, out_shape, *args, scratch=(), limit=1):
    vmem = pl.BlockSpec(memory_space=pltpu.VMEM)
    return pl.pallas_call(
        kernel,
        in_specs=[vmem] * len(args),
        out_specs=[vmem] * len(out_shape),
        out_shape=out_shape,
        scratch_shapes=list(scratch),
        compiler_params=pltpu.CompilerParams(vmem_limit_bytes=limit * SMALL_VMEM),
    )(*args)


def place(unit, radix):
    return lax.axis_index("seq") // unit % radix


def lanes(index, wide):
    return pl.ds(pl.multiple_of(index * wide, HEAD_SIZE), wide)


def projected_and_stacked(down_weight, inputs, key_rows, value_rows):
    rows, width = down_weight.shape
    tokens, kv_width = key_rows.shape
    steps = kv_width // HEAD_SIZE
    args = [
        pltpu.with_memory_space_constraint(a, pltpu.HBM)
        for a in (down_weight, inputs, key_rows, value_rows)
    ]

    def kernel(weight, tokens_in, key, value, down, kv):
        part = mm(weight[...], tokens_in[...], NT)

        @pl.when(pl.program_id(0) == 0)
        def _():
            down[...] = part

        @pl.when(pl.program_id(0) > 0)
        def _():
            down[...] += part

        kv[0] = key[...]
        kv[1] = value[...]

    def columns(high, wide):
        return pl.BlockSpec((high, wide // steps), lambda g: (0, g))

    return pl.pallas_call(
        kernel,
        grid=(steps,),
        in_specs=[
            columns(rows, width),
            columns(tokens, width),
            columns(tokens, kv_width),
            columns(tokens, kv_width),
        ],
        out_specs=[
            pl.BlockSpec((rows, tokens), lambda g: (0, 0)),
            pl.BlockSpec((2, tokens, kv_width // steps), lambda g: (0, 0, g)),
        ],
        out_shape=[
            jax.ShapeDtypeStruct((rows, tokens), jnp.float32),
            jax.ShapeDtypeStruct((2, tokens, kv_width), jnp.bfloat16),
        ],
        compiler_params=pltpu.CompilerParams(
            dimension_semantics=("arbitrary",), vmem_limit_bytes=2 * SMALL_VMEM
        ),
    )(*args)


def up_sums(up_q, up_keep, received):
    rank, tokens = up_q.shape

    def kernel(up_q, keep, other, mine, to_send, previous):
        total = keep[...] + other[...].astype(jnp.float32)
        own = jnp.concatenate([up_q[...], total[: 2 * rank]])
        mine[...] = own
        to_send[...] = own.astype(jnp.bfloat16)
        previous[...] = total[2 * rank :].astype(jnp.bfloat16)

    shape = jax.ShapeDtypeStruct
    return small_call(
        kernel,
        [
            shape((3 * rank, tokens), jnp.float32),
            shape((3 * rank, tokens), jnp.bfloat16),
            shape((2 * rank, tokens), jnp.bfloat16),
        ],
        up_q,
        up_keep,
        received,
    )


def up_terms(mine, to_send, previous):
    heads, count = lax.axis_size("head"), lax.axis_size("seq")
    nearby = moved(previous, "seq", -2)
    if heads == 2:
        pairs = [
            (s * heads + h, (s - 2) % count * heads + 1 - h) for s in range(count) for h in range(heads)
        ]
        return [mine, exchanged(to_send, "head", 1), nearby, lax.ppermute(previous, ("seq", "head"), pairs)]
    rank = mine.shape[0] - previous.shape[0]
    total = jnp.concatenate([mine[:rank], mine[rank:] + nearby.astype(jnp.float32)])
    bit = 1
    while 2 * bit < heads:
        total = total + exchanged(total.astype(jnp.bfloat16), "head", bit).astype(jnp.float32)
        bit *= 2
    return [total, exchanged(total.astype(jnp.bfloat16), "head", bit)]


def weight_halves(terms, inputs, grad_up, scale):
    width = inputs.shape[1]
    wide = width // 2
    up_rows, tokens = terms[0].shape
    rows = up_rows + grad_up.shape[0]
    given = len(terms)

    def kernel(*refs):
        tokens_in, grads, up_low, *out = refs[given:]
        up = jnp.zeros((up_rows, tokens), jnp.float32)
        for term in refs[:given]:
            value = term[...].astype(jnp.float32)
            if value.shape[0] < up_rows:
                value = jnp.concatenate(
                    [jnp.zeros((up_rows - value.shape[0], tokens), jnp.float32), value]
                )
            up = up + value
        up = up.astype(jnp.bfloat16)
        up_low[...] = up
        for d in range(2):
            at = lanes(place(1, 2) ^ d, wide)
            out[d][...] = jnp.concatenate(
                [mm(up, tokens_in[:, at]) * scale, grads[:, at].astype(jnp.float32)]
            ).astype(jnp.bfloat16)

    shape = jax.ShapeDtypeStruct
    return small_call(
        kernel,
        [shape((up_rows, tokens), jnp.bfloat16)] + [shape((rows, wide), jnp.bfloat16)] * 2,
        *terms,
        inputs,
        grad_up,
        limit=2,
    )


def exchanged_pieces(pieces, unit):
    return [pieces[0]] + [exchanged(p, "seq", d * unit) for d, p in enumerate(pieces) if d]


def summed_and_cut(pieces, unit, radix):
    rows, whole = pieces[0].shape
    wide = whole // radix
    if wide % HEAD_SIZE:
        total = sum(p.astype(jnp.float32) for p in pieces).astype(jnp.bfloat16)
        return [
            lax.dynamic_slice_in_dim(total, (place(unit, radix) ^ d) * wide, wide, 1)
            for d in range(radix)
        ]
    given = len(pieces)

    def kernel(*refs):
        total = refs[-1]
        total[...] = sum(p[...].astype(jnp.float32) for p in refs[:given])
        for d in range(radix):
            refs[given + d][...] = total[:, lanes(place(unit, radix) ^ d, wide)].astype(jnp.bfloat16)

    return small_call(
        kernel,
        [jax.ShapeDtypeStruct((rows, wide), jnp.bfloat16)] * radix,
        *pieces,
        scratch=[pltpu.VMEM((rows, whole), jnp.float32)],
    )


def joined(pieces, unit):
    rows, wide = pieces[0].shape
    radix = len(pieces)
    if wide % HEAD_SIZE:
        whole = jnp.zeros((rows, radix * wide), jnp.bfloat16)
        for d in range(radix):
            whole = lax.dynamic_update_slice_in_dim(
                whole, pieces[d], (place(unit, radix) ^ d) * wide, 1
            )
        return whole

    def kernel(*refs):
        for d in range(radix):
            refs[radix][:, lanes(place(unit, radix) ^ d, wide)] = refs[d][...]

    return small_call(kernel, [jax.ShapeDtypeStruct((rows, radix * wide), jnp.bfloat16)], *pieces)[0]


def joined_outputs(pieces, rank, kv_shape):
    rows, wide = pieces[0].shape
    extra = rows - 4 * rank
    each = wide // kv_shape[1]
    per_row = kv_shape[0] // extra

    def kernel(one, two, down, up_q, up_kv):
        for d, half in enumerate((one, two)):
            at = place(1, 2) ^ d
            piece = half[...].astype(jnp.float32)
            down[:, lanes(at, wide)] = piece[: 3 * rank]
            up_q[:, lanes(at, wide)] = piece[3 * rank : 4 * rank]
            for i in range(extra):
                for b in range(each):
                    up_kv[pl.ds(per_row * i + each * at + b, 1), :] = piece[
                        4 * rank + i : 4 * rank + i + 1, b * kv_shape[1] : (b + 1) * kv_shape[1]
                    ]

    shape = jax.ShapeDtypeStruct
    return small_call(
        kernel,
        [
            shape((3 * rank, 2 * wide), jnp.float32),
            shape((rank, 2 * wide), jnp.float32),
            shape(kv_shape, jnp.float32),
        ],
        *pieces,
    )


def per_device(
    queries,
    layer_key_rows,
    layer_value_rows,
    output_gradient,
    output_row_sums,
    shifted_head_flags,
    inputs,
    adapter_down_weight,
    query_up_weight,
    key_value_up_weight,
):
    seq_count = lax.axis_size("seq")
    tokens, width = queries.shape
    kv_width = layer_key_rows.shape[1]
    whole_len = tokens * seq_count
    rank = adapter_down_weight.shape[1]
    assert GROUP == 4 * tokens and SHIFT == 2 * tokens
    levels = (seq_count.bit_length() - 1) // 2
    assert 4**levels == seq_count
    flattened_down = adapter_down_weight.reshape(3 * rank, width)
    scale = adapter_scale / math.sqrt(whole_len)
    down_part, kv_own = projected_and_stacked(flattened_down, inputs, layer_key_rows, layer_value_rows)
    kv_pc = moved(kv_own, "seq", 2)
    kv_sib = exchanged(kv_own, "seq", 1)

    down_low = summed(down_part, "head").astype(jnp.bfloat16)
    down_tiled = jnp.tile(down_low[:rank].T, (1, HEAD_SIZE // rank))
    down_own = down_low[rank:]
    down_pc = moved(down_own, "seq", 2)

    own, previous = attention(
        scale,
        shifted_head_flags,
        queries,
        output_gradient,
        output_row_sums,
        query_up_weight,
        down_tiled,
        kv_own,
        kv_sib,
    )
    own_grads, kv_pc, down_pc = lax.optimization_barrier((own(), kv_pc, down_pc))
    kv_px = exchanged(kv_pc, "seq", 1)
    down_others = exchanged(jnp.concatenate([down_own, down_pc]), "seq", 1)
    down_win = jnp.concatenate(
        [down_others[: 2 * rank], down_own, down_pc, down_others[2 * rank :]], axis=1
    )
    keep_own, keep_pc, send, up_q, up_keep, up_send, grad_up = previous(
        kv_pc, kv_px, own_grads, key_value_up_weight, down_win
    )

    up_received, send = lax.optimization_barrier((exchanged(up_send, "seq", 1), send))
    received = exchanged(send, "seq", 1)
    terms = up_terms(*up_sums(up_q, up_keep, up_received))
    back = (keep_pc + received[1].astype(jnp.float32)).astype(jnp.bfloat16)
    terms, back = lax.optimization_barrier((terms, back))
    back = moved(back, "seq", -2)
    up_low, *pieces = weight_halves(terms, inputs, grad_up, scale)
    pieces = exchanged_pieces(summed_and_cut(exchanged_pieces(pieces, 1), 2, 2), 2)
    for level in range(1, levels):
        pieces = summed_and_cut(pieces, 4**level, 4)
        if level == 1:
            pieces, back = lax.optimization_barrier((pieces, back))
        pieces = exchanged_pieces(pieces, 4**level)
    total = sum(p.astype(jnp.float32) for p in pieces).astype(jnp.bfloat16)
    key_value_gradient = (
        keep_own + received[0].astype(jnp.float32) + back.astype(jnp.float32)
    ).astype(jnp.bfloat16)
    grad_inputs = (
        adapter_scale
        * lax.dot_general(
            up_low, flattened_down, (((0,), (0,)), ((), ())), preferred_element_type=jnp.float32
        )
    ).astype(jnp.bfloat16)
    for level in range(levels - 1, 0, -1):
        total = joined(exchanged_pieces([total] * 4, 4**level), 4**level)
    total, key_value_gradient = lax.optimization_barrier((total, key_value_gradient))
    total = joined(exchanged_pieces([total] * 2, 2), 2)
    total, grad_inputs = lax.optimization_barrier((total, grad_inputs))
    down_gradient, grad_up_q, grad_up_kv = joined_outputs(
        exchanged_pieces([total] * 2, 1), rank, (2 * rank, kv_width)
    )
    return (
        grad_inputs,
        key_value_gradient,
        down_gradient.reshape(3, rank, width),
        grad_up_q,
        grad_up_kv.reshape(2, rank, kv_width),
    )


def solution(mesh):
    placed = (
        P("seq", "head"),
        P("seq", "head"),
        P("seq", "head"),
        P("seq", "head"),
        P("head", "seq"),
        P("head"),
        P("seq", "head"),
        P(None, None, "head"),
        P(None, "head"),
        P(None, None, "head"),
    )
    return jax.shard_map(
        per_device,
        mesh=mesh,
        in_specs=placed,
        out_specs=(
            P("seq", "head"),
            P(None, "seq", "head"),
            P(None, None, "head"),
            P(None, "head"),
            P(None, None, "head"),
        ),
        check_vma=False,
    )
```

```python
import functools
import math

import jax
import jax.numpy as jnp
from jax import lax
from jax.experimental import pallas as pl
from jax.experimental.pallas import tpu as pltpu
from jax.sharding import PartitionSpec as P

HEAD_SIZE = 128
GROUP = 1024
SHIFT = 512
CHUNK = 32
SMALL_VMEM = 8 * 1024 * 1024
VMEM_LIMIT = 32 * 1024 * 1024

adapter_scale = 2.0
masked_score = -1e30
score_scale = HEAD_SIZE ** (-0.5)

NT = (((1,), (1,)), ((), ()))
NN = (((1,), (0,)), ((), ()))


def mm(left, right, dims=NN):
    return lax.dot_general(left, right, dims, preferred_element_type=jnp.float32)


def scores_and_softmax(head, low, diag, keys, values, q_ref, do_ref, term_ref, slot):
    tokens = q_ref.shape[0]
    s_ref, e_ref, ds_ref, inv_ref = slot
    group, column, key_column = head
    query = q_ref[:, column]
    grad = do_ref[:, column]
    term = term_ref[pl.ds(group[0], 1), :]
    top = None
    for block in range(low, len(keys)):
        rows = slice(block * tokens, (block + 1) * tokens)
        scores = mm(keys[block][:, key_column], query, NT)
        if block == diag:
            key_row = lax.broadcasted_iota(jnp.int32, (tokens, tokens), 0)
            query_row = lax.broadcasted_iota(jnp.int32, (tokens, tokens), 1)
            scores = jnp.where(key_row <= query_row, scores, masked_score)
        s_ref[rows, :] = scores
        here = jnp.max(scores.reshape(tokens // 8, 8, tokens), axis=0)
        top = here if top is None else jnp.maximum(top, here)
    top = jnp.max(top, axis=0, keepdims=True)
    total = jnp.zeros((8, tokens), jnp.float32)
    for block in range(low, len(keys)):
        grad_probs = mm(values[block][:, key_column], grad, NT)
        for at in range(0, tokens, CHUNK):
            rows = slice(block * tokens + at, block * tokens + at + CHUNK)
            weights = jnp.exp((s_ref[rows, :] - top) * score_scale)
            total = total + jnp.sum(weights.reshape(CHUNK // 8, 8, tokens), axis=0)
            e_ref[rows, :] = weights.astype(jnp.bfloat16)
            ds_ref[rows, :] = (weights * (grad_probs[at : at + CHUNK, :] - term)).astype(jnp.bfloat16)
    inv_ref[...] = 1.0 / jnp.sum(total, axis=0, keepdims=True)


def add_gradients(head, valid, low, high, q_ref, do_ref, w_q, down, up_q, grad_q, kt, dk_acc, dv_acc, slot):
    tokens = q_ref.shape[0]
    _, e_ref, ds_ref, inv_ref = slot
    (_, group), column, key_column = head
    height = kt.shape[1]
    inverse = inv_ref[...] * valid
    inverse_rows = jnp.broadcast_to(inverse, (HEAD_SIZE, tokens)).T
    grad_n = (do_ref[:, column].astype(jnp.float32) * inverse_rows).astype(jnp.bfloat16)
    query_n = (q_ref[:, column].astype(jnp.float32) * (inverse_rows * score_scale)).astype(jnp.bfloat16)
    rows = pl.ds(pl.multiple_of(group * height + low, tokens), high - low)
    dv_acc[rows, :] += mm(e_ref[low:high, :], grad_n)
    dk_acc[rows, :] += mm(ds_ref[low:high, :], query_n)
    query_grad = mm(kt[key_column, low:high], ds_ref[low:high, :]) * (inverse * score_scale)
    query_grad = query_grad.astype(jnp.bfloat16)
    up_q[...] += mm(w_q[:, column], query_grad)
    grad_q[: down.shape[0], column] = mm(down[...], query_grad, NT)


def all_heads(
    with_previous, per_kv, flags, keys, values, q_hbm, do_hbm, term, w_q, down, up_q, grad_q, dk, dv, scratch
):
    listed, q, do, q_sem, do_sem, kt, *buffers = scratch
    tokens, width = q.shape
    groups = width // (per_kv * HEAD_SIZE)
    loads = []
    for g in range(groups):
        part = slice(g * per_kv * HEAD_SIZE, (g + 1) * per_kv * HEAD_SIZE)
        loads.append(
            [
                pltpu.make_async_copy(q_hbm.at[:, part], q.at[:, part], q_sem.at[g]),
                pltpu.make_async_copy(do_hbm.at[:, part], do.at[:, part], do_sem.at[g]),
            ]
        )
    for load in sum(loads, []):
        load.start()

    def wait(group):
        for load in loads[group]:
            load.wait()

    def wait_between(held, wanted):
        for g in range(1, groups):
            pl.when((g > held) & (g <= wanted))(functools.partial(wait, g))
        return jnp.maximum(held, wanted)

    height = kt.shape[1]
    for g in range(groups):
        columns = slice(g * HEAD_SIZE, (g + 1) * HEAD_SIZE)
        for block, key in enumerate(keys):
            kt[columns, block * tokens : (block + 1) * tokens] = key[:, columns].T
    grad_q[...] = jnp.zeros_like(grad_q)
    dk[...] = jnp.zeros_like(dk)
    dv[...] = jnp.zeros_like(dv)
    slots = (buffers[:4], buffers[4:])
    for _, e_ref, ds_ref, inv_ref in slots:
        e_ref[...] = jnp.zeros_like(e_ref)
        ds_ref[...] = jnp.zeros_like(ds_ref)
        inv_ref[...] = jnp.zeros_like(inv_ref)
    wait(0)
    index = lax.axis_index("seq")
    core = index % 2
    half = index // 2 % 2
    count = jnp.int32(0)
    for h in range(groups * per_kv):
        listed[count] = jnp.int32(h)
        needs = flags[h] != half
        count = count + jnp.where(needs == with_previous, 1, 0).astype(jnp.int32)

    def head_at(i):
        h = listed[jnp.clip(i, 0, count - 1)]
        group = h // per_kv
        return (
            (h, group),
            pl.ds(pl.multiple_of(h * HEAD_SIZE, HEAD_SIZE), HEAD_SIZE),
            pl.ds(pl.multiple_of(group * HEAD_SIZE, HEAD_SIZE), HEAD_SIZE),
        )

    for which in range(2):
        low = 1 - which

        def softmax(i, slot):
            scores_and_softmax(head_at(i), low, 1, keys, values, q, do, term, slot)

        def gradients(i, slot):
            valid = jnp.where((i >= 0) & (i < count), 1.0, 0.0).astype(jnp.float32)
            add_gradients(
                head_at(i), valid, low * tokens, height, q, do, w_q, down, up_q, grad_q, kt, dk, dv, slot
            )

        @pl.when((core == which) & (count > 0))
        def _():
            def two(t, held):
                held = wait_between(held, head_at(2 * t + 1)[0][1])
                softmax(2 * t, slots[0])
                gradients(2 * t - 1, slots[1])
                softmax(2 * t + 1, slots[1])
                gradients(2 * t, slots[0])
                return held

            held = lax.fori_loop(0, (count + 1) // 2, two, jnp.int32(0))
            wait_between(held, jnp.int32(groups - 1))

            @pl.when(count % 2 == 0)
            def _():
                gradients(count - 1, slots[1])

    @pl.when(count == 0)
    def _():
        wait_between(jnp.int32(0), jnp.int32(groups - 1))


def own_kernel(
    per_kv, rank, flags, q, do, term, w_q, down, kv_own, kv_sib, up_q, grad_q, dk, dv, *scratch
):
    up_q[...] = jnp.zeros_like(up_q)
    keys, values = ([kv.at[c] for kv in (kv_sib, kv_own)] for c in range(2))
    all_heads(False, per_kv, flags, keys, values, q, do, term, w_q, down, up_q, grad_q, dk, dv, scratch)


def previous_kernel(
    scale, per_kv, rank, flags, q, do, term, w_q, down, kv_own, kv_sib, kv_pc, kv_px,
    up_q_own, grad_q_own, dk_own, dv_own, w_kv, down_win,
    keep_own, keep_pc, send, up_q, up_keep, up_send, grad_up,
    dk, dv, grads, *scratch,
):
    tokens = q.shape[0]
    up_q[...] = up_q_own[...]
    keys, values = ([kv.at[c] for kv in (kv_sib, kv_own, kv_pc, kv_px)] for c in range(2))
    all_heads(True, per_kv, flags, keys, values, q, do, term, w_q, down, up_q, grads, dk, dv, scratch)
    grads[:rank, :] += grad_q_own[...]
    up_kv = [jnp.zeros((rank, 4 * tokens), jnp.float32) for _ in range(2)]
    kv_width = kv_own.shape[2]
    for g in range(kv_width // HEAD_SIZE):
        columns = slice(g * HEAD_SIZE, (g + 1) * HEAD_SIZE)
        low_row, own_row = g * 4 * tokens, g * 2 * tokens
        for c, acc, start in ((0, dk, dk_own), (1, dv, dv_own)):
            total = acc[low_row : low_row + 4 * tokens, :]
            near = total[: 2 * tokens] + start[own_row : own_row + 2 * tokens, :]
            low = jnp.concatenate([near, total[2 * tokens :]]).astype(jnp.bfloat16)
            keep_own[c, :, columns] = near[tokens:]
            keep_pc[c, :, columns] = total[2 * tokens : 3 * tokens]
            send[0, c, :, columns] = low[:tokens]
            send[1, c, :, columns] = low[3 * tokens :]
            up_kv[c] = up_kv[c] + mm(w_kv[c, :, columns], low, NT)
            own = slice(c * rank, (c + 1) * rank)
            grad_kv = mm(down_win[own, :], low)
            for r in range(rank):
                row, at = divmod((c * rank + r) * kv_width + g * HEAD_SIZE, grads.shape[1])
                grads[rank + row : rank + row + 1, at : at + HEAD_SIZE] = grad_kv[r : r + 1, :]
    sib, near, pc, px = (
        jnp.concatenate([up_kv[c][:, block * tokens : (block + 1) * tokens] for c in range(2)])
        for block in range(4)
    )
    grad_up[...] = (grads[...] * scale).astype(jnp.bfloat16)
    up_keep[...] = jnp.concatenate([near, pc])
    up_send[...] = jnp.concatenate([sib, px]).astype(jnp.bfloat16)


def attention(scale, flags, queries, grads, terms, w_q, down, kv_own, kv_sib):
    tokens, width = queries.shape
    kv_width = kv_own.shape[2]
    kv_local = kv_width // HEAD_SIZE
    per_kv = width // kv_width
    rank = w_q.shape[0]
    f32, bf16 = jnp.float32, jnp.bfloat16
    shape = jax.ShapeDtypeStruct
    pairs = kv_local * per_kv * tokens * tokens
    smem = pl.BlockSpec(memory_space=pltpu.SMEM)
    vmem = pl.BlockSpec(memory_space=pltpu.VMEM)
    hbm = pl.BlockSpec(memory_space=pltpu.HBM)

    def scratch(blocks):
        rows = blocks * tokens
        slot = [
            pltpu.VMEM((rows, tokens), f32),
            pltpu.VMEM((rows, tokens), bf16),
            pltpu.VMEM((rows, tokens), bf16),
            pltpu.VMEM((1, tokens), f32),
        ]
        return [
            pltpu.SMEM((kv_local * per_kv + 1,), jnp.int32),
            pltpu.VMEM((tokens, width), bf16),
            pltpu.VMEM((tokens, width), bf16),
            pltpu.SemaphoreType.DMA((kv_local,)),
            pltpu.SemaphoreType.DMA((kv_local,)),
            pltpu.VMEM((kv_local * HEAD_SIZE, rows), bf16),
        ] + slot * 2

    def call(kernel, out_shape, scratch_shapes, work, name, *args):
        return pl.pallas_call(
            functools.partial(kernel, per_kv, rank),
            in_specs=[smem, hbm, hbm] + [vmem] * (len(args) - 3),
            out_specs=[vmem] * len(out_shape),
            out_shape=out_shape,
            scratch_shapes=scratch_shapes,
            compiler_params=pltpu.CompilerParams(vmem_limit_bytes=VMEM_LIMIT),
            cost_estimate=pl.CostEstimate(
                flops=work * pairs * HEAD_SIZE, bytes_accessed=6 * tokens * width, transcendentals=pairs
            ),
            name=name,
        )(*args)

    queries, grads = (pltpu.with_memory_space_constraint(a, pltpu.HBM) for a in (queries, grads))
    common = (flags, queries, grads, terms, w_q, down, kv_own, kv_sib)

    def own():
        return call(
            own_kernel,
            [
                shape((rank, tokens), f32),
                shape((rank, width), f32),
                shape((2 * tokens * kv_local, HEAD_SIZE), f32),
                shape((2 * tokens * kv_local, HEAD_SIZE), f32),
            ],
            scratch(2),
            40,
            "own_chip_heads",
            *common,
        )

    def previous(kv_pc, kv_px, own_grads, w_kv, down_win):
        grad_rows = rank + 2 * rank * kv_width // width
        return call(
            functools.partial(previous_kernel, scale),
            [
                shape((2, tokens, kv_width), f32),
                shape((2, tokens, kv_width), f32),
                shape((2, 2, tokens, kv_width), bf16),
                shape((rank, tokens), f32),
                shape((4 * rank, tokens), f32),
                shape((4 * rank, tokens), bf16),
                shape((grad_rows, width), bf16),
            ],
            [
                pltpu.VMEM((4 * tokens * kv_local, HEAD_SIZE), f32),
                pltpu.VMEM((4 * tokens * kv_local, HEAD_SIZE), f32),
                pltpu.VMEM((grad_rows, width), f32),
            ]
            + scratch(4),
            80,
            "previous_chip_heads",
            *common,
            kv_pc,
            kv_px,
            *own_grads,
            w_kv,
            down_win,
        )

    return own, previous


def exchanged(value, axis, bit):
    return lax.ppermute(value, axis, [(i, i ^ bit) for i in range(lax.axis_size(axis))])


def moved(value, axis, by):
    count = lax.axis_size(axis)
    return lax.ppermute(value, axis, [(i, (i + by) % count) for i in range(count)])


def summed(value, axis):
    bit = 1
    while bit < lax.axis_size(axis):
        value = value + exchanged(value, axis, bit)
        bit *= 2
    return value


def small_call(kernel, out_shape, *args, scratch=(), limit=1):
    vmem = pl.BlockSpec(memory_space=pltpu.VMEM)
    return pl.pallas_call(
        kernel,
        in_specs=[vmem] * len(args),
        out_specs=[vmem] * len(out_shape),
        out_shape=out_shape,
        scratch_shapes=list(scratch),
        compiler_params=pltpu.CompilerParams(vmem_limit_bytes=limit * SMALL_VMEM),
    )(*args)


def place(unit, radix):
    return lax.axis_index("seq") // unit % radix


def lanes(index, wide):
    return pl.ds(pl.multiple_of(index * wide, HEAD_SIZE), wide)


def projected_and_stacked(down_weight, inputs, key_rows, value_rows):
    rows, width = down_weight.shape
    tokens, kv_width = key_rows.shape
    steps = kv_width // HEAD_SIZE
    args = [
        pltpu.with_memory_space_constraint(a, pltpu.HBM)
        for a in (down_weight, inputs, key_rows, value_rows)
    ]

    def kernel(weight, tokens_in, key, value, down, kv):
        part = mm(weight[...], tokens_in[...], NT)

        @pl.when(pl.program_id(0) == 0)
        def _():
            down[...] = part

        @pl.when(pl.program_id(0) > 0)
        def _():
            down[...] += part

        kv[0] = key[...]
        kv[1] = value[...]

    def columns(high, wide):
        return pl.BlockSpec((high, wide // steps), lambda g: (0, g))

    return pl.pallas_call(
        kernel,
        grid=(steps,),
        in_specs=[
            columns(rows, width),
            columns(tokens, width),
            columns(tokens, kv_width),
            columns(tokens, kv_width),
        ],
        out_specs=[
            pl.BlockSpec((rows, tokens), lambda g: (0, 0)),
            pl.BlockSpec((2, tokens, kv_width // steps), lambda g: (0, 0, g)),
        ],
        out_shape=[
            jax.ShapeDtypeStruct((rows, tokens), jnp.float32),
            jax.ShapeDtypeStruct((2, tokens, kv_width), jnp.bfloat16),
        ],
        compiler_params=pltpu.CompilerParams(
            dimension_semantics=("arbitrary",), vmem_limit_bytes=2 * SMALL_VMEM
        ),
    )(*args)


def up_sums(up_q, up_keep, received):
    rank, tokens = up_q.shape

    def kernel(up_q, keep, other, mine, to_send, previous):
        total = keep[...] + other[...].astype(jnp.float32)
        own = jnp.concatenate([up_q[...], total[: 2 * rank]])
        mine[...] = own
        to_send[...] = own.astype(jnp.bfloat16)
        previous[...] = total[2 * rank :].astype(jnp.bfloat16)

    shape = jax.ShapeDtypeStruct
    return small_call(
        kernel,
        [
            shape((3 * rank, tokens), jnp.float32),
            shape((3 * rank, tokens), jnp.bfloat16),
            shape((2 * rank, tokens), jnp.bfloat16),
        ],
        up_q,
        up_keep,
        received,
    )


def up_terms(mine, to_send, previous):
    heads, count = lax.axis_size("head"), lax.axis_size("seq")
    nearby = moved(previous, "seq", -2)
    if heads == 2:
        pairs = [
            (s * heads + h, (s - 2) % count * heads + 1 - h) for s in range(count) for h in range(heads)
        ]
        return [mine, exchanged(to_send, "head", 1), nearby, lax.ppermute(previous, ("seq", "head"), pairs)]
    rank = mine.shape[0] - previous.shape[0]
    total = jnp.concatenate([mine[:rank], mine[rank:] + nearby.astype(jnp.float32)])
    bit = 1
    while 2 * bit < heads:
        total = total + exchanged(total.astype(jnp.bfloat16), "head", bit).astype(jnp.float32)
        bit *= 2
    return [total, exchanged(total.astype(jnp.bfloat16), "head", bit)]


def weight_halves(terms, inputs, grad_up, scale):
    width = inputs.shape[1]
    wide = width // 2
    up_rows, tokens = terms[0].shape
    rows = up_rows + grad_up.shape[0]
    given = len(terms)

    def kernel(*refs):
        tokens_in, grads, up_low, *out = refs[given:]
        up = jnp.zeros((up_rows, tokens), jnp.float32)
        for term in refs[:given]:
            value = term[...].astype(jnp.float32)
            if value.shape[0] < up_rows:
                value = jnp.concatenate(
                    [jnp.zeros((up_rows - value.shape[0], tokens), jnp.float32), value]
                )
            up = up + value
        up = up.astype(jnp.bfloat16)
        up_low[...] = up
        for d in range(2):
            at = lanes(place(1, 2) ^ d, wide)
            out[d][...] = jnp.concatenate(
                [mm(up, tokens_in[:, at]) * scale, grads[:, at].astype(jnp.float32)]
            ).astype(jnp.bfloat16)

    shape = jax.ShapeDtypeStruct
    return small_call(
        kernel,
        [shape((up_rows, tokens), jnp.bfloat16)] + [shape((rows, wide), jnp.bfloat16)] * 2,
        *terms,
        inputs,
        grad_up,
        limit=2,
    )


def exchanged_pieces(pieces, unit):
    return [pieces[0]] + [exchanged(p, "seq", d * unit) for d, p in enumerate(pieces) if d]


def summed_and_cut(pieces, unit, radix):
    rows, whole = pieces[0].shape
    wide = whole // radix
    if wide % HEAD_SIZE:
        total = sum(p.astype(jnp.float32) for p in pieces).astype(jnp.bfloat16)
        return [
            lax.dynamic_slice_in_dim(total, (place(unit, radix) ^ d) * wide, wide, 1)
            for d in range(radix)
        ]
    given = len(pieces)

    def kernel(*refs):
        total = refs[-1]
        total[...] = sum(p[...].astype(jnp.float32) for p in refs[:given])
        for d in range(radix):
            refs[given + d][...] = total[:, lanes(place(unit, radix) ^ d, wide)].astype(jnp.bfloat16)

    return small_call(
        kernel,
        [jax.ShapeDtypeStruct((rows, wide), jnp.bfloat16)] * radix,
        *pieces,
        scratch=[pltpu.VMEM((rows, whole), jnp.float32)],
    )


def joined(pieces, unit):
    rows, wide = pieces[0].shape
    radix = len(pieces)
    if wide % HEAD_SIZE:
        whole = jnp.zeros((rows, radix * wide), jnp.bfloat16)
        for d in range(radix):
            whole = lax.dynamic_update_slice_in_dim(
                whole, pieces[d], (place(unit, radix) ^ d) * wide, 1
            )
        return whole

    def kernel(*refs):
        for d in range(radix):
            refs[radix][:, lanes(place(unit, radix) ^ d, wide)] = refs[d][...]

    return small_call(kernel, [jax.ShapeDtypeStruct((rows, radix * wide), jnp.bfloat16)], *pieces)[0]


def joined_outputs(pieces, rank, kv_shape):
    rows, wide = pieces[0].shape
    extra = rows - 4 * rank
    each = wide // kv_shape[1]
    per_row = kv_shape[0] // extra

    def kernel(one, two, down, up_q, up_kv):
        for d, half in enumerate((one, two)):
            at = place(1, 2) ^ d
            piece = half[...].astype(jnp.float32)
            down[:, lanes(at, wide)] = piece[: 3 * rank]
            up_q[:, lanes(at, wide)] = piece[3 * rank : 4 * rank]
            for i in range(extra):
                for b in range(each):
                    up_kv[pl.ds(per_row * i + each * at + b, 1), :] = piece[
                        4 * rank + i : 4 * rank + i + 1, b * kv_shape[1] : (b + 1) * kv_shape[1]
                    ]

    shape = jax.ShapeDtypeStruct
    return small_call(
        kernel,
        [
            shape((3 * rank, 2 * wide), jnp.float32),
            shape((rank, 2 * wide), jnp.float32),
            shape(kv_shape, jnp.float32),
        ],
        *pieces,
    )


def per_device(
    queries,
    layer_key_rows,
    layer_value_rows,
    output_gradient,
    output_row_sums,
    shifted_head_flags,
    inputs,
    adapter_down_weight,
    query_up_weight,
    key_value_up_weight,
):
    seq_count = lax.axis_size("seq")
    tokens, width = queries.shape
    kv_width = layer_key_rows.shape[1]
    whole_len = tokens * seq_count
    rank = adapter_down_weight.shape[1]
    assert GROUP == 4 * tokens and SHIFT == 2 * tokens
    levels = (seq_count.bit_length() - 1) // 2
    assert 4**levels == seq_count
    flattened_down = adapter_down_weight.reshape(3 * rank, width)
    scale = adapter_scale / math.sqrt(whole_len)
    down_part, kv_own = projected_and_stacked(flattened_down, inputs, layer_key_rows, layer_value_rows)
    kv_pc = moved(kv_own, "seq", 2)
    kv_sib = exchanged(kv_own, "seq", 1)

    down_low = summed(down_part, "head").astype(jnp.bfloat16)
    down_own = down_low[rank:]
    down_pc = moved(down_own, "seq", 2)

    own, previous = attention(
        scale,
        shifted_head_flags,
        queries,
        output_gradient,
        output_row_sums,
        query_up_weight,
        down_low[:rank],
        kv_own,
        kv_sib,
    )
    own_grads, kv_pc, down_pc = lax.optimization_barrier((own(), kv_pc, down_pc))
    kv_px = exchanged(kv_pc, "seq", 1)
    down_others = exchanged(jnp.concatenate([down_own, down_pc]), "seq", 1)
    down_win = jnp.concatenate(
        [down_others[: 2 * rank], down_own, down_pc, down_others[2 * rank :]], axis=1
    )
    keep_own, keep_pc, send, up_q, up_keep, up_send, grad_up = previous(
        kv_pc, kv_px, own_grads, key_value_up_weight, down_win
    )

    up_received, send = lax.optimization_barrier((exchanged(up_send, "seq", 1), send))
    received = exchanged(send, "seq", 1)
    terms = up_terms(*up_sums(up_q, up_keep, up_received))
    back = (keep_pc + received[1].astype(jnp.float32)).astype(jnp.bfloat16)
    up_low, *pieces = weight_halves(terms, inputs, grad_up, scale)
    pieces = exchanged_pieces(summed_and_cut(exchanged_pieces(pieces, 1), 2, 2), 2)
    pieces, back = lax.optimization_barrier((pieces, back))
    back = moved(back, "seq", -2)
    for level in range(1, levels):
        pieces = exchanged_pieces(summed_and_cut(pieces, 4**level, 4), 4**level)
    total = sum(p.astype(jnp.float32) for p in pieces).astype(jnp.bfloat16)
    key_value_gradient = (
        keep_own + received[0].astype(jnp.float32) + back.astype(jnp.float32)
    ).astype(jnp.bfloat16)
    grad_inputs = (
        adapter_scale
        * lax.dot_general(
            up_low, flattened_down, (((0,), (0,)), ((), ())), preferred_element_type=jnp.float32
        )
    ).astype(jnp.bfloat16)
    for level in range(levels - 1, 0, -1):
        total = joined(exchanged_pieces([total] * 4, 4**level), 4**level)
    total, grad_inputs = lax.optimization_barrier((total, grad_inputs))
    total = joined(exchanged_pieces([total] * 2, 2), 2)
    down_gradient, grad_up_q, grad_up_kv = joined_outputs(
        exchanged_pieces([total] * 2, 1), rank, (2 * rank, kv_width)
    )
    return (
        grad_inputs,
        key_value_gradient,
        down_gradient.reshape(3, rank, width),
        grad_up_q,
        grad_up_kv.reshape(2, rank, kv_width),
    )


def solution(mesh):
    placed = (
        P("seq", "head"),
        P("seq", "head"),
        P("seq", "head"),
        P("seq", "head"),
        P("head", "seq"),
        P("head"),
        P("seq", "head"),
        P(None, None, "head"),
        P(None, "head"),
        P(None, None, "head"),
    )
    return jax.shard_map(
        per_device,
        mesh=mesh,
        in_specs=placed,
        out_specs=(
            P("seq", "head"),
            P(None, "seq", "head"),
            P(None, None, "head"),
            P(None, "head"),
            P(None, None, "head"),
        ),
        check_vma=False,
    )
```

```python
import functools
import math

import jax
import jax.numpy as jnp
from jax import lax
from jax.experimental import pallas as pl
from jax.experimental.pallas import tpu as pltpu
from jax.sharding import PartitionSpec as P

HEAD_SIZE = 128
GROUP = 1024
SHIFT = 512
CHUNK = 32
SMALL_VMEM = 8 * 1024 * 1024
VMEM_LIMIT = 32 * 1024 * 1024

adapter_scale = 2.0
masked_score = -1e30
score_scale = HEAD_SIZE ** (-0.5)

NT = (((1,), (1,)), ((), ()))
NN = (((1,), (0,)), ((), ()))


def mm(left, right, dims=NN):
    return lax.dot_general(left, right, dims, preferred_element_type=jnp.float32)


def scores_and_softmax(head, low, diag, keys, values, q_ref, do_ref, term_ref, slot):
    tokens = q_ref.shape[0]
    s_ref, e_ref, ds_ref, inv_ref = slot
    group, column, key_column = head
    query = q_ref[:, column]
    grad = do_ref[:, column]
    term = term_ref[pl.ds(group[0], 1), :]
    top = None
    for block in range(low, len(keys)):
        rows = slice(block * tokens, (block + 1) * tokens)
        scores = mm(keys[block][:, key_column], query, NT)
        if block == diag:
            key_row = lax.broadcasted_iota(jnp.int32, (tokens, tokens), 0)
            query_row = lax.broadcasted_iota(jnp.int32, (tokens, tokens), 1)
            scores = jnp.where(key_row <= query_row, scores, masked_score)
        s_ref[rows, :] = scores
        here = jnp.max(scores.reshape(tokens // 8, 8, tokens), axis=0)
        top = here if top is None else jnp.maximum(top, here)
    top = jnp.max(top, axis=0, keepdims=True)
    total = jnp.zeros((8, tokens), jnp.float32)
    for block in range(low, len(keys)):
        grad_probs = mm(values[block][:, key_column], grad, NT)
        for at in range(0, tokens, CHUNK):
            rows = slice(block * tokens + at, block * tokens + at + CHUNK)
            weights = jnp.exp((s_ref[rows, :] - top) * score_scale)
            total = total + jnp.sum(weights.reshape(CHUNK // 8, 8, tokens), axis=0)
            e_ref[rows, :] = weights.astype(jnp.bfloat16)
            ds_ref[rows, :] = (weights * (grad_probs[at : at + CHUNK, :] - term)).astype(jnp.bfloat16)
    inv_ref[...] = 1.0 / jnp.sum(total, axis=0, keepdims=True)


def add_gradients(head, valid, low, high, rank, q_ref, do_ref, down, up_q, wk, dk_acc, dv_acc, slot):
    tokens = q_ref.shape[0]
    _, e_ref, ds_ref, inv_ref = slot
    (_, group, inner), column, _ = head
    height = wk.shape[1]
    inverse = inv_ref[...] * valid
    inverse_rows = jnp.broadcast_to(inverse, (HEAD_SIZE, tokens)).T
    scaled = inverse_rows * score_scale
    lane = lax.broadcasted_iota(jnp.int32, (tokens, HEAD_SIZE), 1) // rank
    own_columns = jnp.where(lane == inner, down[...].astype(jnp.float32), 0.0)
    grad_n = (do_ref[:, column].astype(jnp.float32) * inverse_rows).astype(jnp.bfloat16)
    query_n = jnp.concatenate(
        [q_ref[:, column].astype(jnp.float32) * scaled, own_columns * scaled], axis=1
    ).astype(jnp.bfloat16)
    rows = pl.ds(pl.multiple_of(group * height + low, tokens), high - low)
    dv_acc[rows, :] += mm(e_ref[low:high, :], grad_n)
    dk_acc[rows, :] += mm(ds_ref[low:high, :], query_n)
    own = pl.ds(pl.multiple_of(group * HEAD_SIZE + inner * rank, rank), rank)
    up_q[...] += mm(wk[own, low:high], ds_ref[low:high, :]) * (inverse * score_scale)


def all_heads(
    with_previous, per_kv, rank, flags, keys, values, q_hbm, do_hbm, term, w_q, down, up_q, dk, dv, scratch
):
    listed, q, do, q_sem, do_sem, wk, *buffers = scratch
    tokens, width = q.shape
    groups = width // (per_kv * HEAD_SIZE)
    loads = []
    for g in range(groups):
        part = slice(g * per_kv * HEAD_SIZE, (g + 1) * per_kv * HEAD_SIZE)
        loads.append(
            [
                pltpu.make_async_copy(q_hbm.at[:, part], q.at[:, part], q_sem.at[g]),
                pltpu.make_async_copy(do_hbm.at[:, part], do.at[:, part], do_sem.at[g]),
            ]
        )
    for load in sum(loads, []):
        load.start()

    def wait(group):
        for load in loads[group]:
            load.wait()

    def wait_between(held, wanted):
        for g in range(1, groups):
            pl.when((g > held) & (g <= wanted))(functools.partial(wait, g))
        return jnp.maximum(held, wanted)

    height = wk.shape[1]
    for g in range(groups):
        stacked = jnp.concatenate(
            [w_q[:, h * HEAD_SIZE : (h + 1) * HEAD_SIZE] for h in range(g * per_kv, (g + 1) * per_kv)], axis=0
        )
        for block, key in enumerate(keys):
            wk[g * HEAD_SIZE : (g + 1) * HEAD_SIZE, block * tokens : (block + 1) * tokens] = mm(
                stacked, key[:, g * HEAD_SIZE : (g + 1) * HEAD_SIZE], NT
            ).astype(jnp.bfloat16)
    dk[...] = jnp.zeros_like(dk)
    dv[...] = jnp.zeros_like(dv)
    slots = (buffers[:4], buffers[4:])
    for _, e_ref, ds_ref, inv_ref in slots:
        e_ref[...] = jnp.zeros_like(e_ref)
        ds_ref[...] = jnp.zeros_like(ds_ref)
        inv_ref[...] = jnp.zeros_like(inv_ref)
    wait(0)
    index = lax.axis_index("seq")
    core = index % 2
    half = index // 2 % 2
    count = jnp.int32(0)
    for h in range(groups * per_kv):
        listed[count] = jnp.int32(h)
        needs = flags[h] != half
        count = count + jnp.where(needs == with_previous, 1, 0).astype(jnp.int32)

    def head_at(i):
        h = listed[jnp.clip(i, 0, count - 1)]
        group = h // per_kv
        return (
            (h, group, h - group * per_kv),
            pl.ds(pl.multiple_of(h * HEAD_SIZE, HEAD_SIZE), HEAD_SIZE),
            pl.ds(pl.multiple_of(group * HEAD_SIZE, HEAD_SIZE), HEAD_SIZE),
        )

    for which in range(2):
        low = 1 - which

        def softmax(i, slot):
            scores_and_softmax(head_at(i), low, 1, keys, values, q, do, term, slot)

        def gradients(i, slot):
            valid = jnp.where((i >= 0) & (i < count), 1.0, 0.0).astype(jnp.float32)
            add_gradients(
                head_at(i), valid, low * tokens, height, rank, q, do, down, up_q, wk, dk, dv, slot
            )

        @pl.when((core == which) & (count > 0))
        def _():
            def two(t, held):
                held = wait_between(held, head_at(2 * t + 1)[0][1])
                softmax(2 * t, slots[0])
                gradients(2 * t - 1, slots[1])
                softmax(2 * t + 1, slots[1])
                gradients(2 * t, slots[0])
                return held

            held = lax.fori_loop(0, (count + 1) // 2, two, jnp.int32(0))
            wait_between(held, jnp.int32(groups - 1))

            @pl.when(count % 2 == 0)
            def _():
                gradients(count - 1, slots[1])

    @pl.when(count == 0)
    def _():
        wait_between(jnp.int32(0), jnp.int32(groups - 1))


def own_kernel(
    per_kv, rank, flags, q, do, term, w_q, down, kv_own, kv_sib, up_q, dk, dv, *scratch
):
    up_q[...] = jnp.zeros_like(up_q)
    keys, values = ([kv.at[c] for kv in (kv_sib, kv_own)] for c in range(2))
    all_heads(False, per_kv, rank, flags, keys, values, q, do, term, w_q, down, up_q, dk, dv, scratch)


def previous_kernel(
    scale, per_kv, rank, flags, q, do, term, w_q, down, kv_own, kv_sib, kv_pc, kv_px,
    up_q_own, dk_own, dv_own, w_kv, down_win,
    keep_own, keep_pc, send, up_q, up_keep, up_send, grad_up,
    dk, dv, grads, *scratch,
):
    tokens = q.shape[0]
    up_q[...] = up_q_own[...]
    keys, values = ([kv.at[c] for kv in (kv_sib, kv_own, kv_pc, kv_px)] for c in range(2))
    all_heads(True, per_kv, rank, flags, keys, values, q, do, term, w_q, down, up_q, dk, dv, scratch)
    up_kv = [jnp.zeros((rank, 4 * tokens), jnp.float32) for _ in range(2)]
    kv_width = kv_own.shape[2]
    for g in range(kv_width // HEAD_SIZE):
        columns = slice(g * HEAD_SIZE, (g + 1) * HEAD_SIZE)
        low_row, own_row = g * 4 * tokens, g * 2 * tokens
        by_head = None
        for block in range(4):
            tail = dk[low_row + block * tokens : low_row + (block + 1) * tokens, HEAD_SIZE:]
            if block < 2:
                tail = tail + dk_own[own_row + block * tokens : own_row + (block + 1) * tokens, HEAD_SIZE:]
            part = mm(tail.astype(jnp.bfloat16).T, keys[block][:, columns])
            by_head = part if by_head is None else by_head + part
        for h in range(per_kv):
            at = (g * per_kv + h) * HEAD_SIZE
            grads[:rank, at : at + HEAD_SIZE] = by_head[h * rank : (h + 1) * rank, :]
        for c, acc, start in ((0, dk, dk_own), (1, dv, dv_own)):
            total = acc[low_row : low_row + 4 * tokens, :HEAD_SIZE]
            near = total[: 2 * tokens] + start[own_row : own_row + 2 * tokens, :HEAD_SIZE]
            low = jnp.concatenate([near, total[2 * tokens :]]).astype(jnp.bfloat16)
            keep_own[c, :, columns] = near[tokens:]
            keep_pc[c, :, columns] = total[2 * tokens : 3 * tokens]
            send[0, c, :, columns] = low[:tokens]
            send[1, c, :, columns] = low[3 * tokens :]
            up_kv[c] = up_kv[c] + mm(w_kv[c, :, columns], low, NT)
            own = slice(c * rank, (c + 1) * rank)
            grad_kv = mm(down_win[own, :], low)
            for r in range(rank):
                row, at = divmod((c * rank + r) * kv_width + g * HEAD_SIZE, grads.shape[1])
                grads[rank + row : rank + row + 1, at : at + HEAD_SIZE] = grad_kv[r : r + 1, :]
    sib, near, pc, px = (
        jnp.concatenate([up_kv[c][:, block * tokens : (block + 1) * tokens] for c in range(2)])
        for block in range(4)
    )
    grad_up[...] = (grads[...] * scale).astype(jnp.bfloat16)
    up_keep[...] = jnp.concatenate([near, pc])
    up_send[...] = jnp.concatenate([sib, px]).astype(jnp.bfloat16)


def attention(scale, flags, queries, grads, terms, w_q, down, kv_own, kv_sib):
    tokens, width = queries.shape
    kv_width = kv_own.shape[2]
    kv_local = kv_width // HEAD_SIZE
    per_kv = width // kv_width
    rank = w_q.shape[0]
    assert per_kv * rank == HEAD_SIZE
    f32, bf16 = jnp.float32, jnp.bfloat16
    shape = jax.ShapeDtypeStruct
    pairs = kv_local * per_kv * tokens * tokens
    smem = pl.BlockSpec(memory_space=pltpu.SMEM)
    vmem = pl.BlockSpec(memory_space=pltpu.VMEM)
    hbm = pl.BlockSpec(memory_space=pltpu.HBM)

    def scratch(blocks):
        rows = blocks * tokens
        slot = [
            pltpu.VMEM((rows, tokens), f32),
            pltpu.VMEM((rows, tokens), bf16),
            pltpu.VMEM((rows, tokens), bf16),
            pltpu.VMEM((1, tokens), f32),
        ]
        return [
            pltpu.SMEM((kv_local * per_kv + 1,), jnp.int32),
            pltpu.VMEM((tokens, width), bf16),
            pltpu.VMEM((tokens, width), bf16),
            pltpu.SemaphoreType.DMA((kv_local,)),
            pltpu.SemaphoreType.DMA((kv_local,)),
            pltpu.VMEM((kv_local * HEAD_SIZE, rows), bf16),
        ] + slot * 2

    def call(kernel, out_shape, scratch_shapes, work, name, *args):
        return pl.pallas_call(
            functools.partial(kernel, per_kv, rank),
            in_specs=[smem, hbm, hbm] + [vmem] * (len(args) - 3),
            out_specs=[vmem] * len(out_shape),
            out_shape=out_shape,
            scratch_shapes=scratch_shapes,
            compiler_params=pltpu.CompilerParams(vmem_limit_bytes=VMEM_LIMIT),
            cost_estimate=pl.CostEstimate(
                flops=work * pairs * HEAD_SIZE, bytes_accessed=6 * tokens * width, transcendentals=pairs
            ),
            name=name,
        )(*args)

    queries, grads = (pltpu.with_memory_space_constraint(a, pltpu.HBM) for a in (queries, grads))
    common = (flags, queries, grads, terms, w_q, down, kv_own, kv_sib)

    def own():
        return call(
            own_kernel,
            [
                shape((rank, tokens), f32),
                shape((2 * tokens * kv_local, 2 * HEAD_SIZE), f32),
                shape((2 * tokens * kv_local, HEAD_SIZE), f32),
            ],
            scratch(2),
            40,
            "own_chip_heads",
            *common,
        )

    def previous(kv_pc, kv_px, own_grads, w_kv, down_win):
        grad_rows = rank + 2 * rank * kv_width // width
        return call(
            functools.partial(previous_kernel, scale),
            [
                shape((2, tokens, kv_width), f32),
                shape((2, tokens, kv_width), f32),
                shape((2, 2, tokens, kv_width), bf16),
                shape((rank, tokens), f32),
                shape((4 * rank, tokens), f32),
                shape((4 * rank, tokens), bf16),
                shape((grad_rows, width), bf16),
            ],
            [
                pltpu.VMEM((4 * tokens * kv_local, 2 * HEAD_SIZE), f32),
                pltpu.VMEM((4 * tokens * kv_local, HEAD_SIZE), f32),
                pltpu.VMEM((grad_rows, width), f32),
            ]
            + scratch(4),
            80,
            "previous_chip_heads",
            *common,
            kv_pc,
            kv_px,
            *own_grads,
            w_kv,
            down_win,
        )

    return own, previous


def exchanged(value, axis, bit):
    return lax.ppermute(value, axis, [(i, i ^ bit) for i in range(lax.axis_size(axis))])


def moved(value, axis, by):
    count = lax.axis_size(axis)
    return lax.ppermute(value, axis, [(i, (i + by) % count) for i in range(count)])


def summed(value, axis):
    bit = 1
    while bit < lax.axis_size(axis):
        value = value + exchanged(value, axis, bit)
        bit *= 2
    return value


def small_call(kernel, out_shape, *args, scratch=(), limit=1):
    vmem = pl.BlockSpec(memory_space=pltpu.VMEM)
    return pl.pallas_call(
        kernel,
        in_specs=[vmem] * len(args),
        out_specs=[vmem] * len(out_shape),
        out_shape=out_shape,
        scratch_shapes=list(scratch),
        compiler_params=pltpu.CompilerParams(vmem_limit_bytes=limit * SMALL_VMEM),
    )(*args)


def place(unit, radix):
    return lax.axis_index("seq") // unit % radix


def lanes(index, wide):
    return pl.ds(pl.multiple_of(index * wide, HEAD_SIZE), wide)


def projected_and_stacked(down_weight, inputs, key_rows, value_rows):
    rows, width = down_weight.shape
    tokens, kv_width = key_rows.shape
    steps = kv_width // HEAD_SIZE
    args = [
        pltpu.with_memory_space_constraint(a, pltpu.HBM)
        for a in (down_weight, inputs, key_rows, value_rows)
    ]

    def kernel(weight, tokens_in, key, value, down, kv):
        part = mm(weight[...], tokens_in[...], NT)

        @pl.when(pl.program_id(0) == 0)
        def _():
            down[...] = part

        @pl.when(pl.program_id(0) > 0)
        def _():
            down[...] += part

        kv[0] = key[...]
        kv[1] = value[...]

    def columns(high, wide):
        return pl.BlockSpec((high, wide // steps), lambda g: (0, g))

    return pl.pallas_call(
        kernel,
        grid=(steps,),
        in_specs=[
            columns(rows, width),
            columns(tokens, width),
            columns(tokens, kv_width),
            columns(tokens, kv_width),
        ],
        out_specs=[
            pl.BlockSpec((rows, tokens), lambda g: (0, 0)),
            pl.BlockSpec((2, tokens, kv_width // steps), lambda g: (0, 0, g)),
        ],
        out_shape=[
            jax.ShapeDtypeStruct((rows, tokens), jnp.float32),
            jax.ShapeDtypeStruct((2, tokens, kv_width), jnp.bfloat16),
        ],
        compiler_params=pltpu.CompilerParams(
            dimension_semantics=("arbitrary",), vmem_limit_bytes=2 * SMALL_VMEM
        ),
    )(*args)


def up_sums(up_q, up_keep, received):
    rank, tokens = up_q.shape

    def kernel(up_q, keep, other, mine, to_send, previous):
        total = keep[...] + other[...].astype(jnp.float32)
        own = jnp.concatenate([up_q[...], total[: 2 * rank]])
        mine[...] = own
        to_send[...] = own.astype(jnp.bfloat16)
        previous[...] = total[2 * rank :].astype(jnp.bfloat16)

    shape = jax.ShapeDtypeStruct
    return small_call(
        kernel,
        [
            shape((3 * rank, tokens), jnp.float32),
            shape((3 * rank, tokens), jnp.bfloat16),
            shape((2 * rank, tokens), jnp.bfloat16),
        ],
        up_q,
        up_keep,
        received,
    )


def up_terms(mine, to_send, previous):
    heads, count = lax.axis_size("head"), lax.axis_size("seq")
    nearby = moved(previous, "seq", -2)
    if heads == 2:
        pairs = [
            (s * heads + h, (s - 2) % count * heads + 1 - h) for s in range(count) for h in range(heads)
        ]
        return [mine, exchanged(to_send, "head", 1), nearby, lax.ppermute(previous, ("seq", "head"), pairs)]
    rank = mine.shape[0] - previous.shape[0]
    total = jnp.concatenate([mine[:rank], mine[rank:] + nearby.astype(jnp.float32)])
    bit = 1
    while 2 * bit < heads:
        total = total + exchanged(total.astype(jnp.bfloat16), "head", bit).astype(jnp.float32)
        bit *= 2
    return [total, exchanged(total.astype(jnp.bfloat16), "head", bit)]


def weight_halves(terms, inputs, grad_up, scale):
    width = inputs.shape[1]
    wide = width // 2
    up_rows, tokens = terms[0].shape
    rows = up_rows + grad_up.shape[0]
    given = len(terms)

    def kernel(*refs):
        tokens_in, grads, up_low, *out = refs[given:]
        up = jnp.zeros((up_rows, tokens), jnp.float32)
        for term in refs[:given]:
            value = term[...].astype(jnp.float32)
            if value.shape[0] < up_rows:
                value = jnp.concatenate(
                    [jnp.zeros((up_rows - value.shape[0], tokens), jnp.float32), value]
                )
            up = up + value
        up = up.astype(jnp.bfloat16)
        up_low[...] = up
        for d in range(2):
            at = lanes(place(1, 2) ^ d, wide)
            out[d][...] = jnp.concatenate(
                [mm(up, tokens_in[:, at]) * scale, grads[:, at].astype(jnp.float32)]
            ).astype(jnp.bfloat16)

    shape = jax.ShapeDtypeStruct
    return small_call(
        kernel,
        [shape((up_rows, tokens), jnp.bfloat16)] + [shape((rows, wide), jnp.bfloat16)] * 2,
        *terms,
        inputs,
        grad_up,
        limit=2,
    )


def exchanged_pieces(pieces, unit):
    return [pieces[0]] + [exchanged(p, "seq", d * unit) for d, p in enumerate(pieces) if d]


def summed_and_cut(pieces, unit, radix):
    rows, whole = pieces[0].shape
    wide = whole // radix
    if wide % HEAD_SIZE:
        total = sum(p.astype(jnp.float32) for p in pieces).astype(jnp.bfloat16)
        return [
            lax.dynamic_slice_in_dim(total, (place(unit, radix) ^ d) * wide, wide, 1)
            for d in range(radix)
        ]
    given = len(pieces)

    def kernel(*refs):
        total = refs[-1]
        total[...] = sum(p[...].astype(jnp.float32) for p in refs[:given])
        for d in range(radix):
            refs[given + d][...] = total[:, lanes(place(unit, radix) ^ d, wide)].astype(jnp.bfloat16)

    return small_call(
        kernel,
        [jax.ShapeDtypeStruct((rows, wide), jnp.bfloat16)] * radix,
        *pieces,
        scratch=[pltpu.VMEM((rows, whole), jnp.float32)],
    )


def joined(pieces, unit):
    rows, wide = pieces[0].shape
    radix = len(pieces)
    if wide % HEAD_SIZE:
        whole = jnp.zeros((rows, radix * wide), jnp.bfloat16)
        for d in range(radix):
            whole = lax.dynamic_update_slice_in_dim(
                whole, pieces[d], (place(unit, radix) ^ d) * wide, 1
            )
        return whole

    def kernel(*refs):
        for d in range(radix):
            refs[radix][:, lanes(place(unit, radix) ^ d, wide)] = refs[d][...]

    return small_call(kernel, [jax.ShapeDtypeStruct((rows, radix * wide), jnp.bfloat16)], *pieces)[0]


def joined_outputs(pieces, rank, kv_shape):
    rows, wide = pieces[0].shape
    extra = rows - 4 * rank
    each = wide // kv_shape[1]
    per_row = kv_shape[0] // extra

    def kernel(one, two, down, up_q, up_kv):
        for d, half in enumerate((one, two)):
            at = place(1, 2) ^ d
            piece = half[...].astype(jnp.float32)
            down[:, lanes(at, wide)] = piece[: 3 * rank]
            up_q[:, lanes(at, wide)] = piece[3 * rank : 4 * rank]
            for i in range(extra):
                for b in range(each):
                    up_kv[pl.ds(per_row * i + each * at + b, 1), :] = piece[
                        4 * rank + i : 4 * rank + i + 1, b * kv_shape[1] : (b + 1) * kv_shape[1]
                    ]

    shape = jax.ShapeDtypeStruct
    return small_call(
        kernel,
        [
            shape((3 * rank, 2 * wide), jnp.float32),
            shape((rank, 2 * wide), jnp.float32),
            shape(kv_shape, jnp.float32),
        ],
        *pieces,
    )


def per_device(
    queries,
    layer_key_rows,
    layer_value_rows,
    output_gradient,
    output_row_sums,
    shifted_head_flags,
    inputs,
    adapter_down_weight,
    query_up_weight,
    key_value_up_weight,
):
    seq_count = lax.axis_size("seq")
    tokens, width = queries.shape
    kv_width = layer_key_rows.shape[1]
    whole_len = tokens * seq_count
    rank = adapter_down_weight.shape[1]
    assert GROUP == 4 * tokens and SHIFT == 2 * tokens
    levels = (seq_count.bit_length() - 1) // 2
    assert 4**levels == seq_count
    flattened_down = adapter_down_weight.reshape(3 * rank, width)
    scale = adapter_scale / math.sqrt(whole_len)
    down_part, kv_own = projected_and_stacked(flattened_down, inputs, layer_key_rows, layer_value_rows)
    kv_pc = moved(kv_own, "seq", 2)
    kv_sib = exchanged(kv_own, "seq", 1)

    down_low = summed(down_part, "head").astype(jnp.bfloat16)
    down_tiled = jnp.tile(down_low[:rank].T, (1, HEAD_SIZE // rank))
    down_own = down_low[rank:]
    down_pc = moved(down_own, "seq", 2)

    own, previous = attention(
        scale,
        shifted_head_flags,
        queries,
        output_gradient,
        output_row_sums,
        query_up_weight,
        down_tiled,
        kv_own,
        kv_sib,
    )
    own_grads, kv_pc, down_pc = lax.optimization_barrier((own(), kv_pc, down_pc))
    kv_px = exchanged(kv_pc, "seq", 1)
    down_others = exchanged(jnp.concatenate([down_own, down_pc]), "seq", 1)
    down_win = jnp.concatenate(
        [down_others[: 2 * rank], down_own, down_pc, down_others[2 * rank :]], axis=1
    )
    keep_own, keep_pc, send, up_q, up_keep, up_send, grad_up = previous(
        kv_pc, kv_px, own_grads, key_value_up_weight, down_win
    )

    up_received, send = lax.optimization_barrier((exchanged(up_send, "seq", 1), send))
    received = exchanged(send, "seq", 1)
    terms = up_terms(*up_sums(up_q, up_keep, up_received))
    back_k, back_v = (
        (keep_pc[c] + received[1, c].astype(jnp.float32)).astype(jnp.bfloat16) for c in range(2)
    )
    terms[1], back_k = lax.optimization_barrier((terms[1], back_k))
    back_k = moved(back_k, "seq", -2)
    up_low, *pieces = weight_halves(terms, inputs, grad_up, scale)
    pieces = exchanged_pieces(summed_and_cut(exchanged_pieces(pieces, 1), 2, 2), 2)
    pieces, back_k, back_v = lax.optimization_barrier((pieces, back_k, back_v))
    back_v = moved(back_v, "seq", -2)
    for level in range(1, levels):
        pieces = exchanged_pieces(summed_and_cut(pieces, 4**level, 4), 4**level)
    total = sum(p.astype(jnp.float32) for p in pieces).astype(jnp.bfloat16)
    total, back_v = lax.optimization_barrier((total, back_v))
    key_value_gradient = jnp.stack(
        [
            (keep_own[c] + received[0, c].astype(jnp.float32) + back.astype(jnp.float32)).astype(jnp.bfloat16)
            for c, back in enumerate((back_k, back_v))
        ]
    )
    grad_inputs = (
        adapter_scale
        * lax.dot_general(
            up_low, flattened_down, (((0,), (0,)), ((), ())), preferred_element_type=jnp.float32
        )
    ).astype(jnp.bfloat16)
    for level in range(levels - 1, 0, -1):
        total = joined(exchanged_pieces([total] * 4, 4**level), 4**level)
    total, grad_inputs = lax.optimization_barrier((total, grad_inputs))
    total = joined(exchanged_pieces([total] * 2, 2), 2)
    total, key_value_gradient = lax.optimization_barrier((total, key_value_gradient))
    down_gradient, grad_up_q, grad_up_kv = joined_outputs(
        exchanged_pieces([total] * 2, 1), rank, (2 * rank, kv_width)
    )
    return (
        grad_inputs,
        key_value_gradient,
        down_gradient.reshape(3, rank, width),
        grad_up_q,
        grad_up_kv.reshape(2, rank, kv_width),
    )


def solution(mesh):
    placed = (
        P("seq", "head"),
        P("seq", "head"),
        P("seq", "head"),
        P("seq", "head"),
        P("head", "seq"),
        P("head"),
        P("seq", "head"),
        P(None, None, "head"),
        P(None, "head"),
        P(None, None, "head"),
    )
    return jax.shard_map(
        per_device,
        mesh=mesh,
        in_specs=placed,
        out_specs=(
            P("seq", "head"),
            P(None, "seq", "head"),
            P(None, None, "head"),
            P(None, "head"),
            P(None, None, "head"),
        ),
        check_vma=False,
    )
```

```python
import functools
import math

import jax
import jax.numpy as jnp
from jax import lax
from jax.experimental import pallas as pl
from jax.experimental.pallas import tpu as pltpu
from jax.sharding import PartitionSpec as P

HEAD_SIZE = 128
GROUP = 1024
SHIFT = 512
CHUNK = 32
SMALL_VMEM = 8 * 1024 * 1024
VMEM_LIMIT = 32 * 1024 * 1024

adapter_scale = 2.0
masked_score = -1e30
score_scale = HEAD_SIZE ** (-0.5)
exp2_scale = score_scale * math.log2(math.e)

NT = (((1,), (1,)), ((), ()))
NN = (((1,), (0,)), ((), ()))


def mm(left, right, dims=NN):
    return lax.dot_general(left, right, dims, preferred_element_type=jnp.float32)


def scores_and_softmax(head, low, diag, keys, values, q_ref, do_ref, term_ref, slot):
    tokens = q_ref.shape[0]
    s_ref, e_ref, ds_ref, inv_ref = slot
    group, column, key_column = head
    query = q_ref[:, column]
    grad = do_ref[:, column]
    term = term_ref[pl.ds(group[0], 1), :]
    top = None
    for block in range(low, len(keys)):
        rows = slice(block * tokens, (block + 1) * tokens)
        scores = mm(keys[block][:, key_column], query, NT)
        if block == diag:
            key_row = lax.broadcasted_iota(jnp.int32, (tokens, tokens), 0)
            query_row = lax.broadcasted_iota(jnp.int32, (tokens, tokens), 1)
            scores = jnp.where(key_row <= query_row, scores, masked_score)
        s_ref[rows, :] = scores
        here = jnp.max(scores.reshape(tokens // 8, 8, tokens), axis=0)
        top = here if top is None else jnp.maximum(top, here)
    top = jnp.max(top, axis=0, keepdims=True)
    total = jnp.zeros((8, tokens), jnp.float32)
    for block in range(low, len(keys)):
        grad_probs = mm(values[block][:, key_column], grad, NT)
        for at in range(0, tokens, CHUNK):
            rows = slice(block * tokens + at, block * tokens + at + CHUNK)
            weights = jnp.exp2((s_ref[rows, :] - top) * exp2_scale)
            total = total + jnp.sum(weights.reshape(CHUNK // 8, 8, tokens), axis=0)
            e_ref[rows, :] = weights.astype(jnp.bfloat16)
            ds_ref[rows, :] = (weights * (grad_probs[at : at + CHUNK, :] - term)).astype(jnp.bfloat16)
    inv_ref[...] = 1.0 / jnp.sum(total, axis=0, keepdims=True)


def add_gradients(head, valid, low, high, rank, q_ref, do_ref, down, up_q, wk, dk_acc, dv_acc, slot):
    tokens = q_ref.shape[0]
    _, e_ref, ds_ref, inv_ref = slot
    (_, group, inner), column, _ = head
    height = wk.shape[1]
    inverse = inv_ref[...] * valid
    inverse_rows = jnp.broadcast_to(inverse, (HEAD_SIZE, tokens)).T
    scaled = inverse_rows * score_scale
    lane = lax.broadcasted_iota(jnp.int32, (tokens, HEAD_SIZE), 1) // rank
    own_columns = jnp.where(lane == inner, down[...].astype(jnp.float32), 0.0)
    grad_n = (do_ref[:, column].astype(jnp.float32) * inverse_rows).astype(jnp.bfloat16)
    query_n = jnp.concatenate(
        [q_ref[:, column].astype(jnp.float32) * scaled, own_columns * scaled], axis=1
    ).astype(jnp.bfloat16)
    rows = pl.ds(pl.multiple_of(group * height + low, tokens), high - low)
    dv_acc[rows, :] += mm(e_ref[low:high, :], grad_n)
    dk_acc[rows, :] += mm(ds_ref[low:high, :], query_n)
    own = pl.ds(pl.multiple_of(group * HEAD_SIZE + inner * rank, rank), rank)
    up_q[...] += mm(wk[own, low:high], ds_ref[low:high, :]) * (inverse * score_scale)


def all_heads(
    with_previous, per_kv, rank, flags, keys, values, q_hbm, do_hbm, term, w_q, down, up_q, dk, dv, scratch
):
    listed, q, do, q_sem, do_sem, wk, *buffers = scratch
    tokens, width = q.shape
    groups = width // (per_kv * HEAD_SIZE)
    loads = []
    for g in range(groups):
        part = slice(g * per_kv * HEAD_SIZE, (g + 1) * per_kv * HEAD_SIZE)
        loads.append(
            [
                pltpu.make_async_copy(q_hbm.at[:, part], q.at[:, part], q_sem.at[g]),
                pltpu.make_async_copy(do_hbm.at[:, part], do.at[:, part], do_sem.at[g]),
            ]
        )
    for load in sum(loads, []):
        load.start()

    def wait(group):
        for load in loads[group]:
            load.wait()

    def wait_between(held, wanted):
        for g in range(1, groups):
            pl.when((g > held) & (g <= wanted))(functools.partial(wait, g))
        return jnp.maximum(held, wanted)

    height = wk.shape[1]
    for g in range(groups):
        stacked = jnp.concatenate(
            [w_q[:, h * HEAD_SIZE : (h + 1) * HEAD_SIZE] for h in range(g * per_kv, (g + 1) * per_kv)], axis=0
        )
        for block, key in enumerate(keys):
            wk[g * HEAD_SIZE : (g + 1) * HEAD_SIZE, block * tokens : (block + 1) * tokens] = mm(
                stacked, key[:, g * HEAD_SIZE : (g + 1) * HEAD_SIZE], NT
            ).astype(jnp.bfloat16)
    dk[...] = jnp.zeros_like(dk)
    dv[...] = jnp.zeros_like(dv)
    slots = (buffers[:4], buffers[4:])
    for _, e_ref, ds_ref, inv_ref in slots:
        e_ref[...] = jnp.zeros_like(e_ref)
        ds_ref[...] = jnp.zeros_like(ds_ref)
        inv_ref[...] = jnp.zeros_like(inv_ref)
    wait(0)
    index = lax.axis_index("seq")
    core = index % 2
    half = index // 2 % 2
    count = jnp.int32(0)
    for h in range(groups * per_kv):
        listed[count] = jnp.int32(h)
        needs = flags[h] != half
        count = count + jnp.where(needs == with_previous, 1, 0).astype(jnp.int32)

    def head_at(i):
        h = listed[jnp.clip(i, 0, count - 1)]
        group = h // per_kv
        return (
            (h, group, h - group * per_kv),
            pl.ds(pl.multiple_of(h * HEAD_SIZE, HEAD_SIZE), HEAD_SIZE),
            pl.ds(pl.multiple_of(group * HEAD_SIZE, HEAD_SIZE), HEAD_SIZE),
        )

    for which in range(2):
        low = 1 - which

        def softmax(i, slot):
            scores_and_softmax(head_at(i), low, 1, keys, values, q, do, term, slot)

        def gradients(i, slot):
            valid = jnp.where((i >= 0) & (i < count), 1.0, 0.0).astype(jnp.float32)
            add_gradients(
                head_at(i), valid, low * tokens, height, rank, q, do, down, up_q, wk, dk, dv, slot
            )

        @pl.when((core == which) & (count > 0))
        def _():
            def two(t, held):
                held = wait_between(held, head_at(2 * t + 1)[0][1])
                softmax(2 * t, slots[0])
                gradients(2 * t - 1, slots[1])
                softmax(2 * t + 1, slots[1])
                gradients(2 * t, slots[0])
                return held

            held = lax.fori_loop(0, (count + 1) // 2, two, jnp.int32(0))
            wait_between(held, jnp.int32(groups - 1))

            @pl.when(count % 2 == 0)
            def _():
                gradients(count - 1, slots[1])

    @pl.when(count == 0)
    def _():
        wait_between(jnp.int32(0), jnp.int32(groups - 1))


def own_kernel(
    per_kv, rank, flags, q, do, term, w_q, down, kv_own, kv_sib, up_q, dk, dv, *scratch
):
    up_q[...] = jnp.zeros_like(up_q)
    keys, values = ([kv.at[c] for kv in (kv_sib, kv_own)] for c in range(2))
    all_heads(False, per_kv, rank, flags, keys, values, q, do, term, w_q, down, up_q, dk, dv, scratch)


def previous_kernel(
    scale, per_kv, rank, flags, q, do, term, w_q, down, kv_own, kv_sib, kv_pc, kv_px,
    up_q_own, dk_own, dv_own, w_kv, down_win,
    keep_own, keep_pc, send, up_q, up_keep, up_send, grad_up,
    dk, dv, grads, *scratch,
):
    tokens = q.shape[0]
    up_q[...] = up_q_own[...]
    keys, values = ([kv.at[c] for kv in (kv_sib, kv_own, kv_pc, kv_px)] for c in range(2))
    all_heads(True, per_kv, rank, flags, keys, values, q, do, term, w_q, down, up_q, dk, dv, scratch)
    up_kv = [jnp.zeros((rank, 4 * tokens), jnp.float32) for _ in range(2)]
    kv_width = kv_own.shape[2]
    for g in range(kv_width // HEAD_SIZE):
        columns = slice(g * HEAD_SIZE, (g + 1) * HEAD_SIZE)
        low_row, own_row = g * 4 * tokens, g * 2 * tokens
        by_head = None
        for block in range(4):
            tail = dk[low_row + block * tokens : low_row + (block + 1) * tokens, HEAD_SIZE:]
            if block < 2:
                tail = tail + dk_own[own_row + block * tokens : own_row + (block + 1) * tokens, HEAD_SIZE:]
            part = mm(tail.T.astype(jnp.bfloat16), keys[block][:, columns])
            by_head = part if by_head is None else by_head + part
        for h in range(per_kv):
            at = (g * per_kv + h) * HEAD_SIZE
            grads[:rank, at : at + HEAD_SIZE] = by_head[h * rank : (h + 1) * rank, :]
        for c, acc, start in ((0, dk, dk_own), (1, dv, dv_own)):
            total = acc[low_row : low_row + 4 * tokens, :HEAD_SIZE]
            near = total[: 2 * tokens] + start[own_row : own_row + 2 * tokens, :HEAD_SIZE]
            low = jnp.concatenate([near, total[2 * tokens :]]).astype(jnp.bfloat16)
            keep_own[c, :, columns] = near[tokens:]
            keep_pc[c, :, columns] = total[2 * tokens : 3 * tokens]
            send[0, c, :, columns] = low[:tokens]
            send[1, c, :, columns] = low[3 * tokens :]
            up_kv[c] = up_kv[c] + mm(w_kv[c, :, columns], low, NT)
            own = slice(c * rank, (c + 1) * rank)
            grad_kv = mm(down_win[own, :], low)
            for r in range(rank):
                row, at = divmod((c * rank + r) * kv_width + g * HEAD_SIZE, grads.shape[1])
                grads[rank + row : rank + row + 1, at : at + HEAD_SIZE] = grad_kv[r : r + 1, :]
    sib, near, pc, px = (
        jnp.concatenate([up_kv[c][:, block * tokens : (block + 1) * tokens] for c in range(2)])
        for block in range(4)
    )
    grad_up[...] = (grads[...] * scale).astype(jnp.bfloat16)
    up_keep[...] = jnp.concatenate([near, pc])
    up_send[...] = jnp.concatenate([sib, px]).astype(jnp.bfloat16)


def attention(scale, flags, queries, grads, terms, w_q, down, kv_own, kv_sib):
    tokens, width = queries.shape
    kv_width = kv_own.shape[2]
    kv_local = kv_width // HEAD_SIZE
    per_kv = width // kv_width
    rank = w_q.shape[0]
    assert per_kv * rank == HEAD_SIZE
    f32, bf16 = jnp.float32, jnp.bfloat16
    shape = jax.ShapeDtypeStruct
    pairs = kv_local * per_kv * tokens * tokens
    smem = pl.BlockSpec(memory_space=pltpu.SMEM)
    vmem = pl.BlockSpec(memory_space=pltpu.VMEM)
    hbm = pl.BlockSpec(memory_space=pltpu.HBM)

    def scratch(blocks):
        rows = blocks * tokens
        slot = [
            pltpu.VMEM((rows, tokens), f32),
            pltpu.VMEM((rows, tokens), bf16),
            pltpu.VMEM((rows, tokens), bf16),
            pltpu.VMEM((1, tokens), f32),
        ]
        return [
            pltpu.SMEM((kv_local * per_kv + 1,), jnp.int32),
            pltpu.VMEM((tokens, width), bf16),
            pltpu.VMEM((tokens, width), bf16),
            pltpu.SemaphoreType.DMA((kv_local,)),
            pltpu.SemaphoreType.DMA((kv_local,)),
            pltpu.VMEM((kv_local * HEAD_SIZE, rows), bf16),
        ] + slot * 2

    def call(kernel, out_shape, scratch_shapes, work, name, *args):
        return pl.pallas_call(
            functools.partial(kernel, per_kv, rank),
            in_specs=[smem, hbm, hbm] + [vmem] * (len(args) - 3),
            out_specs=[vmem] * len(out_shape),
            out_shape=out_shape,
            scratch_shapes=scratch_shapes,
            compiler_params=pltpu.CompilerParams(vmem_limit_bytes=VMEM_LIMIT),
            cost_estimate=pl.CostEstimate(
                flops=work * pairs * HEAD_SIZE, bytes_accessed=6 * tokens * width, transcendentals=pairs
            ),
            name=name,
        )(*args)

    queries, grads = (pltpu.with_memory_space_constraint(a, pltpu.HBM) for a in (queries, grads))
    common = (flags, queries, grads, terms, w_q, down, kv_own, kv_sib)

    def own():
        return call(
            own_kernel,
            [
                shape((rank, tokens), f32),
                shape((2 * tokens * kv_local, 2 * HEAD_SIZE), f32),
                shape((2 * tokens * kv_local, HEAD_SIZE), f32),
            ],
            scratch(2),
            40,
            "own_chip_heads",
            *common,
        )

    def previous(kv_pc, kv_px, own_grads, w_kv, down_win):
        grad_rows = rank + 2 * rank * kv_width // width
        return call(
            functools.partial(previous_kernel, scale),
            [
                shape((2, tokens, kv_width), f32),
                shape((2, tokens, kv_width), f32),
                shape((2, 2, tokens, kv_width), bf16),
                shape((rank, tokens), f32),
                shape((4 * rank, tokens), f32),
                shape((4 * rank, tokens), bf16),
                shape((grad_rows, width), bf16),
            ],
            [
                pltpu.VMEM((4 * tokens * kv_local, 2 * HEAD_SIZE), f32),
                pltpu.VMEM((4 * tokens * kv_local, HEAD_SIZE), f32),
                pltpu.VMEM((grad_rows, width), f32),
            ]
            + scratch(4),
            80,
            "previous_chip_heads",
            *common,
            kv_pc,
            kv_px,
            *own_grads,
            w_kv,
            down_win,
        )

    return own, previous


def exchanged(value, axis, bit):
    return lax.ppermute(value, axis, [(i, i ^ bit) for i in range(lax.axis_size(axis))])


def moved(value, axis, by):
    count = lax.axis_size(axis)
    return lax.ppermute(value, axis, [(i, (i + by) % count) for i in range(count)])


def summed(value, axis):
    bit = 1
    while bit < lax.axis_size(axis):
        value = value + exchanged(value, axis, bit)
        bit *= 2
    return value


def small_call(kernel, out_shape, *args, scratch=(), limit=1):
    vmem = pl.BlockSpec(memory_space=pltpu.VMEM)
    return pl.pallas_call(
        kernel,
        in_specs=[vmem] * len(args),
        out_specs=[vmem] * len(out_shape),
        out_shape=out_shape,
        scratch_shapes=list(scratch),
        compiler_params=pltpu.CompilerParams(vmem_limit_bytes=limit * SMALL_VMEM),
    )(*args)


def place(unit, radix):
    return lax.axis_index("seq") // unit % radix


def lanes(index, wide):
    return pl.ds(pl.multiple_of(index * wide, HEAD_SIZE), wide)


def projected_and_stacked(down_weight, inputs, key_rows, value_rows):
    rows, width = down_weight.shape
    tokens, kv_width = key_rows.shape
    steps = kv_width // HEAD_SIZE
    args = [
        pltpu.with_memory_space_constraint(a, pltpu.HBM)
        for a in (down_weight, inputs, key_rows, value_rows)
    ]

    def kernel(weight, tokens_in, key, value, down, kv):
        part = mm(weight[...], tokens_in[...], NT)

        @pl.when(pl.program_id(0) == 0)
        def _():
            down[...] = part

        @pl.when(pl.program_id(0) > 0)
        def _():
            down[...] += part

        kv[0] = key[...]
        kv[1] = value[...]

    def columns(high, wide):
        return pl.BlockSpec((high, wide // steps), lambda g: (0, g))

    return pl.pallas_call(
        kernel,
        grid=(steps,),
        in_specs=[
            columns(rows, width),
            columns(tokens, width),
            columns(tokens, kv_width),
            columns(tokens, kv_width),
        ],
        out_specs=[
            pl.BlockSpec((rows, tokens), lambda g: (0, 0)),
            pl.BlockSpec((2, tokens, kv_width // steps), lambda g: (0, 0, g)),
        ],
        out_shape=[
            jax.ShapeDtypeStruct((rows, tokens), jnp.float32),
            jax.ShapeDtypeStruct((2, tokens, kv_width), jnp.bfloat16),
        ],
        compiler_params=pltpu.CompilerParams(
            dimension_semantics=("arbitrary",), vmem_limit_bytes=2 * SMALL_VMEM
        ),
    )(*args)


def up_sums(up_q, up_keep, received):
    rank, tokens = up_q.shape

    def kernel(up_q, keep, other, mine, to_send, previous):
        total = keep[...] + other[...].astype(jnp.float32)
        own = jnp.concatenate([up_q[...], total[: 2 * rank]])
        mine[...] = own
        to_send[...] = own.astype(jnp.bfloat16)
        previous[...] = total[2 * rank :].astype(jnp.bfloat16)

    shape = jax.ShapeDtypeStruct
    return small_call(
        kernel,
        [
            shape((3 * rank, tokens), jnp.float32),
            shape((3 * rank, tokens), jnp.bfloat16),
            shape((2 * rank, tokens), jnp.bfloat16),
        ],
        up_q,
        up_keep,
        received,
    )


def up_terms(mine, to_send, previous):
    heads, count = lax.axis_size("head"), lax.axis_size("seq")
    nearby = moved(previous, "seq", -2)
    if heads == 2:
        pairs = [
            (s * heads + h, (s - 2) % count * heads + 1 - h) for s in range(count) for h in range(heads)
        ]
        return [mine, exchanged(to_send, "head", 1), nearby, lax.ppermute(previous, ("seq", "head"), pairs)]
    rank = mine.shape[0] - previous.shape[0]
    total = jnp.concatenate([mine[:rank], mine[rank:] + nearby.astype(jnp.float32)])
    bit = 1
    while 2 * bit < heads:
        total = total + exchanged(total.astype(jnp.bfloat16), "head", bit).astype(jnp.float32)
        bit *= 2
    return [total, exchanged(total.astype(jnp.bfloat16), "head", bit)]


def weight_halves(terms, inputs, grad_up, scale):
    width = inputs.shape[1]
    wide = width // 2
    up_rows, tokens = terms[0].shape
    rows = up_rows + grad_up.shape[0]
    given = len(terms)

    def kernel(*refs):
        tokens_in, grads, up_low, *out = refs[given:]
        up = jnp.zeros((up_rows, tokens), jnp.float32)
        for term in refs[:given]:
            value = term[...].astype(jnp.float32)
            if value.shape[0] < up_rows:
                value = jnp.concatenate(
                    [jnp.zeros((up_rows - value.shape[0], tokens), jnp.float32), value]
                )
            up = up + value
        up = up.astype(jnp.bfloat16)
        up_low[...] = up
        for d in range(2):
            at = lanes(place(1, 2) ^ d, wide)
            out[d][...] = jnp.concatenate(
                [mm(up, tokens_in[:, at]) * scale, grads[:, at].astype(jnp.float32)]
            ).astype(jnp.bfloat16)

    shape = jax.ShapeDtypeStruct
    return small_call(
        kernel,
        [shape((up_rows, tokens), jnp.bfloat16)] + [shape((rows, wide), jnp.bfloat16)] * 2,
        *terms,
        inputs,
        grad_up,
        limit=2,
    )


def exchanged_pieces(pieces, unit):
    return [pieces[0]] + [exchanged(p, "seq", d * unit) for d, p in enumerate(pieces) if d]


def summed_and_cut(pieces, unit, radix):
    rows, whole = pieces[0].shape
    wide = whole // radix
    if wide % HEAD_SIZE:
        total = sum(p.astype(jnp.float32) for p in pieces).astype(jnp.bfloat16)
        return [
            lax.dynamic_slice_in_dim(total, (place(unit, radix) ^ d) * wide, wide, 1)
            for d in range(radix)
        ]
    given = len(pieces)

    def kernel(*refs):
        total = refs[-1]
        total[...] = sum(p[...].astype(jnp.float32) for p in refs[:given])
        for d in range(radix):
            refs[given + d][...] = total[:, lanes(place(unit, radix) ^ d, wide)].astype(jnp.bfloat16)

    return small_call(
        kernel,
        [jax.ShapeDtypeStruct((rows, wide), jnp.bfloat16)] * radix,
        *pieces,
        scratch=[pltpu.VMEM((rows, whole), jnp.float32)],
    )


def joined(pieces, unit):
    rows, wide = pieces[0].shape
    radix = len(pieces)
    if wide % HEAD_SIZE:
        whole = jnp.zeros((rows, radix * wide), jnp.bfloat16)
        for d in range(radix):
            whole = lax.dynamic_update_slice_in_dim(
                whole, pieces[d], (place(unit, radix) ^ d) * wide, 1
            )
        return whole

    def kernel(*refs):
        for d in range(radix):
            refs[radix][:, lanes(place(unit, radix) ^ d, wide)] = refs[d][...]

    return small_call(kernel, [jax.ShapeDtypeStruct((rows, radix * wide), jnp.bfloat16)], *pieces)[0]


def joined_outputs(pieces, rank, kv_shape):
    rows, wide = pieces[0].shape
    extra = rows - 4 * rank
    each = wide // kv_shape[1]
    per_row = kv_shape[0] // extra

    def kernel(one, two, down, up_q, up_kv):
        for d, half in enumerate((one, two)):
            at = place(1, 2) ^ d
            piece = half[...].astype(jnp.float32)
            down[:, lanes(at, wide)] = piece[: 3 * rank]
            up_q[:, lanes(at, wide)] = piece[3 * rank : 4 * rank]
            for i in range(extra):
                for b in range(each):
                    up_kv[pl.ds(per_row * i + each * at + b, 1), :] = piece[
                        4 * rank + i : 4 * rank + i + 1, b * kv_shape[1] : (b + 1) * kv_shape[1]
                    ]

    shape = jax.ShapeDtypeStruct
    return small_call(
        kernel,
        [
            shape((3 * rank, 2 * wide), jnp.float32),
            shape((rank, 2 * wide), jnp.float32),
            shape(kv_shape, jnp.float32),
        ],
        *pieces,
    )


def per_device(
    queries,
    layer_key_rows,
    layer_value_rows,
    output_gradient,
    output_row_sums,
    shifted_head_flags,
    inputs,
    adapter_down_weight,
    query_up_weight,
    key_value_up_weight,
):
    seq_count = lax.axis_size("seq")
    tokens, width = queries.shape
    kv_width = layer_key_rows.shape[1]
    whole_len = tokens * seq_count
    rank = adapter_down_weight.shape[1]
    assert GROUP == 4 * tokens and SHIFT == 2 * tokens
    levels = (seq_count.bit_length() - 1) // 2
    assert 4**levels == seq_count
    flattened_down = adapter_down_weight.reshape(3 * rank, width)
    scale = adapter_scale / math.sqrt(whole_len)
    down_part, kv_own = projected_and_stacked(flattened_down, inputs, layer_key_rows, layer_value_rows)
    kv_pc = moved(kv_own, "seq", 2)
    kv_sib = exchanged(kv_own, "seq", 1)

    down_low = summed(down_part, "head").astype(jnp.bfloat16)
    down_tiled = jnp.tile(down_low[:rank].T, (1, HEAD_SIZE // rank))
    down_own = down_low[rank:]
    down_pc = moved(down_own, "seq", 2)

    own, previous = attention(
        scale,
        shifted_head_flags,
        queries,
        output_gradient,
        output_row_sums,
        query_up_weight,
        down_tiled,
        kv_own,
        kv_sib,
    )
    own_grads, kv_pc, down_pc = lax.optimization_barrier((own(), kv_pc, down_pc))
    kv_px = exchanged(kv_pc, "seq", 1)
    down_others = exchanged(jnp.concatenate([down_own, down_pc]), "seq", 1)
    down_win = jnp.concatenate(
        [down_others[: 2 * rank], down_own, down_pc, down_others[2 * rank :]], axis=1
    )
    keep_own, keep_pc, send, up_q, up_keep, up_send, grad_up = previous(
        kv_pc, kv_px, own_grads, key_value_up_weight, down_win
    )

    up_received, send = lax.optimization_barrier((exchanged(up_send, "seq", 1), send))
    received = exchanged(send, "seq", 1)
    terms = up_terms(*up_sums(up_q, up_keep, up_received))
    back = (keep_pc + received[1].astype(jnp.float32)).astype(jnp.bfloat16)
    up_low, *pieces = weight_halves(terms, inputs, grad_up, scale)
    pieces = exchanged_pieces(summed_and_cut(exchanged_pieces(pieces, 1), 2, 2), 2)
    pieces, back = lax.optimization_barrier((pieces, back))
    back = moved(back, "seq", -2)
    for level in range(1, levels):
        pieces = exchanged_pieces(summed_and_cut(pieces, 4**level, 4), 4**level)
    total = sum(p.astype(jnp.float32) for p in pieces).astype(jnp.bfloat16)
    key_value_gradient = (
        keep_own + received[0].astype(jnp.float32) + back.astype(jnp.float32)
    ).astype(jnp.bfloat16)
    grad_inputs = (
        adapter_scale
        * lax.dot_general(
            up_low, flattened_down, (((0,), (0,)), ((), ())), preferred_element_type=jnp.float32
        )
    ).astype(jnp.bfloat16)
    for level in range(levels - 1, 0, -1):
        total = joined(exchanged_pieces([total] * 4, 4**level), 4**level)
    total, grad_inputs = lax.optimization_barrier((total, grad_inputs))
    total = joined(exchanged_pieces([total] * 2, 2), 2)
    total, key_value_gradient = lax.optimization_barrier((total, key_value_gradient))
    down_gradient, grad_up_q, grad_up_kv = joined_outputs(
        exchanged_pieces([total] * 2, 1), rank, (2 * rank, kv_width)
    )
    return (
        grad_inputs,
        key_value_gradient,
        down_gradient.reshape(3, rank, width),
        grad_up_q,
        grad_up_kv.reshape(2, rank, kv_width),
    )


def solution(mesh):
    placed = (
        P("seq", "head"),
        P("seq", "head"),
        P("seq", "head"),
        P("seq", "head"),
        P("head", "seq"),
        P("head"),
        P("seq", "head"),
        P(None, None, "head"),
        P(None, "head"),
        P(None, None, "head"),
    )
    return jax.shard_map(
        per_device,
        mesh=mesh,
        in_specs=placed,
        out_specs=(
            P("seq", "head"),
            P(None, "seq", "head"),
            P(None, None, "head"),
            P(None, "head"),
            P(None, None, "head"),
        ),
        check_vma=False,
    )
```

```python
import functools
import math

import jax
import jax.numpy as jnp
from jax import lax
from jax.experimental import pallas as pl
from jax.experimental.pallas import tpu as pltpu
from jax.sharding import PartitionSpec as P

HEAD_SIZE = 128
GROUP = 1024
SHIFT = 512
CHUNK = 32
SMALL_VMEM = 8 * 1024 * 1024
VMEM_LIMIT = 32 * 1024 * 1024

adapter_scale = 2.0
masked_score = -1e30
score_scale = HEAD_SIZE ** (-0.5)
exp2_scale = score_scale * math.log2(math.e)

NT = (((1,), (1,)), ((), ()))
NN = (((1,), (0,)), ((), ()))


def mm(left, right, dims=NN):
    return lax.dot_general(left, right, dims, preferred_element_type=jnp.float32)


def scores_and_softmax(head, low, diag, keys, values, q_ref, do_ref, term_ref, slot):
    tokens = q_ref.shape[0]
    s_ref, e_ref, ds_ref, inv_ref = slot
    group, column, key_column = head
    query = q_ref[:, column]
    grad = do_ref[:, column]
    term = term_ref[pl.ds(group[0], 1), :]
    top = None
    for block in range(low, len(keys)):
        rows = slice(block * tokens, (block + 1) * tokens)
        scores = mm(keys[block][:, key_column], query, NT)
        if block == diag:
            key_row = lax.broadcasted_iota(jnp.int32, (tokens, tokens), 0)
            query_row = lax.broadcasted_iota(jnp.int32, (tokens, tokens), 1)
            scores = jnp.where(key_row <= query_row, scores, masked_score)
        s_ref[rows, :] = scores
        here = jnp.max(scores.reshape(tokens // 8, 8, tokens), axis=0)
        top = here if top is None else jnp.maximum(top, here)
    top = jnp.max(top, axis=0, keepdims=True)
    total = jnp.zeros((8, tokens), jnp.float32)
    for block in range(low, len(keys)):
        grad_probs = mm(values[block][:, key_column], grad, NT)
        for at in range(0, tokens, CHUNK):
            rows = slice(block * tokens + at, block * tokens + at + CHUNK)
            weights = jnp.exp2((s_ref[rows, :] - top) * exp2_scale)
            total = total + jnp.sum(weights.reshape(CHUNK // 8, 8, tokens), axis=0)
            e_ref[rows, :] = weights.astype(jnp.bfloat16)
            ds_ref[rows, :] = (weights * (grad_probs[at : at + CHUNK, :] - term)).astype(jnp.bfloat16)
    inv_ref[...] = 1.0 / jnp.sum(total, axis=0, keepdims=True)


def add_gradients(head, valid, low, high, rank, q_ref, do_ref, down, up_q, wk, dk_acc, dv_acc, slot):
    tokens = q_ref.shape[0]
    _, e_ref, ds_ref, inv_ref = slot
    (_, group, inner), column, _ = head
    height = wk.shape[1]
    inverse = inv_ref[...] * valid
    inverse_rows = jnp.broadcast_to(inverse, (HEAD_SIZE, tokens)).T
    scaled = inverse_rows * score_scale
    lane = lax.broadcasted_iota(jnp.int32, (tokens, HEAD_SIZE), 1) // rank
    own_columns = jnp.where(lane == inner, down[...].astype(jnp.float32), 0.0)
    grad_n = (do_ref[:, column].astype(jnp.float32) * inverse_rows).astype(jnp.bfloat16)
    query_n = jnp.concatenate(
        [q_ref[:, column].astype(jnp.float32) * scaled, own_columns * scaled], axis=1
    ).astype(jnp.bfloat16)
    rows = pl.ds(pl.multiple_of(group * height + low, tokens), high - low)
    dv_acc[rows, :] += mm(e_ref[low:high, :], grad_n)
    dk_acc[rows, :] += mm(ds_ref[low:high, :], query_n)
    own = pl.ds(pl.multiple_of(group * HEAD_SIZE + inner * rank, rank), rank)
    up_q[...] += mm(wk[own, low:high], ds_ref[low:high, :]) * (inverse * score_scale)


def all_heads(
    with_previous, per_kv, rank, flags, keys, values, q_hbm, do_hbm, term, w_q, down, up_q, dk, dv, scratch
):
    listed, q, do, q_sem, do_sem, wk, *buffers = scratch
    tokens, width = q.shape
    groups = width // (per_kv * HEAD_SIZE)
    loads = []
    for g in range(groups):
        part = slice(g * per_kv * HEAD_SIZE, (g + 1) * per_kv * HEAD_SIZE)
        loads.append(
            [
                pltpu.make_async_copy(q_hbm.at[:, part], q.at[:, part], q_sem.at[g]),
                pltpu.make_async_copy(do_hbm.at[:, part], do.at[:, part], do_sem.at[g]),
            ]
        )
    for load in sum(loads, []):
        load.start()

    def wait(group):
        for load in loads[group]:
            load.wait()

    def wait_between(held, wanted):
        for g in range(1, groups):
            pl.when((g > held) & (g <= wanted))(functools.partial(wait, g))
        return jnp.maximum(held, wanted)

    height = wk.shape[1]
    for g in range(groups):
        stacked = jnp.concatenate(
            [w_q[:, h * HEAD_SIZE : (h + 1) * HEAD_SIZE] for h in range(g * per_kv, (g + 1) * per_kv)], axis=0
        )
        for block, key in enumerate(keys):
            wk[g * HEAD_SIZE : (g + 1) * HEAD_SIZE, block * tokens : (block + 1) * tokens] = mm(
                stacked, key[:, g * HEAD_SIZE : (g + 1) * HEAD_SIZE], NT
            ).astype(jnp.bfloat16)
    dk[...] = jnp.zeros_like(dk)
    dv[...] = jnp.zeros_like(dv)
    slots = (buffers[:4], buffers[4:])
    for _, e_ref, ds_ref, inv_ref in slots:
        e_ref[...] = jnp.zeros_like(e_ref)
        ds_ref[...] = jnp.zeros_like(ds_ref)
        inv_ref[...] = jnp.zeros_like(inv_ref)
    wait(0)
    index = lax.axis_index("seq")
    core = index % 2
    half = index // 2 % 2
    count = jnp.int32(0)
    for h in range(groups * per_kv):
        listed[count] = jnp.int32(h)
        needs = flags[h] != half
        count = count + jnp.where(needs == with_previous, 1, 0).astype(jnp.int32)

    def head_at(i):
        h = listed[jnp.clip(i, 0, count - 1)]
        group = h // per_kv
        return (
            (h, group, h - group * per_kv),
            pl.ds(pl.multiple_of(h * HEAD_SIZE, HEAD_SIZE), HEAD_SIZE),
            pl.ds(pl.multiple_of(group * HEAD_SIZE, HEAD_SIZE), HEAD_SIZE),
        )

    for which in range(2):
        low = 1 - which

        def softmax(i, slot):
            scores_and_softmax(head_at(i), low, 1, keys, values, q, do, term, slot)

        def gradients(i, slot):
            valid = jnp.where((i >= 0) & (i < count), 1.0, 0.0).astype(jnp.float32)
            add_gradients(
                head_at(i), valid, low * tokens, height, rank, q, do, down, up_q, wk, dk, dv, slot
            )

        @pl.when((core == which) & (count > 0))
        def _():
            def two(t, held):
                held = wait_between(held, head_at(2 * t + 1)[0][1])
                softmax(2 * t, slots[0])
                gradients(2 * t - 1, slots[1])
                softmax(2 * t + 1, slots[1])
                gradients(2 * t, slots[0])
                return held

            held = lax.fori_loop(0, (count + 1) // 2, two, jnp.int32(0))
            wait_between(held, jnp.int32(groups - 1))

            @pl.when(count % 2 == 0)
            def _():
                gradients(count - 1, slots[1])

    @pl.when(count == 0)
    def _():
        wait_between(jnp.int32(0), jnp.int32(groups - 1))


def own_kernel(
    per_kv, rank, flags, q, do, term, w_q, down, kv_own, kv_sib, up_q, dk, dv, *scratch
):
    up_q[...] = jnp.zeros_like(up_q)
    keys, values = ([kv.at[c] for kv in (kv_sib, kv_own)] for c in range(2))
    all_heads(False, per_kv, rank, flags, keys, values, q, do, term, w_q, down, up_q, dk, dv, scratch)


def previous_kernel(
    scale, per_kv, rank, flags, q, do, term, w_q, down, kv_own, kv_sib, kv_pc, kv_px,
    up_q_own, dk_own, dv_own, w_kv, down_win,
    keep_own, keep_pc, send, up_q, up_keep, up_send, grad_up,
    dk, dv, grads, *scratch,
):
    tokens = q.shape[0]
    up_q[...] = up_q_own[...]
    keys, values = ([kv.at[c] for kv in (kv_sib, kv_own, kv_pc, kv_px)] for c in range(2))
    all_heads(True, per_kv, rank, flags, keys, values, q, do, term, w_q, down, up_q, dk, dv, scratch)
    up_kv = [jnp.zeros((rank, 4 * tokens), jnp.float32) for _ in range(2)]
    kv_width = kv_own.shape[2]
    for g in range(kv_width // HEAD_SIZE):
        columns = slice(g * HEAD_SIZE, (g + 1) * HEAD_SIZE)
        low_row, own_row = g * 4 * tokens, g * 2 * tokens
        by_head = None
        for block in range(4):
            tail = dk[low_row + block * tokens : low_row + (block + 1) * tokens, HEAD_SIZE:]
            if block < 2:
                tail = tail + dk_own[own_row + block * tokens : own_row + (block + 1) * tokens, HEAD_SIZE:]
            part = mm(tail.T.astype(jnp.bfloat16), keys[block][:, columns])
            by_head = part if by_head is None else by_head + part
        for h in range(per_kv):
            at = (g * per_kv + h) * HEAD_SIZE
            grads[:rank, at : at + HEAD_SIZE] = by_head[h * rank : (h + 1) * rank, :]
        for c, acc, start in ((0, dk, dk_own), (1, dv, dv_own)):
            total = acc[low_row : low_row + 4 * tokens, :HEAD_SIZE]
            near = total[: 2 * tokens] + start[own_row : own_row + 2 * tokens, :HEAD_SIZE]
            low = jnp.concatenate([near, total[2 * tokens :]]).astype(jnp.bfloat16)
            keep_own[c, :, columns] = near[tokens:]
            keep_pc[c, :, columns] = total[2 * tokens : 3 * tokens]
            send[0, c, :, columns] = low[:tokens]
            send[1, c, :, columns] = low[3 * tokens :]
            up_kv[c] = up_kv[c] + mm(w_kv[c, :, columns], low, NT)
            own = slice(c * rank, (c + 1) * rank)
            grad_kv = mm(down_win[own, :], low)
            for r in range(rank):
                row, at = divmod((c * rank + r) * kv_width + g * HEAD_SIZE, grads.shape[1])
                grads[rank + row : rank + row + 1, at : at + HEAD_SIZE] = grad_kv[r : r + 1, :]
    sib, near, pc, px = (
        jnp.concatenate([up_kv[c][:, block * tokens : (block + 1) * tokens] for c in range(2)])
        for block in range(4)
    )
    grad_up[...] = (grads[...] * scale).astype(jnp.bfloat16)
    up_keep[...] = jnp.concatenate([near, pc])
    up_send[...] = jnp.concatenate([sib, px]).astype(jnp.bfloat16)


def attention(scale, flags, queries, grads, terms, w_q, down, kv_own, kv_sib):
    tokens, width = queries.shape
    kv_width = kv_own.shape[2]
    kv_local = kv_width // HEAD_SIZE
    per_kv = width // kv_width
    rank = w_q.shape[0]
    assert per_kv * rank == HEAD_SIZE
    f32, bf16 = jnp.float32, jnp.bfloat16
    shape = jax.ShapeDtypeStruct
    pairs = kv_local * per_kv * tokens * tokens
    smem = pl.BlockSpec(memory_space=pltpu.SMEM)
    vmem = pl.BlockSpec(memory_space=pltpu.VMEM)
    hbm = pl.BlockSpec(memory_space=pltpu.HBM)

    def scratch(blocks):
        rows = blocks * tokens
        slot = [
            pltpu.VMEM((rows, tokens), f32),
            pltpu.VMEM((rows, tokens), bf16),
            pltpu.VMEM((rows, tokens), bf16),
            pltpu.VMEM((1, tokens), f32),
        ]
        return [
            pltpu.SMEM((kv_local * per_kv + 1,), jnp.int32),
            pltpu.VMEM((tokens, width), bf16),
            pltpu.VMEM((tokens, width), bf16),
            pltpu.SemaphoreType.DMA((kv_local,)),
            pltpu.SemaphoreType.DMA((kv_local,)),
            pltpu.VMEM((kv_local * HEAD_SIZE, rows), bf16),
        ] + slot * 2

    def call(kernel, out_shape, scratch_shapes, work, name, *args):
        return pl.pallas_call(
            functools.partial(kernel, per_kv, rank),
            in_specs=[smem, hbm, hbm] + [vmem] * (len(args) - 3),
            out_specs=[vmem] * len(out_shape),
            out_shape=out_shape,
            scratch_shapes=scratch_shapes,
            compiler_params=pltpu.CompilerParams(vmem_limit_bytes=VMEM_LIMIT),
            cost_estimate=pl.CostEstimate(
                flops=work * pairs * HEAD_SIZE, bytes_accessed=6 * tokens * width, transcendentals=pairs
            ),
            name=name,
        )(*args)

    queries, grads = (pltpu.with_memory_space_constraint(a, pltpu.HBM) for a in (queries, grads))
    common = (flags, queries, grads, terms, w_q, down, kv_own, kv_sib)

    def own():
        return call(
            own_kernel,
            [
                shape((rank, tokens), f32),
                shape((2 * tokens * kv_local, 2 * HEAD_SIZE), f32),
                shape((2 * tokens * kv_local, HEAD_SIZE), f32),
            ],
            scratch(2),
            40,
            "own_chip_heads",
            *common,
        )

    def previous(kv_pc, kv_px, own_grads, w_kv, down_win):
        grad_rows = rank + 2 * rank * kv_width // width
        return call(
            functools.partial(previous_kernel, scale),
            [
                shape((2, tokens, kv_width), f32),
                shape((2, tokens, kv_width), f32),
                shape((2, 2, tokens, kv_width), bf16),
                shape((rank, tokens), f32),
                shape((4 * rank, tokens), f32),
                shape((4 * rank, tokens), bf16),
                shape((grad_rows, width), bf16),
            ],
            [
                pltpu.VMEM((4 * tokens * kv_local, 2 * HEAD_SIZE), f32),
                pltpu.VMEM((4 * tokens * kv_local, HEAD_SIZE), f32),
                pltpu.VMEM((grad_rows, width), f32),
            ]
            + scratch(4),
            80,
            "previous_chip_heads",
            *common,
            kv_pc,
            kv_px,
            *own_grads,
            w_kv,
            down_win,
        )

    return own, previous


def exchanged(value, axis, bit):
    return lax.ppermute(value, axis, [(i, i ^ bit) for i in range(lax.axis_size(axis))])


def moved(value, axis, by):
    count = lax.axis_size(axis)
    return lax.ppermute(value, axis, [(i, (i + by) % count) for i in range(count)])


def summed(value, axis):
    bit = 1
    while bit < lax.axis_size(axis):
        value = value + exchanged(value, axis, bit)
        bit *= 2
    return value


def small_call(kernel, out_shape, *args, scratch=(), limit=1):
    vmem = pl.BlockSpec(memory_space=pltpu.VMEM)
    return pl.pallas_call(
        kernel,
        in_specs=[vmem] * len(args),
        out_specs=[vmem] * len(out_shape),
        out_shape=out_shape,
        scratch_shapes=list(scratch),
        compiler_params=pltpu.CompilerParams(vmem_limit_bytes=limit * SMALL_VMEM),
    )(*args)


def place(unit, radix):
    return lax.axis_index("seq") // unit % radix


def lanes(index, wide):
    return pl.ds(pl.multiple_of(index * wide, HEAD_SIZE), wide)


def projected_and_stacked(down_weight, inputs, key_rows, value_rows):
    rows, width = down_weight.shape
    tokens, kv_width = key_rows.shape
    steps = kv_width // HEAD_SIZE
    args = [
        pltpu.with_memory_space_constraint(a, pltpu.HBM)
        for a in (down_weight, inputs, key_rows, value_rows)
    ]

    def kernel(weight, tokens_in, key, value, down, kv):
        part = mm(weight[...], tokens_in[...], NT)

        @pl.when(pl.program_id(0) == 0)
        def _():
            down[...] = part

        @pl.when(pl.program_id(0) > 0)
        def _():
            down[...] += part

        kv[0] = key[...]
        kv[1] = value[...]

    def columns(high, wide):
        return pl.BlockSpec((high, wide // steps), lambda g: (0, g))

    return pl.pallas_call(
        kernel,
        grid=(steps,),
        in_specs=[
            columns(rows, width),
            columns(tokens, width),
            columns(tokens, kv_width),
            columns(tokens, kv_width),
        ],
        out_specs=[
            pl.BlockSpec((rows, tokens), lambda g: (0, 0)),
            pl.BlockSpec((2, tokens, kv_width // steps), lambda g: (0, 0, g)),
        ],
        out_shape=[
            jax.ShapeDtypeStruct((rows, tokens), jnp.float32),
            jax.ShapeDtypeStruct((2, tokens, kv_width), jnp.bfloat16),
        ],
        compiler_params=pltpu.CompilerParams(
            dimension_semantics=("arbitrary",), vmem_limit_bytes=2 * SMALL_VMEM
        ),
    )(*args)


def up_sums(up_q, up_keep, received):
    rank, tokens = up_q.shape

    def kernel(up_q, keep, other, mine, to_send, previous):
        total = keep[...] + other[...].astype(jnp.float32)
        own = jnp.concatenate([up_q[...], total[: 2 * rank]])
        mine[...] = own
        to_send[...] = own.astype(jnp.bfloat16)
        previous[...] = total[2 * rank :].astype(jnp.bfloat16)

    shape = jax.ShapeDtypeStruct
    return small_call(
        kernel,
        [
            shape((3 * rank, tokens), jnp.float32),
            shape((3 * rank, tokens), jnp.bfloat16),
            shape((2 * rank, tokens), jnp.bfloat16),
        ],
        up_q,
        up_keep,
        received,
    )


def up_terms(mine, to_send, previous):
    heads, count = lax.axis_size("head"), lax.axis_size("seq")
    nearby = moved(previous, "seq", -2)
    if heads == 2:
        pairs = [
            (s * heads + h, (s - 2) % count * heads + 1 - h) for s in range(count) for h in range(heads)
        ]
        return [mine, exchanged(to_send, "head", 1), nearby, lax.ppermute(previous, ("seq", "head"), pairs)]
    rank = mine.shape[0] - previous.shape[0]
    total = jnp.concatenate([mine[:rank], mine[rank:] + nearby.astype(jnp.float32)])
    bit = 1
    while 2 * bit < heads:
        total = total + exchanged(total.astype(jnp.bfloat16), "head", bit).astype(jnp.float32)
        bit *= 2
    return [total, exchanged(total.astype(jnp.bfloat16), "head", bit)]


def weight_halves(terms, inputs, grad_up, scale):
    width = inputs.shape[1]
    wide = width // 2
    up_rows, tokens = terms[0].shape
    rows = up_rows + grad_up.shape[0]
    given = len(terms)

    def kernel(*refs):
        tokens_in, grads, up_low, *out = refs[given:]
        up = jnp.zeros((up_rows, tokens), jnp.float32)
        for term in refs[:given]:
            value = term[...].astype(jnp.float32)
            if value.shape[0] < up_rows:
                value = jnp.concatenate(
                    [jnp.zeros((up_rows - value.shape[0], tokens), jnp.float32), value]
                )
            up = up + value
        up = up.astype(jnp.bfloat16)
        up_low[...] = up
        for d in range(2):
            at = lanes(place(1, 2) ^ d, wide)
            out[d][...] = jnp.concatenate(
                [mm(up, tokens_in[:, at]) * scale, grads[:, at].astype(jnp.float32)]
            ).astype(jnp.bfloat16)

    shape = jax.ShapeDtypeStruct
    return small_call(
        kernel,
        [shape((up_rows, tokens), jnp.bfloat16)] + [shape((rows, wide), jnp.bfloat16)] * 2,
        *terms,
        inputs,
        grad_up,
        limit=2,
    )


def exchanged_pieces(pieces, unit):
    return [pieces[0]] + [exchanged(p, "seq", d * unit) for d, p in enumerate(pieces) if d]


def summed_and_cut(pieces, unit, radix):
    rows, whole = pieces[0].shape
    wide = whole // radix
    if wide % HEAD_SIZE:
        total = sum(p.astype(jnp.float32) for p in pieces).astype(jnp.bfloat16)
        return [
            lax.dynamic_slice_in_dim(total, (place(unit, radix) ^ d) * wide, wide, 1)
            for d in range(radix)
        ]
    given = len(pieces)

    def kernel(*refs):
        total = refs[-1]
        total[...] = sum(p[...].astype(jnp.float32) for p in refs[:given])
        for d in range(radix):
            refs[given + d][...] = total[:, lanes(place(unit, radix) ^ d, wide)].astype(jnp.bfloat16)

    return small_call(
        kernel,
        [jax.ShapeDtypeStruct((rows, wide), jnp.bfloat16)] * radix,
        *pieces,
        scratch=[pltpu.VMEM((rows, whole), jnp.float32)],
    )


def joined(pieces, unit):
    rows, wide = pieces[0].shape
    radix = len(pieces)
    if wide % HEAD_SIZE:
        whole = jnp.zeros((rows, radix * wide), jnp.bfloat16)
        for d in range(radix):
            whole = lax.dynamic_update_slice_in_dim(
                whole, pieces[d], (place(unit, radix) ^ d) * wide, 1
            )
        return whole

    def kernel(*refs):
        for d in range(radix):
            refs[radix][:, lanes(place(unit, radix) ^ d, wide)] = refs[d][...]

    return small_call(kernel, [jax.ShapeDtypeStruct((rows, radix * wide), jnp.bfloat16)], *pieces)[0]


def joined_outputs(pieces, rank, kv_shape):
    rows, wide = pieces[0].shape
    extra = rows - 4 * rank
    each = wide // kv_shape[1]
    per_row = kv_shape[0] // extra

    def kernel(one, two, down, up_q, up_kv):
        for d, half in enumerate((one, two)):
            at = place(1, 2) ^ d
            piece = half[...].astype(jnp.float32)
            down[:, lanes(at, wide)] = piece[: 3 * rank]
            up_q[:, lanes(at, wide)] = piece[3 * rank : 4 * rank]
            for i in range(extra):
                for b in range(each):
                    up_kv[pl.ds(per_row * i + each * at + b, 1), :] = piece[
                        4 * rank + i : 4 * rank + i + 1, b * kv_shape[1] : (b + 1) * kv_shape[1]
                    ]

    shape = jax.ShapeDtypeStruct
    return small_call(
        kernel,
        [
            shape((3 * rank, 2 * wide), jnp.float32),
            shape((rank, 2 * wide), jnp.float32),
            shape(kv_shape, jnp.float32),
        ],
        *pieces,
    )


def per_device(
    queries,
    layer_key_rows,
    layer_value_rows,
    output_gradient,
    output_row_sums,
    shifted_head_flags,
    inputs,
    adapter_down_weight,
    query_up_weight,
    key_value_up_weight,
):
    seq_count = lax.axis_size("seq")
    tokens, width = queries.shape
    kv_width = layer_key_rows.shape[1]
    whole_len = tokens * seq_count
    rank = adapter_down_weight.shape[1]
    assert GROUP == 4 * tokens and SHIFT == 2 * tokens
    levels = (seq_count.bit_length() - 1) // 2
    assert 4**levels == seq_count
    flattened_down = adapter_down_weight.reshape(3 * rank, width)
    scale = adapter_scale / math.sqrt(whole_len)
    down_part, kv_own = projected_and_stacked(flattened_down, inputs, layer_key_rows, layer_value_rows)
    kv_pc = moved(kv_own, "seq", 2)
    kv_sib = exchanged(kv_own, "seq", 1)

    down_low = summed(down_part, "head").astype(jnp.bfloat16)
    down_tiled = jnp.tile(down_low[:rank].T, (1, HEAD_SIZE // rank))
    down_own = down_low[rank:]
    down_pc = moved(down_own, "seq", 2)

    own, previous = attention(
        scale,
        shifted_head_flags,
        queries,
        output_gradient,
        output_row_sums,
        query_up_weight,
        down_tiled,
        kv_own,
        kv_sib,
    )
    own_grads, kv_pc, down_pc = lax.optimization_barrier((own(), kv_pc, down_pc))
    kv_px = exchanged(kv_pc, "seq", 1)
    down_others = exchanged(jnp.concatenate([down_own, down_pc]), "seq", 1)
    down_win = jnp.concatenate(
        [down_others[: 2 * rank], down_own, down_pc, down_others[2 * rank :]], axis=1
    )
    keep_own, keep_pc, send, up_q, up_keep, up_send, grad_up = previous(
        kv_pc, kv_px, own_grads, key_value_up_weight, down_win
    )

    up_received, send = lax.optimization_barrier((exchanged(up_send, "seq", 1), send))
    received = exchanged(send, "seq", 1)
    terms = up_terms(*up_sums(up_q, up_keep, up_received))
    back = (keep_pc + received[1].astype(jnp.float32)).astype(jnp.bfloat16)
    chunks = list(back.reshape(4, tokens // 2, kv_width))
    beside = [(i, i - 2) for i in range(seq_count) if i % 4 >= 2]
    before = [(i, (i - 2) % seq_count) for i in range(seq_count) if i % 4 < 2]

    terms[1], chunks[0] = lax.optimization_barrier((terms[1], chunks[0]))
    chunks[0] = lax.ppermute(chunks[0], "seq", before)
    up_low, *pieces = weight_halves(terms, inputs, grad_up, scale)
    pieces = summed_and_cut(exchanged_pieces(pieces, 1), 2, 2)
    pieces, chunks[:2] = lax.optimization_barrier((pieces, chunks[:2]))
    chunks[1] = lax.ppermute(chunks[1], "seq", before)
    pieces = exchanged_pieces(pieces, 2)
    pieces, chunks, back = lax.optimization_barrier((pieces, chunks, back))
    chunks[2] = lax.ppermute(chunks[2], "seq", before)
    back = lax.ppermute(back, "seq", beside)
    for level in range(1, levels):
        pieces = exchanged_pieces(summed_and_cut(pieces, 4**level, 4), 4**level)
    total = sum(p.astype(jnp.float32) for p in pieces).astype(jnp.bfloat16)
    total, chunks = lax.optimization_barrier((total, chunks))
    chunks[3] = lax.ppermute(chunks[3], "seq", before)
    grad_inputs = (
        adapter_scale
        * lax.dot_general(
            up_low, flattened_down, (((0,), (0,)), ((), ())), preferred_element_type=jnp.float32
        )
    ).astype(jnp.bfloat16)
    for level in range(levels - 1, 0, -1):
        total = joined(exchanged_pieces([total] * 4, 4**level), 4**level)
    total, grad_inputs, chunks = lax.optimization_barrier((total, grad_inputs, chunks))
    parts = [a.reshape(4, tokens // 2, kv_width) for a in (keep_own, received[0], back)]
    key_value_gradient = jnp.stack(
        [
            sum(a.astype(jnp.float32) for a in (*(p[i] for p in parts), chunk)).astype(jnp.bfloat16)
            for i, chunk in enumerate(chunks)
        ]
    ).reshape(2, tokens, kv_width)
    total = joined(exchanged_pieces([total] * 2, 2), 2)
    total, key_value_gradient = lax.optimization_barrier((total, key_value_gradient))
    down_gradient, grad_up_q, grad_up_kv = joined_outputs(
        exchanged_pieces([total] * 2, 1), rank, (2 * rank, kv_width)
    )
    return (
        grad_inputs,
        key_value_gradient,
        down_gradient.reshape(3, rank, width),
        grad_up_q,
        grad_up_kv.reshape(2, rank, kv_width),
    )


def solution(mesh):
    placed = (
        P("seq", "head"),
        P("seq", "head"),
        P("seq", "head"),
        P("seq", "head"),
        P("head", "seq"),
        P("head"),
        P("seq", "head"),
        P(None, None, "head"),
        P(None, "head"),
        P(None, None, "head"),
    )
    return jax.shard_map(
        per_device,
        mesh=mesh,
        in_specs=placed,
        out_specs=(
            P("seq", "head"),
            P(None, "seq", "head"),
            P(None, None, "head"),
            P(None, "head"),
            P(None, None, "head"),
        ),
        check_vma=False,
    )
```

```python
import functools
import math

import jax
import jax.numpy as jnp
from jax import lax
from jax.experimental import pallas as pl
from jax.experimental.pallas import tpu as pltpu
from jax.sharding import PartitionSpec as P

HEAD_SIZE = 128
GROUP = 1024
SHIFT = 512
CHUNK = 32
SMALL_VMEM = 8 * 1024 * 1024
VMEM_LIMIT = 32 * 1024 * 1024

adapter_scale = 2.0
masked_score = -1e30
score_scale = HEAD_SIZE ** (-0.5)
exp2_scale = score_scale * math.log2(math.e)

NT = (((1,), (1,)), ((), ()))
NN = (((1,), (0,)), ((), ()))


def mm(left, right, dims=NN):
    return lax.dot_general(left, right, dims, preferred_element_type=jnp.float32)


def heads_in_flight(blocks, rank, coming, current, last, valid, keys, values, q, do, term_ref, down, up_q, wk, dk, dv):
    tokens = q.shape[0]

    (_, column, key_column), (s_new, _, _, top_new, _) = coming
    query = q[:, column]

    (numbers, now_column, now_key), (s_ref, e_ref, ds_ref, top_ref, inv_ref) = current
    grad = do[:, now_column]
    term = term_ref[pl.ds(numbers[0], 1), :]
    top_now = top_ref[...]

    ((_, group, inner), last_column, _), (_, e_old, ds_old, _, inv_old) = last
    inverse = inv_old[...] * valid
    inverse_rows = jnp.broadcast_to(inverse, (HEAD_SIZE, tokens)).T
    scaled = inverse_rows * score_scale
    lane = lax.broadcasted_iota(jnp.int32, (tokens, HEAD_SIZE), 1) // rank
    own_columns = jnp.where(lane == inner, down[...].astype(jnp.float32), 0.0)
    grad_n = (do[:, last_column].astype(jnp.float32) * inverse_rows).astype(jnp.bfloat16)
    query_n = jnp.concatenate(
        [q[:, last_column].astype(jnp.float32) * scaled, own_columns * scaled], axis=1
    ).astype(jnp.bfloat16)
    own = pl.ds(pl.multiple_of(group * HEAD_SIZE + inner * rank, rank), rank)
    base = pl.multiple_of(group * wk.shape[1], tokens)

    top = None
    total = jnp.zeros((8, tokens), jnp.float32)
    back = None
    for block in blocks:
        rows = slice(block * tokens, (block + 1) * tokens)
        top = merged_top(top, scores_block(block, keys[block][:, key_column], query, s_new, rows))

        grad_probs = mm(values[block][:, now_key], grad, NT)
        for at in range(0, tokens, CHUNK):
            part = slice(block * tokens + at, block * tokens + at + CHUNK)
            weights = jnp.exp2((s_ref[part, :] - top_now) * exp2_scale)
            total = total + jnp.sum(weights.reshape(CHUNK // 8, 8, tokens), axis=0)
            e_ref[part, :] = weights.astype(jnp.bfloat16)
            ds_ref[part, :] = (weights * (grad_probs[at : at + CHUNK, :] - term)).astype(jnp.bfloat16)

        to = pl.ds(base + block * tokens, tokens)
        dv[to, :] += mm(e_old[rows, :], grad_n)
        dk[to, :] += mm(ds_old[rows, :], query_n)
        part = mm(wk[own, rows], ds_old[rows, :])
        back = part if back is None else back + part
    top_new[...] = jnp.max(top, axis=0, keepdims=True)
    inv_ref[...] = 1.0 / jnp.sum(total, axis=0, keepdims=True)
    up_q[...] += back * (inverse * score_scale)


def merged_top(top, here):
    return here if top is None else jnp.maximum(top, here)


def scores_block(block, key, query, s_ref, rows):
    tokens = query.shape[0]
    scores = mm(key, query, NT)
    if block == 1:
        key_row = lax.broadcasted_iota(jnp.int32, (tokens, tokens), 0)
        query_row = lax.broadcasted_iota(jnp.int32, (tokens, tokens), 1)
        scores = jnp.where(key_row <= query_row, scores, masked_score)
    s_ref[rows, :] = scores
    return jnp.max(scores.reshape(tokens // 8, 8, tokens), axis=0)


def last_gradients(blocks, rank, last, q, do, down, up_q, wk, dk, dv):
    tokens = q.shape[0]
    ((_, group, inner), column, _), (_, e_ref, ds_ref, _, inv_ref) = last
    low, high = blocks[0] * tokens, (blocks[-1] + 1) * tokens
    inverse = inv_ref[...]
    inverse_rows = jnp.broadcast_to(inverse, (HEAD_SIZE, tokens)).T
    scaled = inverse_rows * score_scale
    lane = lax.broadcasted_iota(jnp.int32, (tokens, HEAD_SIZE), 1) // rank
    own_columns = jnp.where(lane == inner, down[...].astype(jnp.float32), 0.0)
    grad_n = (do[:, column].astype(jnp.float32) * inverse_rows).astype(jnp.bfloat16)
    query_n = jnp.concatenate(
        [q[:, column].astype(jnp.float32) * scaled, own_columns * scaled], axis=1
    ).astype(jnp.bfloat16)
    rows = pl.ds(pl.multiple_of(group * wk.shape[1] + low, tokens), high - low)
    dv[rows, :] += mm(e_ref[low:high, :], grad_n)
    dk[rows, :] += mm(ds_ref[low:high, :], query_n)
    own = pl.ds(pl.multiple_of(group * HEAD_SIZE + inner * rank, rank), rank)
    up_q[...] += mm(wk[own, low:high], ds_ref[low:high, :]) * (inverse * score_scale)


def all_heads(
    with_previous, per_kv, rank, flags, keys, values, q_hbm, do_hbm, term, w_q, down, up_q, dk, dv, scratch
):
    listed, q, do, q_sem, do_sem, wk, *buffers = scratch
    tokens, width = q.shape
    groups = width // (per_kv * HEAD_SIZE)
    loads = []
    for g in range(groups):
        part = slice(g * per_kv * HEAD_SIZE, (g + 1) * per_kv * HEAD_SIZE)
        loads.append(
            [
                pltpu.make_async_copy(q_hbm.at[:, part], q.at[:, part], q_sem.at[g]),
                pltpu.make_async_copy(do_hbm.at[:, part], do.at[:, part], do_sem.at[g]),
            ]
        )
    for load in sum(loads, []):
        load.start()

    def wait(group):
        for load in loads[group]:
            load.wait()

    def wait_between(held, wanted):
        for g in range(1, groups):
            pl.when((g > held) & (g <= wanted))(functools.partial(wait, g))
        return jnp.maximum(held, wanted)

    height = wk.shape[1]
    for g in range(groups):
        stacked = jnp.concatenate(
            [w_q[:, h * HEAD_SIZE : (h + 1) * HEAD_SIZE] for h in range(g * per_kv, (g + 1) * per_kv)], axis=0
        )
        for block, key in enumerate(keys):
            wk[g * HEAD_SIZE : (g + 1) * HEAD_SIZE, block * tokens : (block + 1) * tokens] = mm(
                stacked, key[:, g * HEAD_SIZE : (g + 1) * HEAD_SIZE], NT
            ).astype(jnp.bfloat16)
    dk[...] = jnp.zeros_like(dk)
    dv[...] = jnp.zeros_like(dv)
    slots = (buffers[:5], buffers[5:])
    for _, e_ref, ds_ref, _, inv_ref in slots:
        e_ref[...] = jnp.zeros_like(e_ref)
        ds_ref[...] = jnp.zeros_like(ds_ref)
        inv_ref[...] = jnp.zeros_like(inv_ref)
    wait(0)
    index = lax.axis_index("seq")
    core = index % 2
    half = index // 2 % 2
    count = jnp.int32(0)
    for h in range(groups * per_kv):
        listed[count] = jnp.int32(h)
        needs = flags[h] != half
        count = count + jnp.where(needs == with_previous, 1, 0).astype(jnp.int32)

    def head_at(i):
        h = listed[jnp.clip(i, 0, count - 1)]
        group = h // per_kv
        return (
            (h, group, h - group * per_kv),
            pl.ds(pl.multiple_of(h * HEAD_SIZE, HEAD_SIZE), HEAD_SIZE),
            pl.ds(pl.multiple_of(group * HEAD_SIZE, HEAD_SIZE), HEAD_SIZE),
        )

    for which in range(2):
        blocks = range(1 - which, len(keys))

        def step(i, slot, other):
            valid = jnp.where(i > 0, 1.0, 0.0).astype(jnp.float32)
            heads_in_flight(
                blocks, rank, (head_at(i + 1), other), (head_at(i), slot), (head_at(i - 1), other), valid,
                keys, values, q, do, term, down, up_q, wk, dk, dv,
            )

        def finish(slot):
            last_gradients(blocks, rank, (head_at(count - 1), slot), q, do, down, up_q, wk, dk, dv)

        @pl.when((core == which) & (count > 0))
        def _():
            held = wait_between(jnp.int32(0), head_at(0)[0][1])
            s_ref, _, _, top_ref, _ = slots[0]
            _, column, key_column = head_at(0)
            top = None
            for block in blocks:
                rows = slice(block * tokens, (block + 1) * tokens)
                top = merged_top(
                    top, scores_block(block, keys[block][:, key_column], q[:, column], s_ref, rows)
                )
            top_ref[...] = jnp.max(top, axis=0, keepdims=True)

            def two(t, held):
                held = wait_between(held, head_at(2 * t + 2)[0][1])
                step(2 * t, *slots)
                step(2 * t + 1, *slots[::-1])
                return held

            held = lax.fori_loop(0, count // 2, two, held)
            wait_between(held, jnp.int32(groups - 1))

            @pl.when(count % 2 == 1)
            def _():
                step(count - 1, *slots)
                finish(slots[0])

            @pl.when(count % 2 == 0)
            def _():
                finish(slots[1])

    @pl.when(count == 0)
    def _():
        wait_between(jnp.int32(0), jnp.int32(groups - 1))


def own_kernel(
    per_kv, rank, flags, q, do, term, w_q, down, kv_own, kv_sib, up_q, dk, dv, *scratch
):
    up_q[...] = jnp.zeros_like(up_q)
    keys, values = ([kv.at[c] for kv in (kv_sib, kv_own)] for c in range(2))
    all_heads(False, per_kv, rank, flags, keys, values, q, do, term, w_q, down, up_q, dk, dv, scratch)


def previous_kernel(
    scale, per_kv, rank, flags, q, do, term, w_q, down, kv_own, kv_sib, kv_pc, kv_px,
    up_q_own, dk_own, dv_own, w_kv, down_win,
    keep_own, keep_pc, send, up_q, up_keep, up_send, grad_up,
    dk, dv, grads, *scratch,
):
    tokens = q.shape[0]
    up_q[...] = up_q_own[...]
    keys, values = ([kv.at[c] for kv in (kv_sib, kv_own, kv_pc, kv_px)] for c in range(2))
    all_heads(True, per_kv, rank, flags, keys, values, q, do, term, w_q, down, up_q, dk, dv, scratch)
    up_kv = [jnp.zeros((rank, 4 * tokens), jnp.float32) for _ in range(2)]
    kv_width = kv_own.shape[2]
    for g in range(kv_width // HEAD_SIZE):
        columns = slice(g * HEAD_SIZE, (g + 1) * HEAD_SIZE)
        low_row, own_row = g * 4 * tokens, g * 2 * tokens
        by_head = None
        for block in range(4):
            tail = dk[low_row + block * tokens : low_row + (block + 1) * tokens, HEAD_SIZE:]
            if block < 2:
                tail = tail + dk_own[own_row + block * tokens : own_row + (block + 1) * tokens, HEAD_SIZE:]
            part = mm(tail.T.astype(jnp.bfloat16), keys[block][:, columns])
            by_head = part if by_head is None else by_head + part
        for h in range(per_kv):
            at = (g * per_kv + h) * HEAD_SIZE
            grads[:rank, at : at + HEAD_SIZE] = by_head[h * rank : (h + 1) * rank, :]
        for c, acc, start in ((0, dk, dk_own), (1, dv, dv_own)):
            total = acc[low_row : low_row + 4 * tokens, :HEAD_SIZE]
            near = total[: 2 * tokens] + start[own_row : own_row + 2 * tokens, :HEAD_SIZE]
            low = jnp.concatenate([near, total[2 * tokens :]]).astype(jnp.bfloat16)
            keep_own[c, :, columns] = near[tokens:]
            keep_pc[c, :, columns] = total[2 * tokens : 3 * tokens]
            send[0, c, :, columns] = low[:tokens]
            send[1, c, :, columns] = low[3 * tokens :]
            up_kv[c] = up_kv[c] + mm(w_kv[c, :, columns], low, NT)
            own = slice(c * rank, (c + 1) * rank)
            grad_kv = mm(down_win[own, :], low)
            for r in range(rank):
                row, at = divmod((c * rank + r) * kv_width + g * HEAD_SIZE, grads.shape[1])
                grads[rank + row : rank + row + 1, at : at + HEAD_SIZE] = grad_kv[r : r + 1, :]
    sib, near, pc, px = (
        jnp.concatenate([up_kv[c][:, block * tokens : (block + 1) * tokens] for c in range(2)])
        for block in range(4)
    )
    grad_up[...] = (grads[...] * scale).astype(jnp.bfloat16)
    up_keep[...] = jnp.concatenate([near, pc])
    up_send[...] = jnp.concatenate([sib, px]).astype(jnp.bfloat16)


def attention(scale, flags, queries, grads, terms, w_q, down, kv_own, kv_sib):
    tokens, width = queries.shape
    kv_width = kv_own.shape[2]
    kv_local = kv_width // HEAD_SIZE
    per_kv = width // kv_width
    rank = w_q.shape[0]
    assert per_kv * rank == HEAD_SIZE
    f32, bf16 = jnp.float32, jnp.bfloat16
    shape = jax.ShapeDtypeStruct
    pairs = kv_local * per_kv * tokens * tokens
    smem = pl.BlockSpec(memory_space=pltpu.SMEM)
    vmem = pl.BlockSpec(memory_space=pltpu.VMEM)
    hbm = pl.BlockSpec(memory_space=pltpu.HBM)

    def scratch(blocks):
        rows = blocks * tokens
        slot = [
            pltpu.VMEM((rows, tokens), f32),
            pltpu.VMEM((rows, tokens), bf16),
            pltpu.VMEM((rows, tokens), bf16),
            pltpu.VMEM((1, tokens), f32),
            pltpu.VMEM((1, tokens), f32),
        ]
        return [
            pltpu.SMEM((kv_local * per_kv + 1,), jnp.int32),
            pltpu.VMEM((tokens, width), bf16),
            pltpu.VMEM((tokens, width), bf16),
            pltpu.SemaphoreType.DMA((kv_local,)),
            pltpu.SemaphoreType.DMA((kv_local,)),
            pltpu.VMEM((kv_local * HEAD_SIZE, rows), bf16),
        ] + slot * 2

    def call(kernel, out_shape, scratch_shapes, work, name, *args):
        return pl.pallas_call(
            functools.partial(kernel, per_kv, rank),
            in_specs=[smem, hbm, hbm] + [vmem] * (len(args) - 3),
            out_specs=[vmem] * len(out_shape),
            out_shape=out_shape,
            scratch_shapes=scratch_shapes,
            compiler_params=pltpu.CompilerParams(vmem_limit_bytes=VMEM_LIMIT),
            cost_estimate=pl.CostEstimate(
                flops=work * pairs * HEAD_SIZE, bytes_accessed=6 * tokens * width, transcendentals=pairs
            ),
            name=name,
        )(*args)

    queries, grads = (pltpu.with_memory_space_constraint(a, pltpu.HBM) for a in (queries, grads))
    common = (flags, queries, grads, terms, w_q, down, kv_own, kv_sib)

    def own():
        return call(
            own_kernel,
            [
                shape((rank, tokens), f32),
                shape((2 * tokens * kv_local, 2 * HEAD_SIZE), f32),
                shape((2 * tokens * kv_local, HEAD_SIZE), f32),
            ],
            scratch(2),
            40,
            "own_chip_heads",
            *common,
        )

    def previous(kv_pc, kv_px, own_grads, w_kv, down_win):
        grad_rows = rank + 2 * rank * kv_width // width
        return call(
            functools.partial(previous_kernel, scale),
            [
                shape((2, tokens, kv_width), f32),
                shape((2, tokens, kv_width), f32),
                shape((2, 2, tokens, kv_width), bf16),
                shape((rank, tokens), f32),
                shape((4 * rank, tokens), f32),
                shape((4 * rank, tokens), bf16),
                shape((grad_rows, width), bf16),
            ],
            [
                pltpu.VMEM((4 * tokens * kv_local, 2 * HEAD_SIZE), f32),
                pltpu.VMEM((4 * tokens * kv_local, HEAD_SIZE), f32),
                pltpu.VMEM((grad_rows, width), f32),
            ]
            + scratch(4),
            80,
            "previous_chip_heads",
            *common,
            kv_pc,
            kv_px,
            *own_grads,
            w_kv,
            down_win,
        )

    return own, previous


def exchanged(value, axis, bit):
    return lax.ppermute(value, axis, [(i, i ^ bit) for i in range(lax.axis_size(axis))])


def moved(value, axis, by):
    count = lax.axis_size(axis)
    return lax.ppermute(value, axis, [(i, (i + by) % count) for i in range(count)])


def summed(value, axis):
    bit = 1
    while bit < lax.axis_size(axis):
        value = value + exchanged(value, axis, bit)
        bit *= 2
    return value


def small_call(kernel, out_shape, *args, scratch=(), limit=1):
    vmem = pl.BlockSpec(memory_space=pltpu.VMEM)
    return pl.pallas_call(
        kernel,
        in_specs=[vmem] * len(args),
        out_specs=[vmem] * len(out_shape),
        out_shape=out_shape,
        scratch_shapes=list(scratch),
        compiler_params=pltpu.CompilerParams(vmem_limit_bytes=limit * SMALL_VMEM),
    )(*args)


def place(unit, radix):
    return lax.axis_index("seq") // unit % radix


def lanes(index, wide):
    return pl.ds(pl.multiple_of(index * wide, HEAD_SIZE), wide)


def projected_and_stacked(down_weight, inputs, key_rows, value_rows):
    rows, width = down_weight.shape
    tokens, kv_width = key_rows.shape
    steps = kv_width // HEAD_SIZE
    args = [
        pltpu.with_memory_space_constraint(a, pltpu.HBM)
        for a in (down_weight, inputs, key_rows, value_rows)
    ]

    def kernel(weight, tokens_in, key, value, down, kv):
        part = mm(weight[...], tokens_in[...], NT)

        @pl.when(pl.program_id(0) == 0)
        def _():
            down[...] = part

        @pl.when(pl.program_id(0) > 0)
        def _():
            down[...] += part

        kv[0] = key[...]
        kv[1] = value[...]

    def columns(high, wide):
        return pl.BlockSpec((high, wide // steps), lambda g: (0, g))

    return pl.pallas_call(
        kernel,
        grid=(steps,),
        in_specs=[
            columns(rows, width),
            columns(tokens, width),
            columns(tokens, kv_width),
            columns(tokens, kv_width),
        ],
        out_specs=[
            pl.BlockSpec((rows, tokens), lambda g: (0, 0)),
            pl.BlockSpec((2, tokens, kv_width // steps), lambda g: (0, 0, g)),
        ],
        out_shape=[
            jax.ShapeDtypeStruct((rows, tokens), jnp.float32),
            jax.ShapeDtypeStruct((2, tokens, kv_width), jnp.bfloat16),
        ],
        compiler_params=pltpu.CompilerParams(
            dimension_semantics=("arbitrary",), vmem_limit_bytes=2 * SMALL_VMEM
        ),
    )(*args)


def up_sums(up_q, up_keep, received):
    rank, tokens = up_q.shape

    def kernel(up_q, keep, other, mine, to_send, previous):
        total = keep[...] + other[...].astype(jnp.float32)
        own = jnp.concatenate([up_q[...], total[: 2 * rank]])
        mine[...] = own
        to_send[...] = own.astype(jnp.bfloat16)
        previous[...] = total[2 * rank :].astype(jnp.bfloat16)

    shape = jax.ShapeDtypeStruct
    return small_call(
        kernel,
        [
            shape((3 * rank, tokens), jnp.float32),
            shape((3 * rank, tokens), jnp.bfloat16),
            shape((2 * rank, tokens), jnp.bfloat16),
        ],
        up_q,
        up_keep,
        received,
    )


def up_terms(mine, to_send, previous):
    heads, count = lax.axis_size("head"), lax.axis_size("seq")
    nearby = moved(previous, "seq", -2)
    if heads == 2:
        pairs = [
            (s * heads + h, (s - 2) % count * heads + 1 - h) for s in range(count) for h in range(heads)
        ]
        return [mine, exchanged(to_send, "head", 1), nearby, lax.ppermute(previous, ("seq", "head"), pairs)]
    rank = mine.shape[0] - previous.shape[0]
    total = jnp.concatenate([mine[:rank], mine[rank:] + nearby.astype(jnp.float32)])
    bit = 1
    while 2 * bit < heads:
        total = total + exchanged(total.astype(jnp.bfloat16), "head", bit).astype(jnp.float32)
        bit *= 2
    return [total, exchanged(total.astype(jnp.bfloat16), "head", bit)]


def weight_halves(terms, inputs, grad_up, scale):
    width = inputs.shape[1]
    wide = width // 2
    up_rows, tokens = terms[0].shape
    rows = up_rows + grad_up.shape[0]
    given = len(terms)

    def kernel(*refs):
        tokens_in, grads, up_low, *out = refs[given:]
        up = jnp.zeros((up_rows, tokens), jnp.float32)
        for term in refs[:given]:
            value = term[...].astype(jnp.float32)
            if value.shape[0] < up_rows:
                value = jnp.concatenate(
                    [jnp.zeros((up_rows - value.shape[0], tokens), jnp.float32), value]
                )
            up = up + value
        up = up.astype(jnp.bfloat16)
        up_low[...] = up
        for d in range(2):
            at = lanes(place(1, 2) ^ d, wide)
            out[d][...] = jnp.concatenate(
                [mm(up, tokens_in[:, at]) * scale, grads[:, at].astype(jnp.float32)]
            ).astype(jnp.bfloat16)

    shape = jax.ShapeDtypeStruct
    return small_call(
        kernel,
        [shape((up_rows, tokens), jnp.bfloat16)] + [shape((rows, wide), jnp.bfloat16)] * 2,
        *terms,
        inputs,
        grad_up,
        limit=2,
    )


def exchanged_pieces(pieces, unit):
    return [pieces[0]] + [exchanged(p, "seq", d * unit) for d, p in enumerate(pieces) if d]


def summed_and_cut(pieces, unit, radix):
    rows, whole = pieces[0].shape
    wide = whole // radix
    if wide % HEAD_SIZE:
        total = sum(p.astype(jnp.float32) for p in pieces).astype(jnp.bfloat16)
        return [
            lax.dynamic_slice_in_dim(total, (place(unit, radix) ^ d) * wide, wide, 1)
            for d in range(radix)
        ]
    given = len(pieces)

    def kernel(*refs):
        total = refs[-1]
        total[...] = sum(p[...].astype(jnp.float32) for p in refs[:given])
        for d in range(radix):
            refs[given + d][...] = total[:, lanes(place(unit, radix) ^ d, wide)].astype(jnp.bfloat16)

    return small_call(
        kernel,
        [jax.ShapeDtypeStruct((rows, wide), jnp.bfloat16)] * radix,
        *pieces,
        scratch=[pltpu.VMEM((rows, whole), jnp.float32)],
    )


def joined(pieces, unit):
    rows, wide = pieces[0].shape
    radix = len(pieces)
    if wide % HEAD_SIZE:
        whole = jnp.zeros((rows, radix * wide), jnp.bfloat16)
        for d in range(radix):
            whole = lax.dynamic_update_slice_in_dim(
                whole, pieces[d], (place(unit, radix) ^ d) * wide, 1
            )
        return whole

    def kernel(*refs):
        for d in range(radix):
            refs[radix][:, lanes(place(unit, radix) ^ d, wide)] = refs[d][...]

    return small_call(kernel, [jax.ShapeDtypeStruct((rows, radix * wide), jnp.bfloat16)], *pieces)[0]


def joined_outputs(pieces, rank, kv_shape):
    rows, wide = pieces[0].shape
    extra = rows - 4 * rank
    each = wide // kv_shape[1]
    per_row = kv_shape[0] // extra

    def kernel(one, two, down, up_q, up_kv):
        for d, half in enumerate((one, two)):
            at = place(1, 2) ^ d
            piece = half[...].astype(jnp.float32)
            down[:, lanes(at, wide)] = piece[: 3 * rank]
            up_q[:, lanes(at, wide)] = piece[3 * rank : 4 * rank]
            for i in range(extra):
                for b in range(each):
                    up_kv[pl.ds(per_row * i + each * at + b, 1), :] = piece[
                        4 * rank + i : 4 * rank + i + 1, b * kv_shape[1] : (b + 1) * kv_shape[1]
                    ]

    shape = jax.ShapeDtypeStruct
    return small_call(
        kernel,
        [
            shape((3 * rank, 2 * wide), jnp.float32),
            shape((rank, 2 * wide), jnp.float32),
            shape(kv_shape, jnp.float32),
        ],
        *pieces,
    )


def per_device(
    queries,
    layer_key_rows,
    layer_value_rows,
    output_gradient,
    output_row_sums,
    shifted_head_flags,
    inputs,
    adapter_down_weight,
    query_up_weight,
    key_value_up_weight,
):
    seq_count = lax.axis_size("seq")
    tokens, width = queries.shape
    kv_width = layer_key_rows.shape[1]
    whole_len = tokens * seq_count
    rank = adapter_down_weight.shape[1]
    assert GROUP == 4 * tokens and SHIFT == 2 * tokens
    levels = (seq_count.bit_length() - 1) // 2
    assert 4**levels == seq_count
    flattened_down = adapter_down_weight.reshape(3 * rank, width)
    scale = adapter_scale / math.sqrt(whole_len)
    down_part, kv_own = projected_and_stacked(flattened_down, inputs, layer_key_rows, layer_value_rows)
    kv_pc = moved(kv_own, "seq", 2)
    kv_sib = exchanged(kv_own, "seq", 1)

    down_low = summed(down_part, "head").astype(jnp.bfloat16)
    down_tiled = jnp.tile(down_low[:rank].T, (1, HEAD_SIZE // rank))
    down_own = down_low[rank:]
    down_pc = moved(down_own, "seq", 2)

    own, previous = attention(
        scale,
        shifted_head_flags,
        queries,
        output_gradient,
        output_row_sums,
        query_up_weight,
        down_tiled,
        kv_own,
        kv_sib,
    )
    own_grads, kv_pc, down_pc = lax.optimization_barrier((own(), kv_pc, down_pc))
    kv_px = exchanged(kv_pc, "seq", 1)
    down_others = exchanged(jnp.concatenate([down_own, down_pc]), "seq", 1)
    down_win = jnp.concatenate(
        [down_others[: 2 * rank], down_own, down_pc, down_others[2 * rank :]], axis=1
    )
    keep_own, keep_pc, send, up_q, up_keep, up_send, grad_up = previous(
        kv_pc, kv_px, own_grads, key_value_up_weight, down_win
    )

    up_received, send = lax.optimization_barrier((exchanged(up_send, "seq", 1), send))
    received = exchanged(send, "seq", 1)
    terms = up_terms(*up_sums(up_q, up_keep, up_received))
    back = (keep_pc + received[1].astype(jnp.float32)).astype(jnp.bfloat16)
    up_low, *pieces = weight_halves(terms, inputs, grad_up, scale)
    pieces = exchanged_pieces(summed_and_cut(exchanged_pieces(pieces, 1), 2, 2), 2)
    pieces, back = lax.optimization_barrier((pieces, back))
    back = moved(back, "seq", -2)
    for level in range(1, levels):
        pieces = exchanged_pieces(summed_and_cut(pieces, 4**level, 4), 4**level)
    total = sum(p.astype(jnp.float32) for p in pieces).astype(jnp.bfloat16)
    key_value_gradient = (
        keep_own + received[0].astype(jnp.float32) + back.astype(jnp.float32)
    ).astype(jnp.bfloat16)
    grad_inputs = (
        adapter_scale
        * lax.dot_general(
            up_low, flattened_down, (((0,), (0,)), ((), ())), preferred_element_type=jnp.float32
        )
    ).astype(jnp.bfloat16)
    for level in range(levels - 1, 0, -1):
        total = joined(exchanged_pieces([total] * 4, 4**level), 4**level)
    total, grad_inputs = lax.optimization_barrier((total, grad_inputs))
    total = joined(exchanged_pieces([total] * 2, 2), 2)
    total, key_value_gradient = lax.optimization_barrier((total, key_value_gradient))
    down_gradient, grad_up_q, grad_up_kv = joined_outputs(
        exchanged_pieces([total] * 2, 1), rank, (2 * rank, kv_width)
    )
    return (
        grad_inputs,
        key_value_gradient,
        down_gradient.reshape(3, rank, width),
        grad_up_q,
        grad_up_kv.reshape(2, rank, kv_width),
    )


def solution(mesh):
    placed = (
        P("seq", "head"),
        P("seq", "head"),
        P("seq", "head"),
        P("seq", "head"),
        P("head", "seq"),
        P("head"),
        P("seq", "head"),
        P(None, None, "head"),
        P(None, "head"),
        P(None, None, "head"),
    )
    return jax.shard_map(
        per_device,
        mesh=mesh,
        in_specs=placed,
        out_specs=(
            P("seq", "head"),
            P(None, "seq", "head"),
            P(None, None, "head"),
            P(None, "head"),
            P(None, None, "head"),
        ),
        check_vma=False,
    )
```

```python
import functools
import math

import jax
import jax.numpy as jnp
from jax import lax
from jax.experimental import pallas as pl
from jax.experimental.pallas import tpu as pltpu
from jax.sharding import PartitionSpec as P

HEAD_SIZE = 128
GROUP = 1024
SHIFT = 512
CHUNK = 32
CUT_WORK = 5 * 10**9
SMALL_VMEM = 8 * 1024 * 1024
VMEM_LIMIT = 32 * 1024 * 1024

adapter_scale = 2.0
masked_score = -1e30
score_scale = HEAD_SIZE ** (-0.5)
exp2_scale = score_scale * math.log2(math.e)

NT = (((1,), (1,)), ((), ()))
NN = (((1,), (0,)), ((), ()))


def mm(left, right, dims=NN):
    return lax.dot_general(left, right, dims, preferred_element_type=jnp.float32)


def heads_in_flight(blocks, rank, coming, current, last, valid, keys, values, q, do, term_ref, down, up_q, wk, dk, dv):
    tokens = q.shape[0]

    (_, column, key_column), (s_new, _, _, top_new, _) = coming
    query = q[:, column]

    (numbers, now_column, now_key), (s_ref, e_ref, ds_ref, top_ref, inv_ref) = current
    grad = do[:, now_column]
    term = term_ref[pl.ds(numbers[0], 1), :]
    top_now = top_ref[...]

    ((_, group, inner), last_column, _), (_, e_old, ds_old, _, inv_old) = last
    inverse = inv_old[...] * valid
    inverse_rows = jnp.broadcast_to(inverse, (HEAD_SIZE, tokens)).T
    scaled = inverse_rows * score_scale
    lane = lax.broadcasted_iota(jnp.int32, (tokens, HEAD_SIZE), 1) // rank
    own_columns = jnp.where(lane == inner, down[...].astype(jnp.float32), 0.0)
    grad_n = (do[:, last_column].astype(jnp.float32) * inverse_rows).astype(jnp.bfloat16)
    query_n = jnp.concatenate(
        [q[:, last_column].astype(jnp.float32) * scaled, own_columns * scaled], axis=1
    ).astype(jnp.bfloat16)
    own = pl.ds(pl.multiple_of(group * HEAD_SIZE + inner * rank, rank), rank)
    base = pl.multiple_of(group * wk.shape[1], tokens)

    top = None
    total = jnp.zeros((8, tokens), jnp.float32)
    back = None
    for block in blocks:
        rows = slice(block * tokens, (block + 1) * tokens)
        top = merged_top(top, scores_block(block, keys[block][:, key_column], query, s_new, rows))

        grad_probs = mm(values[block][:, now_key], grad, NT)
        for at in range(0, tokens, CHUNK):
            part = slice(block * tokens + at, block * tokens + at + CHUNK)
            weights = jnp.exp2((s_ref[part, :] - top_now) * exp2_scale)
            total = total + jnp.sum(weights.reshape(CHUNK // 8, 8, tokens), axis=0)
            e_ref[part, :] = weights.astype(jnp.bfloat16)
            ds_ref[part, :] = (weights * (grad_probs[at : at + CHUNK, :] - term)).astype(jnp.bfloat16)

        to = pl.ds(base + block * tokens, tokens)
        dv[to, :] += mm(e_old[rows, :], grad_n)
        dk[to, :] += mm(ds_old[rows, :], query_n)
        part = mm(wk[own, rows], ds_old[rows, :])
        back = part if back is None else back + part
    top_new[...] = jnp.max(top, axis=0, keepdims=True)
    inv_ref[...] = 1.0 / jnp.sum(total, axis=0, keepdims=True)
    up_q[...] += back * (inverse * score_scale)


def merged_top(top, here):
    return here if top is None else jnp.maximum(top, here)


def scores_block(block, key, query, s_ref, rows):
    tokens = query.shape[0]
    scores = mm(key, query, NT)
    if block == 1:
        key_row = lax.broadcasted_iota(jnp.int32, (tokens, tokens), 0)
        query_row = lax.broadcasted_iota(jnp.int32, (tokens, tokens), 1)
        scores = jnp.where(key_row <= query_row, scores, masked_score)
    s_ref[rows, :] = scores
    return jnp.max(scores.reshape(tokens // 8, 8, tokens), axis=0)


def last_gradients(blocks, rank, last, q, do, down, up_q, wk, dk, dv):
    tokens = q.shape[0]
    ((_, group, inner), column, _), (_, e_ref, ds_ref, _, inv_ref) = last
    low, high = blocks[0] * tokens, (blocks[-1] + 1) * tokens
    inverse = inv_ref[...]
    inverse_rows = jnp.broadcast_to(inverse, (HEAD_SIZE, tokens)).T
    scaled = inverse_rows * score_scale
    lane = lax.broadcasted_iota(jnp.int32, (tokens, HEAD_SIZE), 1) // rank
    own_columns = jnp.where(lane == inner, down[...].astype(jnp.float32), 0.0)
    grad_n = (do[:, column].astype(jnp.float32) * inverse_rows).astype(jnp.bfloat16)
    query_n = jnp.concatenate(
        [q[:, column].astype(jnp.float32) * scaled, own_columns * scaled], axis=1
    ).astype(jnp.bfloat16)
    rows = pl.ds(pl.multiple_of(group * wk.shape[1] + low, tokens), high - low)
    dv[rows, :] += mm(e_ref[low:high, :], grad_n)
    dk[rows, :] += mm(ds_ref[low:high, :], query_n)
    own = pl.ds(pl.multiple_of(group * HEAD_SIZE + inner * rank, rank), rank)
    up_q[...] += mm(wk[own, low:high], ds_ref[low:high, :]) * (inverse * score_scale)


def all_heads(
    with_previous, per_kv, rank, flags, keys, values, q_hbm, do_hbm, term, w_q, down, up_q, dk, dv, scratch
):
    listed, q, do, q_sem, do_sem, wk, *buffers = scratch
    tokens, width = q.shape
    groups = width // (per_kv * HEAD_SIZE)
    loads = []
    for g in range(groups):
        part = slice(g * per_kv * HEAD_SIZE, (g + 1) * per_kv * HEAD_SIZE)
        loads.append(
            [
                pltpu.make_async_copy(q_hbm.at[:, part], q.at[:, part], q_sem.at[g]),
                pltpu.make_async_copy(do_hbm.at[:, part], do.at[:, part], do_sem.at[g]),
            ]
        )
    for load in sum(loads, []):
        load.start()

    def wait(group):
        for load in loads[group]:
            load.wait()

    def wait_between(held, wanted):
        for g in range(1, groups):
            pl.when((g > held) & (g <= wanted))(functools.partial(wait, g))
        return jnp.maximum(held, wanted)

    height = wk.shape[1]
    for g in range(groups):
        stacked = jnp.concatenate(
            [w_q[:, h * HEAD_SIZE : (h + 1) * HEAD_SIZE] for h in range(g * per_kv, (g + 1) * per_kv)], axis=0
        )
        for block, key in enumerate(keys):
            wk[g * HEAD_SIZE : (g + 1) * HEAD_SIZE, block * tokens : (block + 1) * tokens] = mm(
                stacked, key[:, g * HEAD_SIZE : (g + 1) * HEAD_SIZE], NT
            ).astype(jnp.bfloat16)
    dk[...] = jnp.zeros_like(dk)
    dv[...] = jnp.zeros_like(dv)
    slots = (buffers[:5], buffers[5:])
    _, e_ref, ds_ref, _, inv_ref = slots[1]
    e_ref[...] = jnp.zeros_like(e_ref)
    ds_ref[...] = jnp.zeros_like(ds_ref)
    inv_ref[...] = jnp.zeros_like(inv_ref)
    wait(0)
    index = lax.axis_index("seq")
    core = index % 2
    half = index // 2 % 2
    count = jnp.int32(0)
    for h in range(groups * per_kv):
        listed[count] = jnp.int32(h)
        needs = flags[h] != half
        count = count + jnp.where(needs == with_previous, 1, 0).astype(jnp.int32)

    def head_at(i):
        h = listed[jnp.clip(i, 0, count - 1)]
        group = h // per_kv
        return (
            (h, group, h - group * per_kv),
            pl.ds(pl.multiple_of(h * HEAD_SIZE, HEAD_SIZE), HEAD_SIZE),
            pl.ds(pl.multiple_of(group * HEAD_SIZE, HEAD_SIZE), HEAD_SIZE),
        )

    for which in range(2):
        blocks = range(1 - which, len(keys))

        def step(i, slot, other):
            valid = jnp.where(i > 0, 1.0, 0.0).astype(jnp.float32)
            heads_in_flight(
                blocks, rank, (head_at(i + 1), other), (head_at(i), slot), (head_at(i - 1), other), valid,
                keys, values, q, do, term, down, up_q, wk, dk, dv,
            )

        def finish(slot):
            last_gradients(blocks, rank, (head_at(count - 1), slot), q, do, down, up_q, wk, dk, dv)

        @pl.when((core == which) & (count > 0))
        def _():
            held = wait_between(jnp.int32(0), head_at(0)[0][1])
            s_ref, _, _, top_ref, _ = slots[0]
            _, column, key_column = head_at(0)
            top = None
            for block in blocks:
                rows = slice(block * tokens, (block + 1) * tokens)
                top = merged_top(
                    top, scores_block(block, keys[block][:, key_column], q[:, column], s_ref, rows)
                )
            top_ref[...] = jnp.max(top, axis=0, keepdims=True)

            def two(t, held):
                held = wait_between(held, head_at(2 * t + 2)[0][1])
                step(2 * t, *slots)
                step(2 * t + 1, *slots[::-1])
                return held

            held = lax.fori_loop(0, count // 2, two, held)
            wait_between(held, jnp.int32(groups - 1))

            @pl.when(count % 2 == 1)
            def _():
                step(count - 1, *slots)
                finish(slots[0])

            @pl.when(count % 2 == 0)
            def _():
                finish(slots[1])

    @pl.when(count == 0)
    def _():
        wait_between(jnp.int32(0), jnp.int32(groups - 1))


def own_kernel(
    per_kv, rank, flags, q, do, term, w_q, down, kv_own, kv_sib, up_q, dk, dv, *scratch
):
    up_q[...] = jnp.zeros_like(up_q)
    keys, values = ([kv.at[c] for kv in (kv_sib, kv_own)] for c in range(2))
    all_heads(False, per_kv, rank, flags, keys, values, q, do, term, w_q, down, up_q, dk, dv, scratch)


def previous_kernel(
    scale, per_kv, rank, flags, q, do, term, w_q, down, kv_own, kv_sib, kv_pc, kv_px,
    up_q_own, dk_own, dv_own, w_kv, down_win,
    keep_own, keep_pc, send, up_q, up_keep, up_send, grad_up,
    dk, dv, grads, *scratch,
):
    tokens = q.shape[0]
    up_q[...] = up_q_own[...]
    keys, values = ([kv.at[c] for kv in (kv_sib, kv_own, kv_pc, kv_px)] for c in range(2))
    all_heads(True, per_kv, rank, flags, keys, values, q, do, term, w_q, down, up_q, dk, dv, scratch)
    up_kv = [jnp.zeros((rank, 4 * tokens), jnp.float32) for _ in range(2)]
    kv_width = kv_own.shape[2]
    for g in range(kv_width // HEAD_SIZE):
        columns = slice(g * HEAD_SIZE, (g + 1) * HEAD_SIZE)
        low_row, own_row = g * 4 * tokens, g * 2 * tokens
        by_head = None
        for block in range(4):
            tail = dk[low_row + block * tokens : low_row + (block + 1) * tokens, HEAD_SIZE:]
            if block < 2:
                tail = tail + dk_own[own_row + block * tokens : own_row + (block + 1) * tokens, HEAD_SIZE:]
            part = mm(tail.T.astype(jnp.bfloat16), keys[block][:, columns])
            by_head = part if by_head is None else by_head + part
        for h in range(per_kv):
            at = (g * per_kv + h) * HEAD_SIZE
            grads[:rank, at : at + HEAD_SIZE] = by_head[h * rank : (h + 1) * rank, :]
        for c, acc, start in ((0, dk, dk_own), (1, dv, dv_own)):
            total = acc[low_row : low_row + 4 * tokens, :HEAD_SIZE]
            near = total[: 2 * tokens] + start[own_row : own_row + 2 * tokens, :HEAD_SIZE]
            low = jnp.concatenate([near, total[2 * tokens :]]).astype(jnp.bfloat16)
            keep_own[c, :, columns] = near[tokens:]
            keep_pc[c, :, columns] = total[2 * tokens : 3 * tokens]
            send[0, c, :, columns] = low[:tokens]
            send[1, c, :, columns] = low[3 * tokens :]
            up_kv[c] = up_kv[c] + mm(w_kv[c, :, columns], low, NT)
            own = slice(c * rank, (c + 1) * rank)
            grad_kv = mm(down_win[own, :], low)
            for r in range(rank):
                row, at = divmod((c * rank + r) * kv_width + g * HEAD_SIZE, grads.shape[1])
                grads[rank + row : rank + row + 1, at : at + HEAD_SIZE] = grad_kv[r : r + 1, :]
    sib, near, pc, px = (
        jnp.concatenate([up_kv[c][:, block * tokens : (block + 1) * tokens] for c in range(2)])
        for block in range(4)
    )
    grad_up[...] = (grads[...] * scale).astype(jnp.bfloat16)
    up_keep[...] = jnp.concatenate([near, pc])
    up_send[...] = jnp.concatenate([sib, px]).astype(jnp.bfloat16)


def attention(scale, flags, queries, grads, terms, w_q, down, kv_own, kv_sib):
    tokens, width = queries.shape
    kv_width = kv_own.shape[2]
    kv_local = kv_width // HEAD_SIZE
    per_kv = width // kv_width
    rank = w_q.shape[0]
    assert per_kv * rank == HEAD_SIZE
    f32, bf16 = jnp.float32, jnp.bfloat16
    shape = jax.ShapeDtypeStruct
    pairs = kv_local * per_kv * tokens * tokens
    smem = pl.BlockSpec(memory_space=pltpu.SMEM)
    vmem = pl.BlockSpec(memory_space=pltpu.VMEM)
    hbm = pl.BlockSpec(memory_space=pltpu.HBM)

    def scratch(blocks):
        rows = blocks * tokens
        slot = [
            pltpu.VMEM((rows, tokens), f32),
            pltpu.VMEM((rows, tokens), bf16),
            pltpu.VMEM((rows, tokens), bf16),
            pltpu.VMEM((1, tokens), f32),
            pltpu.VMEM((1, tokens), f32),
        ]
        return [
            pltpu.SMEM((kv_local * per_kv + 1,), jnp.int32),
            pltpu.VMEM((tokens, width), bf16),
            pltpu.VMEM((tokens, width), bf16),
            pltpu.SemaphoreType.DMA((kv_local,)),
            pltpu.SemaphoreType.DMA((kv_local,)),
            pltpu.VMEM((kv_local * HEAD_SIZE, rows), bf16),
        ] + slot * 2

    def call(kernel, out_shape, scratch_shapes, work, name, *args):
        return pl.pallas_call(
            functools.partial(kernel, per_kv, rank),
            in_specs=[smem, hbm, hbm] + [vmem] * (len(args) - 3),
            out_specs=[vmem] * len(out_shape),
            out_shape=out_shape,
            scratch_shapes=scratch_shapes,
            compiler_params=pltpu.CompilerParams(vmem_limit_bytes=VMEM_LIMIT),
            cost_estimate=pl.CostEstimate(
                flops=work * pairs * HEAD_SIZE, bytes_accessed=6 * tokens * width, transcendentals=pairs
            ),
            name=name,
        )(*args)

    queries, grads = (pltpu.with_memory_space_constraint(a, pltpu.HBM) for a in (queries, grads))
    common = (flags, queries, grads, terms, w_q, down, kv_own, kv_sib)

    def own():
        return call(
            own_kernel,
            [
                shape((rank, tokens), f32),
                shape((2 * tokens * kv_local, 2 * HEAD_SIZE), f32),
                shape((2 * tokens * kv_local, HEAD_SIZE), f32),
            ],
            scratch(2),
            40,
            "own_chip_heads",
            *common,
        )

    def previous(kv_pc, kv_px, own_grads, w_kv, down_win):
        grad_rows = rank + 2 * rank * kv_width // width
        return call(
            functools.partial(previous_kernel, scale),
            [
                shape((2, tokens, kv_width), f32),
                shape((2, tokens, kv_width), f32),
                shape((2, 2, tokens, kv_width), bf16),
                shape((rank, tokens), f32),
                shape((4 * rank, tokens), f32),
                shape((4 * rank, tokens), bf16),
                shape((grad_rows, width), bf16),
            ],
            [
                pltpu.VMEM((4 * tokens * kv_local, 2 * HEAD_SIZE), f32),
                pltpu.VMEM((4 * tokens * kv_local, HEAD_SIZE), f32),
                pltpu.VMEM((grad_rows, width), f32),
            ]
            + scratch(4),
            80,
            "previous_chip_heads",
            *common,
            kv_pc,
            kv_px,
            *own_grads,
            w_kv,
            down_win,
        )

    return own, previous


def exchanged(value, axis, bit):
    return lax.ppermute(value, axis, [(i, i ^ bit) for i in range(lax.axis_size(axis))])


def moved(value, axis, by):
    count = lax.axis_size(axis)
    return lax.ppermute(value, axis, [(i, (i + by) % count) for i in range(count)])


def summed(value, axis):
    bit = 1
    while bit < lax.axis_size(axis):
        value = value + exchanged(value, axis, bit)
        bit *= 2
    return value


def small_call(kernel, out_shape, *args, scratch=(), limit=1, work=0):
    vmem = pl.BlockSpec(memory_space=pltpu.VMEM)
    return pl.pallas_call(
        kernel,
        in_specs=[vmem] * len(args),
        out_specs=[vmem] * len(out_shape),
        out_shape=out_shape,
        scratch_shapes=list(scratch),
        compiler_params=pltpu.CompilerParams(vmem_limit_bytes=limit * SMALL_VMEM),
        cost_estimate=pl.CostEstimate(flops=work, bytes_accessed=1 << 20, transcendentals=0),
    )(*args)


def place(unit, radix):
    return lax.axis_index("seq") // unit % radix


def lanes(index, wide):
    return pl.ds(pl.multiple_of(index * wide, HEAD_SIZE), wide)


def projected_and_stacked(down_weight, inputs, key_rows, value_rows):
    rows, width = down_weight.shape
    tokens, kv_width = key_rows.shape
    steps = kv_width // HEAD_SIZE
    args = [
        pltpu.with_memory_space_constraint(a, pltpu.HBM)
        for a in (down_weight, inputs, key_rows, value_rows)
    ]

    def kernel(weight, tokens_in, key, value, down, kv):
        part = mm(weight[...], tokens_in[...], NT)

        @pl.when(pl.program_id(0) == 0)
        def _():
            down[...] = part

        @pl.when(pl.program_id(0) > 0)
        def _():
            down[...] += part

        kv[0] = key[...]
        kv[1] = value[...]

    def columns(high, wide):
        return pl.BlockSpec((high, wide // steps), lambda g: (0, g))

    return pl.pallas_call(
        kernel,
        grid=(steps,),
        in_specs=[
            columns(rows, width),
            columns(tokens, width),
            columns(tokens, kv_width),
            columns(tokens, kv_width),
        ],
        out_specs=[
            pl.BlockSpec((rows, tokens), lambda g: (0, 0)),
            pl.BlockSpec((2, tokens, kv_width // steps), lambda g: (0, 0, g)),
        ],
        out_shape=[
            jax.ShapeDtypeStruct((rows, tokens), jnp.float32),
            jax.ShapeDtypeStruct((2, tokens, kv_width), jnp.bfloat16),
        ],
        compiler_params=pltpu.CompilerParams(
            dimension_semantics=("arbitrary",), vmem_limit_bytes=2 * SMALL_VMEM
        ),
    )(*args)


def up_sums(up_q, up_keep, received):
    rank, tokens = up_q.shape

    def kernel(up_q, keep, other, mine, to_send, previous):
        total = keep[...] + other[...].astype(jnp.float32)
        own = jnp.concatenate([up_q[...], total[: 2 * rank]])
        mine[...] = own
        to_send[...] = own.astype(jnp.bfloat16)
        previous[...] = total[2 * rank :].astype(jnp.bfloat16)

    shape = jax.ShapeDtypeStruct
    return small_call(
        kernel,
        [
            shape((3 * rank, tokens), jnp.float32),
            shape((3 * rank, tokens), jnp.bfloat16),
            shape((2 * rank, tokens), jnp.bfloat16),
        ],
        up_q,
        up_keep,
        received,
    )


def up_terms(mine, to_send, previous):
    heads, count = lax.axis_size("head"), lax.axis_size("seq")
    nearby = moved(previous, "seq", -2)
    if heads == 2:
        pairs = [
            (s * heads + h, (s - 2) % count * heads + 1 - h) for s in range(count) for h in range(heads)
        ]
        return [mine, exchanged(to_send, "head", 1), nearby, lax.ppermute(previous, ("seq", "head"), pairs)]
    rank = mine.shape[0] - previous.shape[0]
    total = jnp.concatenate([mine[:rank], mine[rank:] + nearby.astype(jnp.float32)])
    bit = 1
    while 2 * bit < heads:
        total = total + exchanged(total.astype(jnp.bfloat16), "head", bit).astype(jnp.float32)
        bit *= 2
    return [total, exchanged(total.astype(jnp.bfloat16), "head", bit)]


def weight_halves(terms, inputs, grad_up, scale):
    width = inputs.shape[1]
    wide = width // 2
    up_rows, tokens = terms[0].shape
    rows = up_rows + grad_up.shape[0]
    given = len(terms)

    def kernel(*refs):
        tokens_in, grads, up_low, *out = refs[given:]
        up = jnp.zeros((up_rows, tokens), jnp.float32)
        for term in refs[:given]:
            value = term[...].astype(jnp.float32)
            if value.shape[0] < up_rows:
                value = jnp.concatenate(
                    [jnp.zeros((up_rows - value.shape[0], tokens), jnp.float32), value]
                )
            up = up + value
        up = up.astype(jnp.bfloat16)
        up_low[...] = up
        for d in range(2):
            at = lanes(place(1, 2) ^ d, wide)
            out[d][...] = jnp.concatenate(
                [mm(up, tokens_in[:, at]) * scale, grads[:, at].astype(jnp.float32)]
            ).astype(jnp.bfloat16)

    shape = jax.ShapeDtypeStruct
    return small_call(
        kernel,
        [shape((up_rows, tokens), jnp.bfloat16)] + [shape((rows, wide), jnp.bfloat16)] * 2,
        *terms,
        inputs,
        grad_up,
        limit=2,
    )


def exchanged_pieces(pieces, unit):
    return [pieces[0]] + [exchanged(p, "seq", d * unit) for d, p in enumerate(pieces) if d]


def summed_and_cut(pieces, unit, radix, work=0):
    rows, whole = pieces[0].shape
    wide = whole // radix
    if wide % HEAD_SIZE:
        total = sum(p.astype(jnp.float32) for p in pieces).astype(jnp.bfloat16)
        return [
            lax.dynamic_slice_in_dim(total, (place(unit, radix) ^ d) * wide, wide, 1)
            for d in range(radix)
        ]
    given = len(pieces)

    def kernel(*refs):
        total = refs[-1]
        total[...] = sum(p[...].astype(jnp.float32) for p in refs[:given])
        for d in range(radix):
            refs[given + d][...] = total[:, lanes(place(unit, radix) ^ d, wide)].astype(jnp.bfloat16)

    return small_call(
        kernel,
        [jax.ShapeDtypeStruct((rows, wide), jnp.bfloat16)] * radix,
        *pieces,
        scratch=[pltpu.VMEM((rows, whole), jnp.float32)],
        work=work,
    )


def joined(pieces, unit):
    rows, wide = pieces[0].shape
    radix = len(pieces)
    if wide % HEAD_SIZE:
        whole = jnp.zeros((rows, radix * wide), jnp.bfloat16)
        for d in range(radix):
            whole = lax.dynamic_update_slice_in_dim(
                whole, pieces[d], (place(unit, radix) ^ d) * wide, 1
            )
        return whole

    def kernel(*refs):
        for d in range(radix):
            refs[radix][:, lanes(place(unit, radix) ^ d, wide)] = refs[d][...]

    return small_call(kernel, [jax.ShapeDtypeStruct((rows, radix * wide), jnp.bfloat16)], *pieces)[0]


def joined_outputs(pieces, rank, kv_shape):
    rows, wide = pieces[0].shape
    extra = rows - 4 * rank
    each = wide // kv_shape[1]
    per_row = kv_shape[0] // extra

    def kernel(one, two, down, up_q, up_kv):
        for d, half in enumerate((one, two)):
            at = place(1, 2) ^ d
            piece = half[...].astype(jnp.float32)
            down[:, lanes(at, wide)] = piece[: 3 * rank]
            up_q[:, lanes(at, wide)] = piece[3 * rank : 4 * rank]
            for i in range(extra):
                for b in range(each):
                    up_kv[pl.ds(per_row * i + each * at + b, 1), :] = piece[
                        4 * rank + i : 4 * rank + i + 1, b * kv_shape[1] : (b + 1) * kv_shape[1]
                    ]

    shape = jax.ShapeDtypeStruct
    return small_call(
        kernel,
        [
            shape((3 * rank, 2 * wide), jnp.float32),
            shape((rank, 2 * wide), jnp.float32),
            shape(kv_shape, jnp.float32),
        ],
        *pieces,
    )


def per_device(
    queries,
    layer_key_rows,
    layer_value_rows,
    output_gradient,
    output_row_sums,
    shifted_head_flags,
    inputs,
    adapter_down_weight,
    query_up_weight,
    key_value_up_weight,
):
    seq_count = lax.axis_size("seq")
    tokens, width = queries.shape
    kv_width = layer_key_rows.shape[1]
    whole_len = tokens * seq_count
    rank = adapter_down_weight.shape[1]
    assert GROUP == 4 * tokens and SHIFT == 2 * tokens
    levels = (seq_count.bit_length() - 1) // 2
    assert 4**levels == seq_count
    flattened_down = adapter_down_weight.reshape(3 * rank, width)
    scale = adapter_scale / math.sqrt(whole_len)
    down_part, kv_own = projected_and_stacked(flattened_down, inputs, layer_key_rows, layer_value_rows)
    kv_pc = moved(kv_own, "seq", 2)
    kv_sib = exchanged(kv_own, "seq", 1)

    down_low = summed(down_part, "head").astype(jnp.bfloat16)
    down_tiled = jnp.tile(down_low[:rank].T, (1, HEAD_SIZE // rank))
    down_own = down_low[rank:]
    down_pc = moved(down_own, "seq", 2)

    own, previous = attention(
        scale,
        shifted_head_flags,
        queries,
        output_gradient,
        output_row_sums,
        query_up_weight,
        down_tiled,
        kv_own,
        kv_sib,
    )
    own_grads, kv_pc, down_pc = lax.optimization_barrier((own(), kv_pc, down_pc))
    kv_px = exchanged(kv_pc, "seq", 1)
    down_others = exchanged(jnp.concatenate([down_own, down_pc]), "seq", 1)
    down_win = jnp.concatenate(
        [down_others[: 2 * rank], down_own, down_pc, down_others[2 * rank :]], axis=1
    )
    keep_own, keep_pc, send, up_q, up_keep, up_send, grad_up = previous(
        kv_pc, kv_px, own_grads, key_value_up_weight, down_win
    )

    up_received, send = lax.optimization_barrier((exchanged(up_send, "seq", 1), send))
    received = exchanged(send, "seq", 1)
    terms = up_terms(*up_sums(up_q, up_keep, up_received))
    back = (keep_pc + received[1].astype(jnp.float32)).astype(jnp.bfloat16)
    terms[1], back = lax.optimization_barrier((terms[1], back))
    up_low, *pieces = weight_halves(terms, inputs, grad_up, scale)
    pieces, back = lax.optimization_barrier((summed_and_cut(exchanged_pieces(pieces, 1), 2, 2), back))
    pieces = exchanged_pieces(pieces, 2)
    back = moved(back, "seq", -2)
    for level in range(1, levels):
        pieces = exchanged_pieces(summed_and_cut(pieces, 4**level, 4, CUT_WORK), 4**level)
    total = sum(p.astype(jnp.float32) for p in pieces).astype(jnp.bfloat16)
    total, back = lax.optimization_barrier((total, back))
    key_value_gradient = (
        keep_own + received[0].astype(jnp.float32) + back.astype(jnp.float32)
    ).astype(jnp.bfloat16)
    grad_inputs = (
        adapter_scale
        * lax.dot_general(
            up_low, flattened_down, (((0,), (0,)), ((), ())), preferred_element_type=jnp.float32
        )
    ).astype(jnp.bfloat16)
    for level in range(levels - 1, 0, -1):
        total = joined(exchanged_pieces([total] * 4, 4**level), 4**level)
    total, grad_inputs = lax.optimization_barrier((total, grad_inputs))
    total = joined(exchanged_pieces([total] * 2, 2), 2)
    total, key_value_gradient = lax.optimization_barrier((total, key_value_gradient))
    down_gradient, grad_up_q, grad_up_kv = joined_outputs(
        exchanged_pieces([total] * 2, 1), rank, (2 * rank, kv_width)
    )
    return (
        grad_inputs,
        key_value_gradient,
        down_gradient.reshape(3, rank, width),
        grad_up_q,
        grad_up_kv.reshape(2, rank, kv_width),
    )


def solution(mesh):
    placed = (
        P("seq", "head"),
        P("seq", "head"),
        P("seq", "head"),
        P("seq", "head"),
        P("head", "seq"),
        P("head"),
        P("seq", "head"),
        P(None, None, "head"),
        P(None, "head"),
        P(None, None, "head"),
    )
    return jax.shard_map(
        per_device,
        mesh=mesh,
        in_specs=placed,
        out_specs=(
            P("seq", "head"),
            P(None, "seq", "head"),
            P(None, None, "head"),
            P(None, "head"),
            P(None, None, "head"),
        ),
        check_vma=False,
    )
```

```python
import functools
import math

import jax
import jax.numpy as jnp
from jax import lax
from jax.experimental import pallas as pl
from jax.experimental.pallas import tpu as pltpu
from jax.sharding import PartitionSpec as P

HEAD_SIZE = 128
GROUP = 1024
SHIFT = 512
CHUNK = 32
SMALL_VMEM = 8 * 1024 * 1024
VMEM_LIMIT = 32 * 1024 * 1024

adapter_scale = 2.0
masked_score = -1e30
score_scale = HEAD_SIZE ** (-0.5)
exp2_scale = score_scale * math.log2(math.e)

NT = (((1,), (1,)), ((), ()))
NN = (((1,), (0,)), ((), ()))


def mm(left, right, dims=NN):
    return lax.dot_general(left, right, dims, preferred_element_type=jnp.float32)


def heads_in_flight(blocks, rank, coming, current, last, valid, keys, values, q, do, term_ref, down, up_q, wk, dk, dv):
    tokens = q.shape[0]

    (_, column, key_column), (s_new, _, _, top_new, _) = coming
    query = q[:, column]

    (numbers, now_column, now_key), (s_ref, e_ref, ds_ref, top_ref, inv_ref) = current
    grad = do[:, now_column]
    term = term_ref[pl.ds(numbers[0], 1), :]
    top_now = top_ref[...]

    ((_, group, inner), last_column, _), (_, e_old, ds_old, _, inv_old) = last
    inverse = inv_old[...] * valid
    inverse_rows = jnp.broadcast_to(inverse, (HEAD_SIZE, tokens)).T
    scaled = inverse_rows * score_scale
    lane = lax.broadcasted_iota(jnp.int32, (tokens, HEAD_SIZE), 1) // rank
    own_columns = jnp.where(lane == inner, down[...].astype(jnp.float32), 0.0)
    grad_n = (do[:, last_column].astype(jnp.float32) * inverse_rows).astype(jnp.bfloat16)
    query_n = jnp.concatenate(
        [q[:, last_column].astype(jnp.float32) * scaled, own_columns * scaled], axis=1
    ).astype(jnp.bfloat16)
    own = pl.ds(pl.multiple_of(group * HEAD_SIZE + inner * rank, rank), rank)
    base = pl.multiple_of(group * wk.shape[1], tokens)

    top = None
    total = jnp.zeros((8, tokens), jnp.float32)
    back = None
    for block in blocks:
        rows = slice(block * tokens, (block + 1) * tokens)
        top = merged_top(top, scores_block(block, keys[block][:, key_column], query, s_new, rows))

        grad_probs = mm(values[block][:, now_key], grad, NT)
        for at in range(0, tokens, CHUNK):
            part = slice(block * tokens + at, block * tokens + at + CHUNK)
            weights = jnp.exp2((s_ref[part, :] - top_now) * exp2_scale)
            total = total + jnp.sum(weights.reshape(CHUNK // 8, 8, tokens), axis=0)
            e_ref[part, :] = weights.astype(jnp.bfloat16)
            ds_ref[part, :] = (weights * (grad_probs[at : at + CHUNK, :] - term)).astype(jnp.bfloat16)

        to = pl.ds(base + block * tokens, tokens)
        dv[to, :] += mm(e_old[rows, :], grad_n)
        dk[to, :] += mm(ds_old[rows, :], query_n)
        part = mm(wk[own, rows], ds_old[rows, :])
        back = part if back is None else back + part
    top_new[...] = jnp.max(top, axis=0, keepdims=True)
    inv_ref[...] = 1.0 / jnp.sum(total, axis=0, keepdims=True)
    up_q[...] += back * (inverse * score_scale)


def merged_top(top, here):
    return here if top is None else jnp.maximum(top, here)


def scores_block(block, key, query, s_ref, rows):
    tokens = query.shape[0]
    scores = mm(key, query, NT)
    if block == 1:
        key_row = lax.broadcasted_iota(jnp.int32, (tokens, tokens), 0)
        query_row = lax.broadcasted_iota(jnp.int32, (tokens, tokens), 1)
        scores = jnp.where(key_row <= query_row, scores, masked_score)
    s_ref[rows, :] = scores
    return jnp.max(scores.reshape(tokens // 8, 8, tokens), axis=0)


def last_gradients(blocks, rank, last, q, do, down, up_q, wk, dk, dv):
    tokens = q.shape[0]
    ((_, group, inner), column, _), (_, e_ref, ds_ref, _, inv_ref) = last
    low, high = blocks[0] * tokens, (blocks[-1] + 1) * tokens
    inverse = inv_ref[...]
    inverse_rows = jnp.broadcast_to(inverse, (HEAD_SIZE, tokens)).T
    scaled = inverse_rows * score_scale
    lane = lax.broadcasted_iota(jnp.int32, (tokens, HEAD_SIZE), 1) // rank
    own_columns = jnp.where(lane == inner, down[...].astype(jnp.float32), 0.0)
    grad_n = (do[:, column].astype(jnp.float32) * inverse_rows).astype(jnp.bfloat16)
    query_n = jnp.concatenate(
        [q[:, column].astype(jnp.float32) * scaled, own_columns * scaled], axis=1
    ).astype(jnp.bfloat16)
    rows = pl.ds(pl.multiple_of(group * wk.shape[1] + low, tokens), high - low)
    dv[rows, :] += mm(e_ref[low:high, :], grad_n)
    dk[rows, :] += mm(ds_ref[low:high, :], query_n)
    own = pl.ds(pl.multiple_of(group * HEAD_SIZE + inner * rank, rank), rank)
    up_q[...] += mm(wk[own, low:high], ds_ref[low:high, :]) * (inverse * score_scale)


def all_heads(
    with_previous, per_kv, rank, flags, keys, values, q_hbm, do_hbm, term, w_q, down, up_q, dk, dv, scratch
):
    listed, q, do, q_sem, do_sem, wk, *buffers = scratch
    tokens, width = q.shape
    groups = width // (per_kv * HEAD_SIZE)
    loads = []
    for g in range(groups):
        part = slice(g * per_kv * HEAD_SIZE, (g + 1) * per_kv * HEAD_SIZE)
        loads.append(
            [
                pltpu.make_async_copy(q_hbm.at[:, part], q.at[:, part], q_sem.at[g]),
                pltpu.make_async_copy(do_hbm.at[:, part], do.at[:, part], do_sem.at[g]),
            ]
        )
    for load in sum(loads, []):
        load.start()

    def wait(group):
        for load in loads[group]:
            load.wait()

    def wait_between(held, wanted):
        for g in range(1, groups):
            pl.when((g > held) & (g <= wanted))(functools.partial(wait, g))
        return jnp.maximum(held, wanted)

    height = wk.shape[1]
    for g in range(groups):
        stacked = jnp.concatenate(
            [w_q[:, h * HEAD_SIZE : (h + 1) * HEAD_SIZE] for h in range(g * per_kv, (g + 1) * per_kv)], axis=0
        )
        for block, key in enumerate(keys):
            wk[g * HEAD_SIZE : (g + 1) * HEAD_SIZE, block * tokens : (block + 1) * tokens] = mm(
                stacked, key[:, g * HEAD_SIZE : (g + 1) * HEAD_SIZE], NT
            ).astype(jnp.bfloat16)
    dk[...] = jnp.zeros_like(dk)
    dv[...] = jnp.zeros_like(dv)
    slots = (buffers[:5], buffers[5:])
    _, e_ref, ds_ref, _, inv_ref = slots[1]
    e_ref[...] = jnp.zeros_like(e_ref)
    ds_ref[...] = jnp.zeros_like(ds_ref)
    inv_ref[...] = jnp.zeros_like(inv_ref)
    wait(0)
    index = lax.axis_index("seq")
    core = index % 2
    half = index // 2 % 2
    count = jnp.int32(0)
    for h in range(groups * per_kv):
        listed[count] = jnp.int32(h)
        needs = flags[h] != half
        count = count + jnp.where(needs == with_previous, 1, 0).astype(jnp.int32)

    def head_at(i):
        h = listed[jnp.clip(i, 0, count - 1)]
        group = h // per_kv
        return (
            (h, group, h - group * per_kv),
            pl.ds(pl.multiple_of(h * HEAD_SIZE, HEAD_SIZE), HEAD_SIZE),
            pl.ds(pl.multiple_of(group * HEAD_SIZE, HEAD_SIZE), HEAD_SIZE),
        )

    for which in range(2):
        blocks = range(1 - which, len(keys))

        def step(i, slot, other):
            valid = jnp.where(i > 0, 1.0, 0.0).astype(jnp.float32)
            heads_in_flight(
                blocks, rank, (head_at(i + 1), other), (head_at(i), slot), (head_at(i - 1), other), valid,
                keys, values, q, do, term, down, up_q, wk, dk, dv,
            )

        def finish(slot):
            last_gradients(blocks, rank, (head_at(count - 1), slot), q, do, down, up_q, wk, dk, dv)

        @pl.when((core == which) & (count > 0))
        def _():
            held = wait_between(jnp.int32(0), head_at(0)[0][1])
            s_ref, _, _, top_ref, _ = slots[0]
            _, column, key_column = head_at(0)
            top = None
            for block in blocks:
                rows = slice(block * tokens, (block + 1) * tokens)
                top = merged_top(
                    top, scores_block(block, keys[block][:, key_column], q[:, column], s_ref, rows)
                )
            top_ref[...] = jnp.max(top, axis=0, keepdims=True)

            def two(t, held):
                held = wait_between(held, head_at(2 * t + 2)[0][1])
                step(2 * t, *slots)
                step(2 * t + 1, *slots[::-1])
                return held

            held = lax.fori_loop(0, count // 2, two, held)
            wait_between(held, jnp.int32(groups - 1))

            @pl.when(count % 2 == 1)
            def _():
                step(count - 1, *slots)
                finish(slots[0])

            @pl.when(count % 2 == 0)
            def _():
                finish(slots[1])

    @pl.when(count == 0)
    def _():
        wait_between(jnp.int32(0), jnp.int32(groups - 1))


def own_kernel(
    per_kv, rank, flags, q, do, term, w_q, down, kv_own, kv_sib, up_q, dk, dv, *scratch
):
    up_q[...] = jnp.zeros_like(up_q)
    keys, values = ([kv.at[c] for kv in (kv_sib, kv_own)] for c in range(2))
    all_heads(False, per_kv, rank, flags, keys, values, q, do, term, w_q, down, up_q, dk, dv, scratch)


def previous_kernel(
    scale, per_kv, rank, flags, q, do, term, w_q, down, kv_own, kv_sib, kv_pc, kv_px,
    up_q_own, dk_own, dv_own, w_kv, down_win,
    keep_own, keep_pc, send, up_q, up_keep, up_send, grad_up,
    dk, dv, grads, *scratch,
):
    tokens = q.shape[0]
    up_q[...] = up_q_own[...]
    keys, values = ([kv.at[c] for kv in (kv_sib, kv_own, kv_pc, kv_px)] for c in range(2))
    all_heads(True, per_kv, rank, flags, keys, values, q, do, term, w_q, down, up_q, dk, dv, scratch)
    up_kv = [jnp.zeros((rank, 4 * tokens), jnp.float32) for _ in range(2)]
    kv_width = kv_own.shape[2]
    for g in range(kv_width // HEAD_SIZE):
        columns = slice(g * HEAD_SIZE, (g + 1) * HEAD_SIZE)
        low_row, own_row = g * 4 * tokens, g * 2 * tokens
        by_head = None
        for block in range(4):
            tail = dk[low_row + block * tokens : low_row + (block + 1) * tokens, HEAD_SIZE:]
            if block < 2:
                tail = tail + dk_own[own_row + block * tokens : own_row + (block + 1) * tokens, HEAD_SIZE:]
            part = mm(tail.T.astype(jnp.bfloat16), keys[block][:, columns])
            by_head = part if by_head is None else by_head + part
        for h in range(per_kv):
            at = (g * per_kv + h) * HEAD_SIZE
            grads[:rank, at : at + HEAD_SIZE] = by_head[h * rank : (h + 1) * rank, :]
        for c, acc, start in ((0, dk, dk_own), (1, dv, dv_own)):
            total = acc[low_row : low_row + 4 * tokens, :HEAD_SIZE]
            near = total[: 2 * tokens] + start[own_row : own_row + 2 * tokens, :HEAD_SIZE]
            low = jnp.concatenate([near, total[2 * tokens :]]).astype(jnp.bfloat16)
            keep_own[c, :, columns] = near[tokens:]
            keep_pc[c, :, columns] = total[2 * tokens : 3 * tokens]
            send[0, c, :, columns] = low[:tokens]
            send[1, c, :, columns] = low[3 * tokens :]
            up_kv[c] = up_kv[c] + mm(w_kv[c, :, columns], low, NT)
            own = slice(c * rank, (c + 1) * rank)
            grad_kv = mm(down_win[own, :], low)
            for r in range(rank):
                row, at = divmod((c * rank + r) * kv_width + g * HEAD_SIZE, grads.shape[1])
                grads[rank + row : rank + row + 1, at : at + HEAD_SIZE] = grad_kv[r : r + 1, :]
    sib, near, pc, px = (
        jnp.concatenate([up_kv[c][:, block * tokens : (block + 1) * tokens] for c in range(2)])
        for block in range(4)
    )
    grad_up[...] = (grads[...] * scale).astype(jnp.bfloat16)
    up_keep[...] = jnp.concatenate([near, pc])
    up_send[...] = jnp.concatenate([sib, px]).astype(jnp.bfloat16)


def attention(scale, flags, queries, grads, terms, w_q, down, kv_own, kv_sib):
    tokens, width = queries.shape
    kv_width = kv_own.shape[2]
    kv_local = kv_width // HEAD_SIZE
    per_kv = width // kv_width
    rank = w_q.shape[0]
    assert per_kv * rank == HEAD_SIZE
    f32, bf16 = jnp.float32, jnp.bfloat16
    shape = jax.ShapeDtypeStruct
    pairs = kv_local * per_kv * tokens * tokens
    smem = pl.BlockSpec(memory_space=pltpu.SMEM)
    vmem = pl.BlockSpec(memory_space=pltpu.VMEM)
    hbm = pl.BlockSpec(memory_space=pltpu.HBM)

    def scratch(blocks):
        rows = blocks * tokens
        slot = [
            pltpu.VMEM((rows, tokens), f32),
            pltpu.VMEM((rows, tokens), bf16),
            pltpu.VMEM((rows, tokens), bf16),
            pltpu.VMEM((1, tokens), f32),
            pltpu.VMEM((1, tokens), f32),
        ]
        return [
            pltpu.SMEM((kv_local * per_kv + 1,), jnp.int32),
            pltpu.VMEM((tokens, width), bf16),
            pltpu.VMEM((tokens, width), bf16),
            pltpu.SemaphoreType.DMA((kv_local,)),
            pltpu.SemaphoreType.DMA((kv_local,)),
            pltpu.VMEM((kv_local * HEAD_SIZE, rows), bf16),
        ] + slot * 2

    def call(kernel, out_shape, scratch_shapes, work, name, *args):
        return pl.pallas_call(
            functools.partial(kernel, per_kv, rank),
            in_specs=[smem, hbm, hbm] + [vmem] * (len(args) - 3),
            out_specs=[vmem] * len(out_shape),
            out_shape=out_shape,
            scratch_shapes=scratch_shapes,
            compiler_params=pltpu.CompilerParams(vmem_limit_bytes=VMEM_LIMIT),
            cost_estimate=pl.CostEstimate(
                flops=work * pairs * HEAD_SIZE, bytes_accessed=6 * tokens * width, transcendentals=pairs
            ),
            name=name,
        )(*args)

    queries, grads = (pltpu.with_memory_space_constraint(a, pltpu.HBM) for a in (queries, grads))
    common = (flags, queries, grads, terms, w_q, down, kv_own, kv_sib)

    def own():
        return call(
            own_kernel,
            [
                shape((rank, tokens), f32),
                shape((2 * tokens * kv_local, 2 * HEAD_SIZE), f32),
                shape((2 * tokens * kv_local, HEAD_SIZE), f32),
            ],
            scratch(2),
            40,
            "own_chip_heads",
            *common,
        )

    def previous(kv_pc, kv_px, own_grads, w_kv, down_win):
        grad_rows = rank + 2 * rank * kv_width // width
        return call(
            functools.partial(previous_kernel, scale),
            [
                shape((2, tokens, kv_width), f32),
                shape((2, tokens, kv_width), f32),
                shape((2, 2, tokens, kv_width), bf16),
                shape((rank, tokens), f32),
                shape((4 * rank, tokens), f32),
                shape((4 * rank, tokens), bf16),
                shape((grad_rows, width), bf16),
            ],
            [
                pltpu.VMEM((4 * tokens * kv_local, 2 * HEAD_SIZE), f32),
                pltpu.VMEM((4 * tokens * kv_local, HEAD_SIZE), f32),
                pltpu.VMEM((grad_rows, width), f32),
            ]
            + scratch(4),
            80,
            "previous_chip_heads",
            *common,
            kv_pc,
            kv_px,
            *own_grads,
            w_kv,
            down_win,
        )

    return own, previous


def exchanged(value, axis, bit):
    return lax.ppermute(value, axis, [(i, i ^ bit) for i in range(lax.axis_size(axis))])


def moved(value, axis, by):
    count = lax.axis_size(axis)
    return lax.ppermute(value, axis, [(i, (i + by) % count) for i in range(count)])


def summed(value, axis):
    bit = 1
    while bit < lax.axis_size(axis):
        value = value + exchanged(value, axis, bit)
        bit *= 2
    return value


def small_call(kernel, out_shape, *args, scratch=(), limit=1):
    vmem = pl.BlockSpec(memory_space=pltpu.VMEM)
    return pl.pallas_call(
        kernel,
        in_specs=[vmem] * len(args),
        out_specs=[vmem] * len(out_shape),
        out_shape=out_shape,
        scratch_shapes=list(scratch),
        compiler_params=pltpu.CompilerParams(vmem_limit_bytes=limit * SMALL_VMEM),
    )(*args)


def place(unit, radix):
    return lax.axis_index("seq") // unit % radix


def lanes(index, wide):
    return pl.ds(pl.multiple_of(index * wide, HEAD_SIZE), wide)


def projected_and_stacked(down_weight, inputs, key_rows, value_rows):
    rows, width = down_weight.shape
    tokens, kv_width = key_rows.shape
    steps = kv_width // HEAD_SIZE
    args = [
        pltpu.with_memory_space_constraint(a, pltpu.HBM)
        for a in (down_weight, inputs, key_rows, value_rows)
    ]

    def kernel(weight, tokens_in, key, value, down, kv):
        part = mm(weight[...], tokens_in[...], NT)

        @pl.when(pl.program_id(0) == 0)
        def _():
            down[...] = part

        @pl.when(pl.program_id(0) > 0)
        def _():
            down[...] += part

        kv[0] = key[...]
        kv[1] = value[...]

    def columns(high, wide):
        return pl.BlockSpec((high, wide // steps), lambda g: (0, g))

    return pl.pallas_call(
        kernel,
        grid=(steps,),
        in_specs=[
            columns(rows, width),
            columns(tokens, width),
            columns(tokens, kv_width),
            columns(tokens, kv_width),
        ],
        out_specs=[
            pl.BlockSpec((rows, tokens), lambda g: (0, 0)),
            pl.BlockSpec((2, tokens, kv_width // steps), lambda g: (0, 0, g)),
        ],
        out_shape=[
            jax.ShapeDtypeStruct((rows, tokens), jnp.float32),
            jax.ShapeDtypeStruct((2, tokens, kv_width), jnp.bfloat16),
        ],
        compiler_params=pltpu.CompilerParams(
            dimension_semantics=("arbitrary",), vmem_limit_bytes=2 * SMALL_VMEM
        ),
    )(*args)


def up_sums(up_q, up_keep, received):
    rank, tokens = up_q.shape

    def kernel(up_q, keep, other, mine, to_send, previous):
        total = keep[...] + other[...].astype(jnp.float32)
        own = jnp.concatenate([up_q[...], total[: 2 * rank]])
        mine[...] = own
        to_send[...] = own.astype(jnp.bfloat16)
        previous[...] = total[2 * rank :].astype(jnp.bfloat16)

    shape = jax.ShapeDtypeStruct
    return small_call(
        kernel,
        [
            shape((3 * rank, tokens), jnp.float32),
            shape((3 * rank, tokens), jnp.bfloat16),
            shape((2 * rank, tokens), jnp.bfloat16),
        ],
        up_q,
        up_keep,
        received,
    )


def up_terms(mine, to_send, previous):
    heads, count = lax.axis_size("head"), lax.axis_size("seq")
    nearby = moved(previous, "seq", -2)
    if heads == 2:
        pairs = [
            (s * heads + h, (s - 2) % count * heads + 1 - h) for s in range(count) for h in range(heads)
        ]
        return [mine, exchanged(to_send, "head", 1), nearby, lax.ppermute(previous, ("seq", "head"), pairs)]
    rank = mine.shape[0] - previous.shape[0]
    total = jnp.concatenate([mine[:rank], mine[rank:] + nearby.astype(jnp.float32)])
    bit = 1
    while 2 * bit < heads:
        total = total + exchanged(total.astype(jnp.bfloat16), "head", bit).astype(jnp.float32)
        bit *= 2
    return [total, exchanged(total.astype(jnp.bfloat16), "head", bit)]


def weight_halves(terms, inputs, grad_up, scale):
    width = inputs.shape[1]
    wide = width // 2
    up_rows, tokens = terms[0].shape
    rows = up_rows + grad_up.shape[0]
    given = len(terms)

    def kernel(*refs):
        tokens_in, grads, up_low, *out = refs[given:]
        up = jnp.zeros((up_rows, tokens), jnp.float32)
        for term in refs[:given]:
            value = term[...].astype(jnp.float32)
            if value.shape[0] < up_rows:
                value = jnp.concatenate(
                    [jnp.zeros((up_rows - value.shape[0], tokens), jnp.float32), value]
                )
            up = up + value
        up = up.astype(jnp.bfloat16)
        up_low[...] = up
        for d in range(2):
            at = lanes(place(1, 2) ^ d, wide)
            out[d][...] = jnp.concatenate(
                [mm(up, tokens_in[:, at]) * scale, grads[:, at].astype(jnp.float32)]
            ).astype(jnp.bfloat16)

    shape = jax.ShapeDtypeStruct
    return small_call(
        kernel,
        [shape((up_rows, tokens), jnp.bfloat16)] + [shape((rows, wide), jnp.bfloat16)] * 2,
        *terms,
        inputs,
        grad_up,
        limit=2,
    )


def exchanged_pieces(pieces, unit):
    return [pieces[0]] + [exchanged(p, "seq", d * unit) for d, p in enumerate(pieces) if d]


def summed_and_cut(pieces, unit, radix):
    rows, whole = pieces[0].shape
    wide = whole // radix
    if wide % HEAD_SIZE:
        total = sum(p.astype(jnp.float32) for p in pieces).astype(jnp.bfloat16)
        return [
            lax.dynamic_slice_in_dim(total, (place(unit, radix) ^ d) * wide, wide, 1)
            for d in range(radix)
        ]
    given = len(pieces)

    def kernel(*refs):
        total = refs[-1]
        total[...] = sum(p[...].astype(jnp.float32) for p in refs[:given])
        for d in range(radix):
            refs[given + d][...] = total[:, lanes(place(unit, radix) ^ d, wide)].astype(jnp.bfloat16)

    return small_call(
        kernel,
        [jax.ShapeDtypeStruct((rows, wide), jnp.bfloat16)] * radix,
        *pieces,
        scratch=[pltpu.VMEM((rows, whole), jnp.float32)],
    )


def joined(pieces, unit):
    rows, wide = pieces[0].shape
    radix = len(pieces)
    if wide % HEAD_SIZE:
        whole = jnp.zeros((rows, radix * wide), jnp.bfloat16)
        for d in range(radix):
            whole = lax.dynamic_update_slice_in_dim(
                whole, pieces[d], (place(unit, radix) ^ d) * wide, 1
            )
        return whole

    def kernel(*refs):
        for d in range(radix):
            refs[radix][:, lanes(place(unit, radix) ^ d, wide)] = refs[d][...]

    return small_call(kernel, [jax.ShapeDtypeStruct((rows, radix * wide), jnp.bfloat16)], *pieces)[0]


def joined_outputs(pieces, rank, kv_shape):
    rows, wide = pieces[0].shape
    extra = rows - 4 * rank
    each = wide // kv_shape[1]
    per_row = kv_shape[0] // extra

    def kernel(one, two, down, up_q, up_kv):
        for d, half in enumerate((one, two)):
            at = place(1, 2) ^ d
            piece = half[...].astype(jnp.float32)
            down[:, lanes(at, wide)] = piece[: 3 * rank]
            up_q[:, lanes(at, wide)] = piece[3 * rank : 4 * rank]
            for i in range(extra):
                for b in range(each):
                    up_kv[pl.ds(per_row * i + each * at + b, 1), :] = piece[
                        4 * rank + i : 4 * rank + i + 1, b * kv_shape[1] : (b + 1) * kv_shape[1]
                    ]

    shape = jax.ShapeDtypeStruct
    return small_call(
        kernel,
        [
            shape((3 * rank, 2 * wide), jnp.float32),
            shape((rank, 2 * wide), jnp.float32),
            shape(kv_shape, jnp.float32),
        ],
        *pieces,
    )


def per_device(
    queries,
    layer_key_rows,
    layer_value_rows,
    output_gradient,
    output_row_sums,
    shifted_head_flags,
    inputs,
    adapter_down_weight,
    query_up_weight,
    key_value_up_weight,
):
    seq_count = lax.axis_size("seq")
    tokens, width = queries.shape
    kv_width = layer_key_rows.shape[1]
    whole_len = tokens * seq_count
    rank = adapter_down_weight.shape[1]
    assert GROUP == 4 * tokens and SHIFT == 2 * tokens
    levels = (seq_count.bit_length() - 1) // 2
    assert 4**levels == seq_count
    flattened_down = adapter_down_weight.reshape(3 * rank, width)
    scale = adapter_scale / math.sqrt(whole_len)
    down_part, kv_own = projected_and_stacked(flattened_down, inputs, layer_key_rows, layer_value_rows)
    kv_pc = moved(kv_own, "seq", 2)
    kv_sib = exchanged(kv_own, "seq", 1)

    down_low = summed(down_part, "head").astype(jnp.bfloat16)
    down_tiled = jnp.tile(down_low[:rank].T, (1, HEAD_SIZE // rank))
    down_own = down_low[rank:]
    down_pc = moved(down_own, "seq", 2)

    own, previous = attention(
        scale,
        shifted_head_flags,
        queries,
        output_gradient,
        output_row_sums,
        query_up_weight,
        down_tiled,
        kv_own,
        kv_sib,
    )
    own_grads, kv_pc, down_pc = lax.optimization_barrier((own(), kv_pc, down_pc))
    kv_px = exchanged(kv_pc, "seq", 1)
    down_others = exchanged(jnp.concatenate([down_own, down_pc]), "seq", 1)
    down_win = jnp.concatenate(
        [down_others[: 2 * rank], down_own, down_pc, down_others[2 * rank :]], axis=1
    )
    keep_own, keep_pc, send, up_q, up_keep, up_send, grad_up = previous(
        kv_pc, kv_px, own_grads, key_value_up_weight, down_win
    )

    up_received, send = lax.optimization_barrier((exchanged(up_send, "seq", 1), send))
    received = exchanged(send, "seq", 1)
    terms = up_terms(*up_sums(up_q, up_keep, up_received))
    back = (keep_pc + received[1].astype(jnp.float32)).astype(jnp.bfloat16)
    up_low, *pieces = weight_halves(terms, inputs, grad_up, scale)
    pieces = exchanged_pieces(summed_and_cut(exchanged_pieces(pieces, 1), 2, 2), 2)
    pieces, back = lax.optimization_barrier((pieces, back))
    back = moved(back, "seq", -2)
    for level in range(1, levels):
        pieces = exchanged_pieces(summed_and_cut(pieces, 4**level, 4), 4**level)
    total = sum(p.astype(jnp.float32) for p in pieces).astype(jnp.bfloat16)
    grad_inputs = (
        adapter_scale
        * lax.dot_general(
            up_low, flattened_down, (((0,), (0,)), ((), ())), preferred_element_type=jnp.float32
        )
    ).astype(jnp.bfloat16)
    for level in range(levels - 1, 0, -1):
        total = joined(exchanged_pieces([total] * 4, 4**level), 4**level)
    total, grad_inputs, back = lax.optimization_barrier((total, grad_inputs, back))
    key_value_gradient = (
        keep_own + received[0].astype(jnp.float32) + back.astype(jnp.float32)
    ).astype(jnp.bfloat16)
    total = joined(exchanged_pieces([total] * 2, 2), 2)
    total, key_value_gradient = lax.optimization_barrier((total, key_value_gradient))
    down_gradient, grad_up_q, grad_up_kv = joined_outputs(
        exchanged_pieces([total] * 2, 1), rank, (2 * rank, kv_width)
    )
    return (
        grad_inputs,
        key_value_gradient,
        down_gradient.reshape(3, rank, width),
        grad_up_q,
        grad_up_kv.reshape(2, rank, kv_width),
    )


def solution(mesh):
    placed = (
        P("seq", "head"),
        P("seq", "head"),
        P("seq", "head"),
        P("seq", "head"),
        P("head", "seq"),
        P("head"),
        P("seq", "head"),
        P(None, None, "head"),
        P(None, "head"),
        P(None, None, "head"),
    )
    return jax.shard_map(
        per_device,
        mesh=mesh,
        in_specs=placed,
        out_specs=(
            P("seq", "head"),
            P(None, "seq", "head"),
            P(None, None, "head"),
            P(None, "head"),
            P(None, None, "head"),
        ),
        check_vma=False,
    )
```

```python
import functools
import math

import jax
import jax.numpy as jnp
from jax import lax
from jax.experimental import pallas as pl
from jax.experimental.pallas import tpu as pltpu
from jax.sharding import PartitionSpec as P

HEAD_SIZE = 128
GROUP = 1024
SHIFT = 512
CHUNK = 32
SMALL_VMEM = 8 * 1024 * 1024
VMEM_LIMIT = 32 * 1024 * 1024

adapter_scale = 2.0
masked_score = -1e30
score_scale = HEAD_SIZE ** (-0.5)
exp2_scale = score_scale * math.log2(math.e)

NT = (((1,), (1,)), ((), ()))
NN = (((1,), (0,)), ((), ()))


def mm(left, right, dims=NN):
    return lax.dot_general(left, right, dims, preferred_element_type=jnp.float32)


def heads_in_flight(blocks, rank, coming, current, last, valid, keys, values, q, do, term_ref, down, up_q, wk, dk, dv):
    tokens = q.shape[0]

    (_, column, key_column), (s_new, _, _, top_new, _) = coming
    query = q[:, column]

    (numbers, now_column, now_key), (s_ref, e_ref, ds_ref, top_ref, inv_ref) = current
    grad = do[:, now_column]
    term = term_ref[pl.ds(numbers[0], 1), :]
    top_now = top_ref[...]

    ((_, group, inner), last_column, _), (_, e_old, ds_old, _, inv_old) = last
    inverse = inv_old[...] * valid
    inverse_rows = jnp.broadcast_to(inverse, (HEAD_SIZE, tokens)).T
    scaled = inverse_rows * score_scale
    lane = lax.broadcasted_iota(jnp.int32, (tokens, HEAD_SIZE), 1) // rank
    own_columns = jnp.where(lane == inner, down[...].astype(jnp.float32), 0.0)
    grad_n = (do[:, last_column].astype(jnp.float32) * inverse_rows).astype(jnp.bfloat16)
    query_n = jnp.concatenate(
        [q[:, last_column].astype(jnp.float32) * scaled, own_columns * scaled], axis=1
    ).astype(jnp.bfloat16)
    own = pl.ds(pl.multiple_of(group * HEAD_SIZE + inner * rank, rank), rank)
    base = pl.multiple_of(group * wk.shape[1], tokens)

    top = None
    total = jnp.zeros((8, tokens), jnp.float32)
    back = None
    waiting = []
    for block in blocks:
        rows = slice(block * tokens, (block + 1) * tokens)
        top = merged_top(top, scores_block(block, keys[block][:, key_column], query, s_new, rows))

        grad_probs = mm(values[block][:, now_key], grad, NT)
        for at in range(0, tokens, CHUNK):
            part = slice(block * tokens + at, block * tokens + at + CHUNK)
            weights = jnp.exp2((s_ref[part, :] - top_now) * exp2_scale)
            total = total + jnp.sum(weights.reshape(CHUNK // 8, 8, tokens), axis=0)
            e_ref[part, :] = weights.astype(jnp.bfloat16)
            ds_ref[part, :] = (weights * (grad_probs[at : at + CHUNK, :] - term)).astype(jnp.bfloat16)

        waiting.append(block)
        if len(waiting) < 2 and block != blocks[-1]:
            continue
        rows = slice(waiting[0] * tokens, (block + 1) * tokens)
        to = pl.ds(base + rows.start, rows.stop - rows.start)
        dv[to, :] += mm(e_old[rows, :], grad_n)
        dk[to, :] += mm(ds_old[rows, :], query_n)
        part = mm(wk[own, rows], ds_old[rows, :])
        back = part if back is None else back + part
        waiting = []
    top_new[...] = jnp.max(top, axis=0, keepdims=True)
    inv_ref[...] = 1.0 / jnp.sum(total, axis=0, keepdims=True)
    up_q[...] += back * (inverse * score_scale)


def merged_top(top, here):
    return here if top is None else jnp.maximum(top, here)


def scores_block(block, key, query, s_ref, rows):
    tokens = query.shape[0]
    scores = mm(key, query, NT)
    if block == 1:
        key_row = lax.broadcasted_iota(jnp.int32, (tokens, tokens), 0)
        query_row = lax.broadcasted_iota(jnp.int32, (tokens, tokens), 1)
        scores = jnp.where(key_row <= query_row, scores, masked_score)
    s_ref[rows, :] = scores
    return jnp.max(scores.reshape(tokens // 8, 8, tokens), axis=0)


def last_gradients(blocks, rank, last, q, do, down, up_q, wk, dk, dv):
    tokens = q.shape[0]
    ((_, group, inner), column, _), (_, e_ref, ds_ref, _, inv_ref) = last
    low, high = blocks[0] * tokens, (blocks[-1] + 1) * tokens
    inverse = inv_ref[...]
    inverse_rows = jnp.broadcast_to(inverse, (HEAD_SIZE, tokens)).T
    scaled = inverse_rows * score_scale
    lane = lax.broadcasted_iota(jnp.int32, (tokens, HEAD_SIZE), 1) // rank
    own_columns = jnp.where(lane == inner, down[...].astype(jnp.float32), 0.0)
    grad_n = (do[:, column].astype(jnp.float32) * inverse_rows).astype(jnp.bfloat16)
    query_n = jnp.concatenate(
        [q[:, column].astype(jnp.float32) * scaled, own_columns * scaled], axis=1
    ).astype(jnp.bfloat16)
    rows = pl.ds(pl.multiple_of(group * wk.shape[1] + low, tokens), high - low)
    dv[rows, :] += mm(e_ref[low:high, :], grad_n)
    dk[rows, :] += mm(ds_ref[low:high, :], query_n)
    own = pl.ds(pl.multiple_of(group * HEAD_SIZE + inner * rank, rank), rank)
    up_q[...] += mm(wk[own, low:high], ds_ref[low:high, :]) * (inverse * score_scale)


def all_heads(
    with_previous, per_kv, rank, flags, keys, values, q_hbm, do_hbm, term, w_q, down, up_q, dk, dv, scratch
):
    listed, q, do, q_sem, do_sem, wk, *buffers = scratch
    tokens, width = q.shape
    groups = width // (per_kv * HEAD_SIZE)
    loads = []
    for g in range(groups):
        part = slice(g * per_kv * HEAD_SIZE, (g + 1) * per_kv * HEAD_SIZE)
        loads.append(
            [
                pltpu.make_async_copy(q_hbm.at[:, part], q.at[:, part], q_sem.at[g]),
                pltpu.make_async_copy(do_hbm.at[:, part], do.at[:, part], do_sem.at[g]),
            ]
        )
    for load in sum(loads, []):
        load.start()

    def wait(group):
        for load in loads[group]:
            load.wait()

    def wait_between(held, wanted):
        for g in range(1, groups):
            pl.when((g > held) & (g <= wanted))(functools.partial(wait, g))
        return jnp.maximum(held, wanted)

    height = wk.shape[1]
    for g in range(groups):
        stacked = jnp.concatenate(
            [w_q[:, h * HEAD_SIZE : (h + 1) * HEAD_SIZE] for h in range(g * per_kv, (g + 1) * per_kv)], axis=0
        )
        for block, key in enumerate(keys):
            wk[g * HEAD_SIZE : (g + 1) * HEAD_SIZE, block * tokens : (block + 1) * tokens] = mm(
                stacked, key[:, g * HEAD_SIZE : (g + 1) * HEAD_SIZE], NT
            ).astype(jnp.bfloat16)
    dk[...] = jnp.zeros_like(dk)
    dv[...] = jnp.zeros_like(dv)
    slots = (buffers[:5], buffers[5:])
    _, e_ref, ds_ref, _, inv_ref = slots[1]
    e_ref[...] = jnp.zeros_like(e_ref)
    ds_ref[...] = jnp.zeros_like(ds_ref)
    inv_ref[...] = jnp.zeros_like(inv_ref)
    wait(0)
    index = lax.axis_index("seq")
    core = index % 2
    half = index // 2 % 2
    count = jnp.int32(0)
    for h in range(groups * per_kv):
        listed[count] = jnp.int32(h)
        needs = flags[h] != half
        count = count + jnp.where(needs == with_previous, 1, 0).astype(jnp.int32)

    def head_at(i):
        h = listed[jnp.clip(i, 0, count - 1)]
        group = h // per_kv
        return (
            (h, group, h - group * per_kv),
            pl.ds(pl.multiple_of(h * HEAD_SIZE, HEAD_SIZE), HEAD_SIZE),
            pl.ds(pl.multiple_of(group * HEAD_SIZE, HEAD_SIZE), HEAD_SIZE),
        )

    for which in range(2):
        blocks = range(1 - which, len(keys))

        def step(i, slot, other):
            valid = jnp.where(i > 0, 1.0, 0.0).astype(jnp.float32)
            heads_in_flight(
                blocks, rank, (head_at(i + 1), other), (head_at(i), slot), (head_at(i - 1), other), valid,
                keys, values, q, do, term, down, up_q, wk, dk, dv,
            )

        def finish(slot):
            last_gradients(blocks, rank, (head_at(count - 1), slot), q, do, down, up_q, wk, dk, dv)

        @pl.when((core == which) & (count > 0))
        def _():
            held = wait_between(jnp.int32(0), head_at(0)[0][1])
            s_ref, _, _, top_ref, _ = slots[0]
            _, column, key_column = head_at(0)
            top = None
            for block in blocks:
                rows = slice(block * tokens, (block + 1) * tokens)
                top = merged_top(
                    top, scores_block(block, keys[block][:, key_column], q[:, column], s_ref, rows)
                )
            top_ref[...] = jnp.max(top, axis=0, keepdims=True)

            def two(t, held):
                held = wait_between(held, head_at(2 * t + 2)[0][1])
                step(2 * t, *slots)
                step(2 * t + 1, *slots[::-1])
                return held

            held = lax.fori_loop(0, count // 2, two, held)
            wait_between(held, jnp.int32(groups - 1))

            @pl.when(count % 2 == 1)
            def _():
                step(count - 1, *slots)
                finish(slots[0])

            @pl.when(count % 2 == 0)
            def _():
                finish(slots[1])

    @pl.when(count == 0)
    def _():
        wait_between(jnp.int32(0), jnp.int32(groups - 1))


def own_kernel(
    per_kv, rank, flags, q, do, term, w_q, down, kv_own, kv_sib, up_q, dk, dv, *scratch
):
    up_q[...] = jnp.zeros_like(up_q)
    keys, values = ([kv.at[c] for kv in (kv_sib, kv_own)] for c in range(2))
    all_heads(False, per_kv, rank, flags, keys, values, q, do, term, w_q, down, up_q, dk, dv, scratch)


def previous_kernel(
    scale, per_kv, rank, flags, q, do, term, w_q, down, kv_own, kv_sib, kv_pc, kv_px,
    up_q_own, dk_own, dv_own, w_kv, down_win,
    keep_own, keep_pc, send, up_q, up_keep, up_send, grad_up,
    dk, dv, grads, *scratch,
):
    tokens = q.shape[0]
    up_q[...] = up_q_own[...]
    keys, values = ([kv.at[c] for kv in (kv_sib, kv_own, kv_pc, kv_px)] for c in range(2))
    all_heads(True, per_kv, rank, flags, keys, values, q, do, term, w_q, down, up_q, dk, dv, scratch)
    up_kv = [jnp.zeros((rank, 4 * tokens), jnp.float32) for _ in range(2)]
    kv_width = kv_own.shape[2]
    for g in range(kv_width // HEAD_SIZE):
        columns = slice(g * HEAD_SIZE, (g + 1) * HEAD_SIZE)
        low_row, own_row = g * 4 * tokens, g * 2 * tokens
        by_head = None
        for block in range(4):
            tail = dk[low_row + block * tokens : low_row + (block + 1) * tokens, HEAD_SIZE:]
            if block < 2:
                tail = tail + dk_own[own_row + block * tokens : own_row + (block + 1) * tokens, HEAD_SIZE:]
            part = mm(tail.T.astype(jnp.bfloat16), keys[block][:, columns])
            by_head = part if by_head is None else by_head + part
        for h in range(per_kv):
            at = (g * per_kv + h) * HEAD_SIZE
            grads[:rank, at : at + HEAD_SIZE] = by_head[h * rank : (h + 1) * rank, :]
        for c, acc, start in ((0, dk, dk_own), (1, dv, dv_own)):
            total = acc[low_row : low_row + 4 * tokens, :HEAD_SIZE]
            near = total[: 2 * tokens] + start[own_row : own_row + 2 * tokens, :HEAD_SIZE]
            low = jnp.concatenate([near, total[2 * tokens :]]).astype(jnp.bfloat16)
            keep_own[c, :, columns] = near[tokens:]
            keep_pc[c, :, columns] = total[2 * tokens : 3 * tokens]
            send[0, c, :, columns] = low[:tokens]
            send[1, c, :, columns] = low[3 * tokens :]
            up_kv[c] = up_kv[c] + mm(w_kv[c, :, columns], low, NT)
            own = slice(c * rank, (c + 1) * rank)
            grad_kv = mm(down_win[own, :], low)
            for r in range(rank):
                row, at = divmod((c * rank + r) * kv_width + g * HEAD_SIZE, grads.shape[1])
                grads[rank + row : rank + row + 1, at : at + HEAD_SIZE] = grad_kv[r : r + 1, :]
    sib, near, pc, px = (
        jnp.concatenate([up_kv[c][:, block * tokens : (block + 1) * tokens] for c in range(2)])
        for block in range(4)
    )
    grad_up[...] = (grads[...] * scale).astype(jnp.bfloat16)
    up_keep[...] = jnp.concatenate([near, pc])
    up_send[...] = jnp.concatenate([sib, px]).astype(jnp.bfloat16)


def attention(scale, flags, queries, grads, terms, w_q, down, kv_own, kv_sib):
    tokens, width = queries.shape
    kv_width = kv_own.shape[2]
    kv_local = kv_width // HEAD_SIZE
    per_kv = width // kv_width
    rank = w_q.shape[0]
    assert per_kv * rank == HEAD_SIZE
    f32, bf16 = jnp.float32, jnp.bfloat16
    shape = jax.ShapeDtypeStruct
    pairs = kv_local * per_kv * tokens * tokens
    smem = pl.BlockSpec(memory_space=pltpu.SMEM)
    vmem = pl.BlockSpec(memory_space=pltpu.VMEM)
    hbm = pl.BlockSpec(memory_space=pltpu.HBM)

    def scratch(blocks):
        rows = blocks * tokens
        slot = [
            pltpu.VMEM((rows, tokens), f32),
            pltpu.VMEM((rows, tokens), bf16),
            pltpu.VMEM((rows, tokens), bf16),
            pltpu.VMEM((1, tokens), f32),
            pltpu.VMEM((1, tokens), f32),
        ]
        return [
            pltpu.SMEM((kv_local * per_kv + 1,), jnp.int32),
            pltpu.VMEM((tokens, width), bf16),
            pltpu.VMEM((tokens, width), bf16),
            pltpu.SemaphoreType.DMA((kv_local,)),
            pltpu.SemaphoreType.DMA((kv_local,)),
            pltpu.VMEM((kv_local * HEAD_SIZE, rows), bf16),
        ] + slot * 2

    def call(kernel, out_shape, scratch_shapes, work, name, *args):
        return pl.pallas_call(
            functools.partial(kernel, per_kv, rank),
            in_specs=[smem, hbm, hbm] + [vmem] * (len(args) - 3),
            out_specs=[vmem] * len(out_shape),
            out_shape=out_shape,
            scratch_shapes=scratch_shapes,
            compiler_params=pltpu.CompilerParams(vmem_limit_bytes=VMEM_LIMIT),
            cost_estimate=pl.CostEstimate(
                flops=work * pairs * HEAD_SIZE, bytes_accessed=6 * tokens * width, transcendentals=pairs
            ),
            name=name,
        )(*args)

    queries, grads = (pltpu.with_memory_space_constraint(a, pltpu.HBM) for a in (queries, grads))
    common = (flags, queries, grads, terms, w_q, down, kv_own, kv_sib)

    def own():
        return call(
            own_kernel,
            [
                shape((rank, tokens), f32),
                shape((2 * tokens * kv_local, 2 * HEAD_SIZE), f32),
                shape((2 * tokens * kv_local, HEAD_SIZE), f32),
            ],
            scratch(2),
            40,
            "own_chip_heads",
            *common,
        )

    def previous(kv_pc, kv_px, own_grads, w_kv, down_win):
        grad_rows = rank + 2 * rank * kv_width // width
        return call(
            functools.partial(previous_kernel, scale),
            [
                shape((2, tokens, kv_width), f32),
                shape((2, tokens, kv_width), f32),
                shape((2, 2, tokens, kv_width), bf16),
                shape((rank, tokens), f32),
                shape((4 * rank, tokens), f32),
                shape((4 * rank, tokens), bf16),
                shape((grad_rows, width), bf16),
            ],
            [
                pltpu.VMEM((4 * tokens * kv_local, 2 * HEAD_SIZE), f32),
                pltpu.VMEM((4 * tokens * kv_local, HEAD_SIZE), f32),
                pltpu.VMEM((grad_rows, width), f32),
            ]
            + scratch(4),
            80,
            "previous_chip_heads",
            *common,
            kv_pc,
            kv_px,
            *own_grads,
            w_kv,
            down_win,
        )

    return own, previous


def exchanged(value, axis, bit):
    return lax.ppermute(value, axis, [(i, i ^ bit) for i in range(lax.axis_size(axis))])


def moved(value, axis, by):
    count = lax.axis_size(axis)
    return lax.ppermute(value, axis, [(i, (i + by) % count) for i in range(count)])


def summed(value, axis):
    bit = 1
    while bit < lax.axis_size(axis):
        value = value + exchanged(value, axis, bit)
        bit *= 2
    return value


def small_call(kernel, out_shape, *args, scratch=(), limit=1):
    vmem = pl.BlockSpec(memory_space=pltpu.VMEM)
    return pl.pallas_call(
        kernel,
        in_specs=[vmem] * len(args),
        out_specs=[vmem] * len(out_shape),
        out_shape=out_shape,
        scratch_shapes=list(scratch),
        compiler_params=pltpu.CompilerParams(vmem_limit_bytes=limit * SMALL_VMEM),
    )(*args)


def place(unit, radix):
    return lax.axis_index("seq") // unit % radix


def lanes(index, wide):
    return pl.ds(pl.multiple_of(index * wide, HEAD_SIZE), wide)


def projected_and_stacked(down_weight, inputs, key_rows, value_rows):
    rows, width = down_weight.shape
    tokens, kv_width = key_rows.shape
    steps = kv_width // HEAD_SIZE
    args = [
        pltpu.with_memory_space_constraint(a, pltpu.HBM)
        for a in (down_weight, inputs, key_rows, value_rows)
    ]

    def kernel(weight, tokens_in, key, value, down, kv):
        part = mm(weight[...], tokens_in[...], NT)

        @pl.when(pl.program_id(0) == 0)
        def _():
            down[...] = part

        @pl.when(pl.program_id(0) > 0)
        def _():
            down[...] += part

        kv[0] = key[...]
        kv[1] = value[...]

    def columns(high, wide):
        return pl.BlockSpec((high, wide // steps), lambda g: (0, g))

    return pl.pallas_call(
        kernel,
        grid=(steps,),
        in_specs=[
            columns(rows, width),
            columns(tokens, width),
            columns(tokens, kv_width),
            columns(tokens, kv_width),
        ],
        out_specs=[
            pl.BlockSpec((rows, tokens), lambda g: (0, 0)),
            pl.BlockSpec((2, tokens, kv_width // steps), lambda g: (0, 0, g)),
        ],
        out_shape=[
            jax.ShapeDtypeStruct((rows, tokens), jnp.float32),
            jax.ShapeDtypeStruct((2, tokens, kv_width), jnp.bfloat16),
        ],
        compiler_params=pltpu.CompilerParams(
            dimension_semantics=("arbitrary",), vmem_limit_bytes=2 * SMALL_VMEM
        ),
    )(*args)


def up_sums(up_q, up_keep, received):
    rank, tokens = up_q.shape

    def kernel(up_q, keep, other, mine, to_send, previous):
        total = keep[...] + other[...].astype(jnp.float32)
        own = jnp.concatenate([up_q[...], total[: 2 * rank]])
        mine[...] = own
        to_send[...] = own.astype(jnp.bfloat16)
        previous[...] = total[2 * rank :].astype(jnp.bfloat16)

    shape = jax.ShapeDtypeStruct
    return small_call(
        kernel,
        [
            shape((3 * rank, tokens), jnp.float32),
            shape((3 * rank, tokens), jnp.bfloat16),
            shape((2 * rank, tokens), jnp.bfloat16),
        ],
        up_q,
        up_keep,
        received,
    )


def up_terms(mine, to_send, previous):
    heads, count = lax.axis_size("head"), lax.axis_size("seq")
    nearby = moved(previous, "seq", -2)
    if heads == 2:
        pairs = [
            (s * heads + h, (s - 2) % count * heads + 1 - h) for s in range(count) for h in range(heads)
        ]
        return [mine, exchanged(to_send, "head", 1), nearby, lax.ppermute(previous, ("seq", "head"), pairs)]
    rank = mine.shape[0] - previous.shape[0]
    total = jnp.concatenate([mine[:rank], mine[rank:] + nearby.astype(jnp.float32)])
    bit = 1
    while 2 * bit < heads:
        total = total + exchanged(total.astype(jnp.bfloat16), "head", bit).astype(jnp.float32)
        bit *= 2
    return [total, exchanged(total.astype(jnp.bfloat16), "head", bit)]


def weight_halves(terms, inputs, grad_up, scale):
    width = inputs.shape[1]
    wide = width // 2
    up_rows, tokens = terms[0].shape
    rows = up_rows + grad_up.shape[0]
    given = len(terms)

    def kernel(*refs):
        tokens_in, grads, up_low, *out = refs[given:]
        up = jnp.zeros((up_rows, tokens), jnp.float32)
        for term in refs[:given]:
            value = term[...].astype(jnp.float32)
            if value.shape[0] < up_rows:
                value = jnp.concatenate(
                    [jnp.zeros((up_rows - value.shape[0], tokens), jnp.float32), value]
                )
            up = up + value
        up = up.astype(jnp.bfloat16)
        up_low[...] = up
        for d in range(2):
            at = lanes(place(1, 2) ^ d, wide)
            out[d][...] = jnp.concatenate(
                [mm(up, tokens_in[:, at]) * scale, grads[:, at].astype(jnp.float32)]
            ).astype(jnp.bfloat16)

    shape = jax.ShapeDtypeStruct
    return small_call(
        kernel,
        [shape((up_rows, tokens), jnp.bfloat16)] + [shape((rows, wide), jnp.bfloat16)] * 2,
        *terms,
        inputs,
        grad_up,
        limit=2,
    )


def exchanged_pieces(pieces, unit):
    return [pieces[0]] + [exchanged(p, "seq", d * unit) for d, p in enumerate(pieces) if d]


def summed_and_cut(pieces, unit, radix):
    rows, whole = pieces[0].shape
    wide = whole // radix
    if wide % HEAD_SIZE:
        total = sum(p.astype(jnp.float32) for p in pieces).astype(jnp.bfloat16)
        return [
            lax.dynamic_slice_in_dim(total, (place(unit, radix) ^ d) * wide, wide, 1)
            for d in range(radix)
        ]
    given = len(pieces)

    def kernel(*refs):
        total = refs[-1]
        total[...] = sum(p[...].astype(jnp.float32) for p in refs[:given])
        for d in range(radix):
            refs[given + d][...] = total[:, lanes(place(unit, radix) ^ d, wide)].astype(jnp.bfloat16)

    return small_call(
        kernel,
        [jax.ShapeDtypeStruct((rows, wide), jnp.bfloat16)] * radix,
        *pieces,
        scratch=[pltpu.VMEM((rows, whole), jnp.float32)],
    )


def joined(pieces, unit):
    rows, wide = pieces[0].shape
    radix = len(pieces)
    if wide % HEAD_SIZE:
        whole = jnp.zeros((rows, radix * wide), jnp.bfloat16)
        for d in range(radix):
            whole = lax.dynamic_update_slice_in_dim(
                whole, pieces[d], (place(unit, radix) ^ d) * wide, 1
            )
        return whole

    def kernel(*refs):
        for d in range(radix):
            refs[radix][:, lanes(place(unit, radix) ^ d, wide)] = refs[d][...]

    return small_call(kernel, [jax.ShapeDtypeStruct((rows, radix * wide), jnp.bfloat16)], *pieces)[0]


def joined_outputs(pieces, rank, kv_shape):
    rows, wide = pieces[0].shape
    extra = rows - 4 * rank
    each = wide // kv_shape[1]
    per_row = kv_shape[0] // extra

    def kernel(one, two, down, up_q, up_kv):
        for d, half in enumerate((one, two)):
            at = place(1, 2) ^ d
            piece = half[...].astype(jnp.float32)
            down[:, lanes(at, wide)] = piece[: 3 * rank]
            up_q[:, lanes(at, wide)] = piece[3 * rank : 4 * rank]
            for i in range(extra):
                for b in range(each):
                    up_kv[pl.ds(per_row * i + each * at + b, 1), :] = piece[
                        4 * rank + i : 4 * rank + i + 1, b * kv_shape[1] : (b + 1) * kv_shape[1]
                    ]

    shape = jax.ShapeDtypeStruct
    return small_call(
        kernel,
        [
            shape((3 * rank, 2 * wide), jnp.float32),
            shape((rank, 2 * wide), jnp.float32),
            shape(kv_shape, jnp.float32),
        ],
        *pieces,
    )


def per_device(
    queries,
    layer_key_rows,
    layer_value_rows,
    output_gradient,
    output_row_sums,
    shifted_head_flags,
    inputs,
    adapter_down_weight,
    query_up_weight,
    key_value_up_weight,
):
    seq_count = lax.axis_size("seq")
    tokens, width = queries.shape
    kv_width = layer_key_rows.shape[1]
    whole_len = tokens * seq_count
    rank = adapter_down_weight.shape[1]
    assert GROUP == 4 * tokens and SHIFT == 2 * tokens
    levels = (seq_count.bit_length() - 1) // 2
    assert 4**levels == seq_count
    flattened_down = adapter_down_weight.reshape(3 * rank, width)
    scale = adapter_scale / math.sqrt(whole_len)
    down_part, kv_own = projected_and_stacked(flattened_down, inputs, layer_key_rows, layer_value_rows)
    kv_pc = moved(kv_own, "seq", 2)
    kv_sib = exchanged(kv_own, "seq", 1)

    down_low = summed(down_part, "head").astype(jnp.bfloat16)
    down_tiled = jnp.tile(down_low[:rank].T, (1, HEAD_SIZE // rank))
    down_own = down_low[rank:]
    down_pc = moved(down_own, "seq", 2)

    own, previous = attention(
        scale,
        shifted_head_flags,
        queries,
        output_gradient,
        output_row_sums,
        query_up_weight,
        down_tiled,
        kv_own,
        kv_sib,
    )
    own_grads, kv_pc, down_pc = lax.optimization_barrier((own(), kv_pc, down_pc))
    kv_px = exchanged(kv_pc, "seq", 1)
    down_others = exchanged(jnp.concatenate([down_own, down_pc]), "seq", 1)
    down_win = jnp.concatenate(
        [down_others[: 2 * rank], down_own, down_pc, down_others[2 * rank :]], axis=1
    )
    keep_own, keep_pc, send, up_q, up_keep, up_send, grad_up = previous(
        kv_pc, kv_px, own_grads, key_value_up_weight, down_win
    )

    up_received, send = lax.optimization_barrier((exchanged(up_send, "seq", 1), send))
    received = exchanged(send, "seq", 1)
    terms = up_terms(*up_sums(up_q, up_keep, up_received))
    back = (keep_pc + received[1].astype(jnp.float32)).astype(jnp.bfloat16)
    up_low, *pieces = weight_halves(terms, inputs, grad_up, scale)
    pieces = exchanged_pieces(summed_and_cut(exchanged_pieces(pieces, 1), 2, 2), 2)
    pieces, back = lax.optimization_barrier((pieces, back))
    back = moved(back, "seq", -2)
    for level in range(1, levels):
        pieces = exchanged_pieces(summed_and_cut(pieces, 4**level, 4), 4**level)
    total = sum(p.astype(jnp.float32) for p in pieces).astype(jnp.bfloat16)
    grad_inputs = (
        adapter_scale
        * lax.dot_general(
            up_low, flattened_down, (((0,), (0,)), ((), ())), preferred_element_type=jnp.float32
        )
    ).astype(jnp.bfloat16)
    for level in range(levels - 1, 0, -1):
        total = joined(exchanged_pieces([total] * 4, 4**level), 4**level)
    total, grad_inputs, back = lax.optimization_barrier((total, grad_inputs, back))
    key_value_gradient = (
        keep_own + received[0].astype(jnp.float32) + back.astype(jnp.float32)
    ).astype(jnp.bfloat16)
    total = joined(exchanged_pieces([total] * 2, 2), 2)
    total, key_value_gradient = lax.optimization_barrier((total, key_value_gradient))
    down_gradient, grad_up_q, grad_up_kv = joined_outputs(
        exchanged_pieces([total] * 2, 1), rank, (2 * rank, kv_width)
    )
    return (
        grad_inputs,
        key_value_gradient,
        down_gradient.reshape(3, rank, width),
        grad_up_q,
        grad_up_kv.reshape(2, rank, kv_width),
    )


def solution(mesh):
    placed = (
        P("seq", "head"),
        P("seq", "head"),
        P("seq", "head"),
        P("seq", "head"),
        P("head", "seq"),
        P("head"),
        P("seq", "head"),
        P(None, None, "head"),
        P(None, "head"),
        P(None, None, "head"),
    )
    return jax.shard_map(
        per_device,
        mesh=mesh,
        in_specs=placed,
        out_specs=(
            P("seq", "head"),
            P(None, "seq", "head"),
            P(None, None, "head"),
            P(None, "head"),
            P(None, None, "head"),
        ),
        check_vma=False,
    )
```
